128 devices in a mesh: section: 2 (over y_lo), dp: 16 (over x, y_hi, core), tensor: 4 (over z).
Axes of the slice: x: 4, y: 4 (y_hi: 2, y_lo: 2; y = y_hi * 2 + y_lo), z: 4, core: 2. Of those that a mesh axis runs over, the one named last changes fastest.
Arguments:
- series: float32 [512, 512], P('dp'), may hold values from -6 to 6
- missing: int32 [512, 512], P('dp'), may hold values 0 or 1
- w_in: bfloat16 [64, 1280], P(None, 'tensor'), may hold values from -0.75 to 0.75
- w_hid: bfloat16 [1280, 1280], P('tensor'), may hold values from -0.15625 to 0.15625
- w_res: bfloat16 [64, 1280], replicated, may hold values from -0.75 to 0.75
- gain_attn: float32 [2, 1280], P('section'), may hold values from 0.5 to 1.5
- w_qkv: bfloat16 [2, 1280, 3, 1280], P('section', None, None, 'tensor'), may hold values from -0.15625 to 0.15625
- w_out: bfloat16 [2, 1280, 1280], P('section', 'tensor'), may hold values from -0.5 to 0.5
- gain_mlp: float32 [2, 1280], P('section'), may hold values from 0.5 to 1.5
- w_up: bfloat16 [2, 1280, 5120], P('section', None, 'tensor'), may hold values from -0.15625 to 0.15625
- w_down: bfloat16 [2, 5120, 1280], P('section', 'tensor'), may hold values from -0.125 to 0.125
- cotangent: bfloat16 [8192, 1280], P('dp'), may hold values from -6 to 6
Outputs:
- layer_outputs: bfloat16 [2, 8192, 1280], P('section', 'dp')
- series_grad: float32 [512, 512], P('dp', ('section', 'tensor'))
- w_in_grad: float32 [64, 1280], P('section', 'tensor')
- w_hid_grad: float32 [1280, 1280], P('tensor', 'section')
- w_res_grad: float32 [64, 1280], P(None, 'section')
- gain_attn_grad: float32 [2, 1280], P('section')
- w_qkv_grad: float32 [2, 1280, 3, 1280], P('section', None, None, 'tensor')
- w_out_grad: float32 [2, 1280, 1280], P('section', 'tensor')
- gain_mlp_grad: float32 [2, 1280], P('section')
- w_up_grad: float32 [2, 1280, 5120], P('section', None, 'tensor')
- w_down_grad: float32 [2, 5120, 1280], P('section', 'tensor')
The draws below stay inside these ranges and needn't reach their ends.
All inputs are finite; a program needn't handle non-finite values. No bound on the sum of `missing` on one device may be relied on, other than what follows from the above.
Results may differ from the reference program's by a relative error of at most 0.035.
Values may be sent and summed in bfloat16 or wider, within the bound.
A program may use at most 192 MiB of HBM per device.

```python
import math
import jax
import jax.numpy as jnp
from jax import lax

D = 1280
HEADS = 16
HEAD_DIM = 80
FF = 5120
TOK_HIDDEN = 1280
PATCH = 32
PATCHES = 16
LAYERS = 2
POINTS = 512
CONTEXTS = 512
TOKENS = 8192


def plant(drawn, stream_key, least, largest):
    dims = drawn.shape
    index_at = [jax.random.randint(jax.random.fold_in(stream_key, axis), (), 0, dims[axis]) for axis in range(len(dims))]
    drawn = drawn.at[tuple(index_at)].set(least)
    longest = dims.index(max(dims))
    index_at[longest] = (index_at[longest] + 1) % dims[longest]
    return drawn.at[tuple(index_at)].set(largest)


def shard_levels(own_key, shape, shards, low, top_value):
    gain, own = 1.0, jax.random.fold_in(own_key, 6)
    for axis_at, blocks in shards:
        steps = jnp.exp(jax.random.uniform(jax.random.fold_in(own, axis_at), (blocks,), jnp.float32, low / len(shards), top_value / len(shards)))
        gain = gain * jnp.repeat(steps, shape[axis_at] // blocks).reshape([-1 if axis == axis_at else 1 for axis in range(len(shape))])
    return gain


def gaussian(own_key, extent, width, reach, cuts=(), held_as=jnp.bfloat16):
    level = shard_levels(own_key, extent, cuts, -0.22, 0.18) if cuts else 1.0
    entries = jax.random.normal(own_key, extent, jnp.float32) * width * level
    return jnp.minimum(jnp.maximum(entries, -reach), reach).astype(held_as)


def setup_inputs(seed: int = 0) -> dict:
    key_of = jax.random.split(jax.random.key(seed), 13)
    series = gaussian(key_of[0], (CONTEXTS, POINTS), 1.0, 6.0, ((0, 16),), jnp.float32)
    missing = plant((jax.random.randint(key_of[1], (CONTEXTS, POINTS), 0, 8) < 1).astype(jnp.int32), jax.random.fold_in(key_of[1], 1), 0, 1)
    w_in = gaussian(key_of[2], (2 * PATCH, TOK_HIDDEN), (2 * PATCH) ** -0.5, 0.75, ((1, 4),))
    w_hid = gaussian(key_of[3], (TOK_HIDDEN, D), TOK_HIDDEN ** -0.5, 0.15625, ((0, 4),))
    w_res = gaussian(key_of[4], (2 * PATCH, D), (2 * PATCH) ** -0.5, 0.75)
    gain_attn = jnp.clip(1.0 + 0.1 * jax.random.normal(key_of[5], (LAYERS, D), jnp.float32), 0.5, 1.5)
    w_qkv = gaussian(key_of[6], (LAYERS, D, 3, D), D ** -0.5, 0.15625, ((0, 2), (3, 4)))
    w_out = gaussian(key_of[7], (LAYERS, D, D), (D // 8) ** -0.5, 0.5, ((0, 2), (1, 4)))
    gain_mlp = jnp.clip(1.0 + 0.1 * jax.random.normal(key_of[8], (LAYERS, D), jnp.float32), 0.5, 1.5)
    w_up = gaussian(key_of[9], (LAYERS, D, FF), D ** -0.5, 0.15625, ((0, 2), (2, 4)))
    w_down = gaussian(key_of[10], (LAYERS, FF, D), (FF // 2) ** -0.5, 0.125, ((0, 2), (1, 4)))
    cotangent = gaussian(key_of[11], (TOKENS, D), 1.0, 6.0, ((0, 16),))
    return {"series": series, "missing": missing, "w_in": w_in, "w_hid": w_hid, "w_res": w_res, "gain_attn": gain_attn, "w_qkv": w_qkv, "w_out": w_out, "gain_mlp": gain_mlp, "w_up": w_up, "w_down": w_down, "cotangent": cotangent}


eps_norm = 1e-06
masked_score = -1e+30
highest = lax.Precision.HIGHEST

@jax.custom_vjp
def low(v):
    return lax.optimization_barrier(v.astype(jnp.bfloat16)).astype(jnp.float32)

@jax.custom_vjp
def low_back(v):
    return v

def low_keep(v):
    return (low(v), None)

def low_pass(kept, grad):
    return (grad,)

def back_keep(v):
    return (v, None)

def back_low(kept, grad):
    return (low(grad),)
low.defvjp(low_keep, low_pass)
low_back.defvjp(back_keep, back_low)

def rms_scale(stream, gain_vec):
    return stream * lax.rsqrt(lax.optimization_barrier(jnp.mean(stream * stream, axis=-1, keepdims=True)) + eps_norm) * gain_vec

def rotary_tables(row_count):
    half_dim = HEAD_DIM // 2
    position = (lax.iota(jnp.int32, row_count) % PATCHES).astype(jnp.float32)
    frequency = jnp.exp(lax.iota(jnp.float32, half_dim) * (-2.0 * math.log(10000.0) / HEAD_DIM))
    angles = position[:, None] * frequency[None, :]
    return (jnp.cos(angles)[:, None, :], jnp.sin(angles)[:, None, :])

def rotate(field, cosine_table, sine_table):
    half_dim = field.shape[-1] // 2
    leading = field[..., :half_dim]
    trailing = field[..., half_dim:]
    return jnp.concatenate([leading * cosine_table - trailing * sine_table, trailing * cosine_table + leading * sine_table], axis=-1)

def apply_layer(stream, gain_attn, w_qkv, w_out, gain_mlp, w_up, w_down, cosine_table, sine_table, allowed):
    row_count = stream.shape[0]
    contexts = row_count // PATCHES
    normed = low(rms_scale(stream, gain_attn))
    qkv = low_back(jnp.einsum('rd,dcj->rcj', normed, w_qkv, precision=highest))
    split_qkv = qkv.reshape(row_count, 3, HEADS, HEAD_DIM)
    head_queries = low(rotate(split_qkv[:, 0], cosine_table, sine_table)).reshape(contexts, PATCHES, HEADS, HEAD_DIM)
    head_keys = low(rotate(split_qkv[:, 1], cosine_table, sine_table)).reshape(contexts, PATCHES, HEADS, HEAD_DIM)
    head_values = low(split_qkv[:, 2]).reshape(contexts, PATCHES, HEADS, HEAD_DIM)
    scores = low_back(jnp.einsum('cqhe,ckhe->chqk', head_queries, head_keys, precision=highest) * (1.0 / math.sqrt(HEAD_DIM)))
    scores = jnp.where(allowed, scores, masked_score)
    attention = low(jax.nn.softmax(scores, axis=-1))
    context = low_back(low(jnp.einsum('chqk,ckhe->cqhe', attention, head_values, precision=highest)))
    context = context.reshape(row_count, HEADS * HEAD_DIM)
    middle = stream + low_back(jnp.dot(context, w_out, precision=highest, preferred_element_type=jnp.float32))
    normed_mlp = low(rms_scale(middle, gain_mlp))
    upward = low_back(jnp.dot(normed_mlp, w_up, precision=highest, preferred_element_type=jnp.float32))
    hidden = low(jax.nn.gelu(upward))
    return middle + low_back(jnp.dot(hidden, w_down, precision=highest, preferred_element_type=jnp.float32))

def reference(series, missing, w_in, w_hid, w_res, gain_attn, w_qkv, w_out, gain_mlp, w_up, w_down, cotangent):
    keep_point = (1 - missing).astype(jnp.float32)
    mask_cols = missing.astype(jnp.float32).reshape(TOKENS, PATCH)
    cosine_table, sine_table = rotary_tables(TOKENS)
    position = lax.iota(jnp.int32, PATCHES)
    allowed = position[None, :] <= position[:, None]

    def forward(series_in, in_matrix, hid_matrix, res_matrix, gains_attn, qkv_matrix, out_matrix, gains_mlp, up_matrix, down_matrix):
        patch_in = low(jnp.concatenate([(series_in * keep_point).reshape(TOKENS, PATCH), mask_cols], axis=1))
        hidden = low(jax.nn.silu(low_back(jnp.dot(patch_in, in_matrix, precision=highest, preferred_element_type=jnp.float32))))
        stream = low_back(jnp.dot(hidden, hid_matrix, precision=highest, preferred_element_type=jnp.float32) + jnp.dot(patch_in, res_matrix, precision=highest, preferred_element_type=jnp.float32))
        results = []
        for layer_index in range(LAYERS):
            stream = apply_layer(stream, gains_attn[layer_index], qkv_matrix[layer_index], out_matrix[layer_index], gains_mlp[layer_index], up_matrix[layer_index], down_matrix[layer_index], cosine_table, sine_table, allowed)
            if layer_index + 1 < LAYERS:
                stream = low_back(low(stream))
            results.append(stream)
        return jnp.stack(results)
    outputs, pullback = jax.vjp(forward, series, w_in.astype(jnp.float32), w_hid.astype(jnp.float32), w_res.astype(jnp.float32), gain_attn, w_qkv.astype(jnp.float32), w_out.astype(jnp.float32), gain_mlp, w_up.astype(jnp.float32), w_down.astype(jnp.float32))
    cotangents = jnp.zeros_like(outputs).at[LAYERS - 1].set(cotangent.astype(jnp.float32))
    gradients = pullback(cotangents)
    return (outputs.astype(jnp.bfloat16), gradients[0], gradients[1], gradients[2], gradients[3], gradients[4], gradients[5], gradients[6], gradients[7], gradients[8], gradients[9])
```

```python
import math

import jax
import jax.numpy as jnp
import numpy as np
from jax import lax
from jax.experimental import pallas as pl
from jax.experimental.pallas import tpu as pltpu
from jax.sharding import PartitionSpec as P

D = 1280
HEADS_HERE = 4
HEAD_DIM = 80
ATT = HEADS_HERE * HEAD_DIM
PATCH = 32
PATCHES = 16
ROWS = 256
HALVES = 2
RH = ROWS // HALVES
RQ = RH // 4
TILE = 256
BLOCK = 128
MATS = ((0, 960), (960, 320), (1280, 1280), (2560, 1280))
LAYER_ROWS = 3840
PACK_ROWS = 4096
MESH = pl.DeviceIdType.MESH
f32 = jnp.float32
bf16 = jnp.bfloat16
eps_norm = 1e-06
masked_score = -1e30
GELU_A = math.sqrt(2.0 / math.pi)
GELU_B = 0.044715


def mm(a, b):
    return lax.dot_general(a, b, (((1,), (0,)), ((), ())), preferred_element_type=f32)


def mm_t(a, b):
    return lax.dot_general(a, b, (((1,), (1,)), ((), ())), preferred_element_type=f32)


def tm(a, b):
    return lax.dot_general(a, b, (((0,), (0,)), ((), ())), preferred_element_type=f32)


def rotary_arrays():
    half = HEAD_DIM // 2
    position = (np.arange(BLOCK) % PATCHES).astype(np.float32)
    frequency = np.exp(
        np.arange(half, dtype=np.float32) * np.float32(-2.0 * math.log(10000.0) / HEAD_DIM)
    )
    angles = position[:, None] * frequency[None, :]
    lane = np.arange(ATT) % half
    turn = np.zeros((ATT, ATT), np.float32)
    for j in range(ATT):
        if j % HEAD_DIM < half:
            turn[j + half, j] = -1.0
        else:
            turn[j - half, j] = 1.0
    return np.cos(angles)[:, lane], np.sin(angles)[:, lane], turn


def places():
    s = lax.axis_index("section")
    dp = lax.axis_index("dp")
    z = lax.axis_index("tensor")
    c = lax.rem(dp, 2)
    yh = lax.rem(lax.div(dp, 2), 2)
    x = lax.div(dp, 4)
    return s, dp, z, x, yh, c


def layers_kernel(
    patch_ref, w_in_ref, w_hid_ref, w_res_ref, gains_ref, wq_ref, wo_ref, wu_ref, wd_ref,
    cot_ref, cos_ref, sin_ref, turn_ref,
    lo_ref, gp_ref, points_ref,
    wb, gn, tokh, pre, sx, mid, nb, nm, qb, pb, ct, upb, hb, gb, mb, du, dqb, dctx, gv, gt,
    sb, rb, dmid, ob, gg, ggr, dps, dpr, gpad,
    w_loc, w_s, w_r, f_s, f_r, gn_l, gn_s, gn_r, cot_l,
    rs_s, rs_r, ag_s, ag_r, lo_l, lo_s, lo_r, gg_s, gg_r, dp_s, dp_r, gp_l,
):
    s, dp, z, x, yh, c = places()
    other = 1 - s
    z_peer = [None] + [(s, dp, lax.rem(z + d, 4)) for d in (1, 2, 3)]
    z_at = [z] + [lax.rem(z + d, 4) for d in (1, 2, 3)]
    y_a = (other, dp, z)
    y_b = (other, dp + 2 - 4 * yh, z)
    core = (s, dp + 1 - 2 * c, z)
    across = [(other, dp, z_at[d]) for d in range(4)]
    w_refs = (wq_ref, wo_ref, wu_ref, wd_ref)

    barrier = pltpu.get_barrier_semaphore()
    peers = z_peer[1:] + across + [y_b, core]
    for peer in peers:
        pl.semaphore_signal(barrier, inc=1, device_id=peer, device_id_type=MESH)
    pl.semaphore_wait(barrier, len(peers))

    def remote(src, dst, ssem, rsem, peer):
        return pltpu.make_async_remote_copy(
            src_ref=src, dst_ref=dst, send_sem=ssem, recv_sem=rsem,
            device_id=peer, device_id_type=MESH,
        )

    def quarter(m, q):
        off, n = MATS[m]
        return pl.ds(pl.multiple_of(off + q * (n // 4), 16), n // 4)

    def w_local(m):
        off, n = MATS[m]
        return pltpu.make_async_copy(w_refs[m], wb.at[s, pl.ds(off, n)], w_loc.at[m])

    def w_quarter(m, k):
        off, n = MATS[m]
        q = 2 * c + k
        src = w_refs[m].at[pl.ds(pl.multiple_of(q * (n // 4), 16), n // 4)]
        return remote(src, wb.at[s, quarter(m, q)], w_s.at[m, k], w_r.at[m, k], (y_a, y_b)[k])

    def w_forward(m):
        off, n = MATS[m]
        half = pl.ds(pl.multiple_of(off + c * (n // 2), 16), n // 2)
        return remote(wb.at[other, half], wb.at[other, half], f_s.at[m], f_r.at[m], core)

    def pump(layer, m):
        @pl.when(s != layer)
        def _():
            for k in range(2):
                w_quarter(m, k).wait_recv()
            w_forward(m).start()

    def need(layer, m):
        @pl.when(s != layer)
        def _():
            w_forward(m).wait_recv()

    gn_copy = pltpu.make_async_copy(gains_ref, gn.at[s], gn_l)
    gn_send = remote(gains_ref, gn.at[s], gn_s, gn_r, y_a)
    cot_copy = pltpu.make_async_copy(
        cot_ref.at[pl.ds(pl.multiple_of(s * ROWS, ROWS), ROWS)], gb.at[2], cot_l
    )
    gn_send.start()
    gn_copy.start()
    for m in range(4):
        for k in range(2):
            w_quarter(m, k).start()
        w_local(m).start()
    cot_copy.start()

    def rows_of(h):
        return pl.ds(h * RH, RH)

    def chunk(h, zz):
        return pl.ds(pl.multiple_of(h * RH + zz * RQ, RQ), RQ)

    def cols_of(j):
        return pl.ds(pl.multiple_of(j * TILE, TILE), TILE)

    def rs_copy(st, h, d, cols=None):
        src = sb.at[st % 2, chunk(h, z_at[d])]
        dst = rb.at[st, d - 1, pl.ds(h * RQ, RQ)]
        if cols is not None:
            src = sb.at[st % 2, chunk(h, z_at[d]), cols]
            dst = rb.at[st, d - 1, pl.ds(h * RQ, RQ), cols]
        return remote(src, dst, rs_s.at[st, h, d - 1], rs_r.at[st, h, d - 1], z_peer[d])

    def rs_send(st, h, produce):
        if st >= 2:
            for d in (1, 2, 3):
                rs_copy(st - 2, h, d).wait_send()

        def body(j, carry):
            cols = cols_of(j)
            sb[st % 2, rows_of(h), cols] = produce(j, cols).astype(bf16)
            for d in (2, 1, 3):
                rs_copy(st, h, d, cols).start()
            return carry

        lax.fori_loop(0, D // TILE, body, 0)

    def rs_take(st, h):
        total = sb[st % 2, chunk(h, z), :].astype(f32)
        for d in (1, 3, 2):
            rs_copy(st, h, d).wait_recv()
            total = total + rb[st, d - 1, pl.ds(h * RQ, RQ), :].astype(f32)
        return total

    def ag_copy(st, h, d, dst):
        at = dst.at[chunk(h, z)]
        return remote(at, at, ag_s.at[st, h, d - 1], ag_r.at[st, h, d - 1], z_peer[d])

    def ag_send(st, h, dst, value):
        dst[chunk(h, z), :] = value.astype(bf16)
        for d in (2, 1, 3):
            ag_copy(st, h, d, dst).start()

    def ag_wait(st, h, dst):
        for d in (1, 3, 2):
            ag_copy(st, h, d, dst).wait_recv()

    def own(h):
        return pl.ds(h * RQ, RQ)

    def scale_of(v):
        return lax.rsqrt(jnp.mean(v * v, axis=-1, keepdims=True) + eps_norm)

    def norm(v, g):
        return v * scale_of(v) * g

    def norm_back(dn, v, g):
        r = scale_of(v)
        weighted = g * dn
        inner = jnp.mean(v * weighted, axis=-1, keepdims=True)
        return r * weighted - v * (r * r * r * inner), jnp.sum(dn * v * r, axis=0, keepdims=True)

    head_lane = lax.broadcasted_iota(jnp.int32, (1, ATT), 1)
    head_mask = [
        (head_lane >= HEAD_DIM * h) & (head_lane < HEAD_DIM * (h + 1)) for h in range(HEADS_HERE)
    ]

    def spread(v):
        wide = v.astype(f32)
        return jnp.concatenate(
            [jnp.where(m, wide, 0.0) for m in head_mask], axis=0
        ).astype(bf16)

    def gather(v):
        total = jnp.where(head_mask[0], v[:BLOCK], 0.0)
        for h in range(1, HEADS_HERE):
            total = total + jnp.where(head_mask[h], v[h * BLOCK : (h + 1) * BLOCK], 0.0)
        return total

    def turned(v, sign):
        high = v.astype(bf16)
        low = (v - high.astype(f32)).astype(bf16)
        swapped = mm(high, turn_ref[...]) + mm(low, turn_ref[...])
        if sign < 0:
            swapped = -swapped
        return v * cos_ref[...] + swapped * sin_ref[...]

    inv = 1.0 / math.sqrt(HEAD_DIM)

    def blocks_of(h):
        return range(h * RH // BLOCK, (h + 1) * RH // BLOCK)

    def attention_front(layer, h):
        for b in blocks_of(h):
            at = pl.ds(b * BLOCK, BLOCK)
            normed = nb[layer, at, :]
            q = turned(mm_t(normed, wb[layer, 0:ATT, :]), 1).astype(bf16)
            k = turned(mm_t(normed, wb[layer, ATT : 2 * ATT, :]), 1).astype(bf16)
            v = mm_t(normed, wb[layer, 2 * ATT : 3 * ATT, :]).astype(bf16)
            qb[layer, 0, at, :] = q
            qb[layer, 1, at, :] = k
            qb[layer, 2, at, :] = v
            scores = mm_t(spread(q), k) * inv
            row = lax.broadcasted_iota(jnp.int32, scores.shape, 0) & (BLOCK - 1)
            col = lax.broadcasted_iota(jnp.int32, scores.shape, 1)
            allowed = (col <= row) & (col >= (row & (BLOCK - PATCHES)))
            scores = jnp.where(allowed, scores, masked_score)
            e = jnp.exp(scores - jnp.max(scores, axis=-1, keepdims=True))
            probs = e / jnp.sum(e, axis=-1, keepdims=True)
            pb[layer, b] = probs
            ct[layer, at, :] = gather(mm(probs.astype(bf16), v)).astype(bf16)

    def attention_back(layer, h):
        for b in blocks_of(h):
            at = pl.ds(b * BLOCK, BLOCK)
            spread_d = spread(mm_t(mb[layer, at, :], wb[layer, 960:1280, :]).astype(bf16))
            spread_q = spread(qb[layer, 0, at, :])
            k = qb[layer, 1, at, :]
            v = qb[layer, 2, at, :]
            probs = pb[layer, b]
            d_probs = mm_t(spread_d, v)
            d_scores = (
                probs * (d_probs - jnp.sum(probs * d_probs, axis=-1, keepdims=True))
            ).astype(bf16)
            d_q = gather(mm(d_scores, k)) * inv
            d_k = tm(d_scores, spread_q) * inv
            dqb[0, at, :] = turned(d_q, -1).astype(bf16)
            dqb[1, at, :] = turned(d_k, -1).astype(bf16)
            dqb[2, at, :] = tm(probs.astype(bf16), spread_d).astype(bf16)

    for h in range(HALVES):
        at = rows_of(h)
        before = mm(patch_ref[at, :], w_in_ref[...])
        pre[at, :] = before
        tokh[at, :] = (before * jax.nn.sigmoid(before)).astype(bf16)
        rs_send(0, h, lambda j, cols: mm(tokh[at, :], w_hid_ref[:, cols]))
    gn_copy.wait()
    gn_send.wait_recv()
    for m in range(4):
        w_local(m).wait()
    for h in range(HALVES):
        stream = rs_take(0, h) + mm(patch_ref[chunk(h, z), :], w_res_ref[...])
        sx[0, own(h), :] = stream
        ag_send(0, h, nb.at[0], norm(stream, gn[0, 0:1, :]))
    pump(0, 0)
    pump(0, 1)
    need(0, 0)

    def send_out(layer, h, value):
        ob[layer, own(h), :] = value
        dst = lo_ref.at[pl.ds(pl.multiple_of(s * ROWS + h * RH + z * RQ, RQ), RQ)]
        src = ob.at[layer, own(h)]

        @pl.when(s == layer)
        def _():
            pltpu.make_async_copy(src, dst, lo_l.at[h]).start()

        @pl.when(s != layer)
        def _():
            remote(src, dst, lo_s.at[layer, 0, h], lo_r.at[s, 0, h], (layer, dp, z)).start()

        for d in (1, 2, 3):
            remote(
                src, dst, lo_s.at[layer, d, h], lo_r.at[s, d, h], (layer, dp, z_at[d])
            ).start()

    def mlp_out(layer, h):
        out = (mid[layer, own(h), :] + rs_take(2 + 2 * layer, h)).astype(bf16)
        send_out(layer, h, out)
        return out

    for layer in range(2):
        for h in range(HALVES):
            ag_wait(2 * layer, h, nb.at[layer])
            attention_front(layer, h)
            if h == 0:
                need(layer, 1)
            at = rows_of(h)
            rs_send(
                1 + 2 * layer, h, lambda j, cols: mm(ct[layer, at, :], wb[layer, 960:1280, cols])
            )
        pump(layer, 2)
        for h in range(HALVES):
            middle = sx[layer, own(h), :] + rs_take(1 + 2 * layer, h)
            mid[layer, own(h), :] = middle
            ag_send(1 + 2 * layer, h, nm.at[layer], norm(middle, gn[layer, 1:2, :]))
        need(layer, 2)
        for h in range(HALVES):
            ag_wait(1 + 2 * layer, h, nm.at[layer])
            at = rows_of(h)

            def up_tile(j, carry):
                cols = cols_of(j)
                up = mm(nm[layer, at, :], wb[layer, 1280:2560, cols])
                upb[layer, at, cols] = up
                t = jnp.tanh(GELU_A * (up + GELU_B * up * up * up))
                hb[layer, at, cols] = (0.5 * up * (1.0 + t)).astype(bf16)
                return carry

            lax.fori_loop(0, D // TILE, up_tile, 0)
            if h == 0:
                pump(layer, 3)
                need(layer, 3)
            rs_send(
                2 + 2 * layer, h, lambda j, cols: mm(hb[layer, at, :], wb[layer, 2560:3840, cols])
            )
        if layer == 0:
            for h in range(HALVES):
                out = mlp_out(0, h)
                stream = out.astype(f32)
                sx[1, own(h), :] = stream
                ag_send(2, h, nb.at[1], norm(stream, gn[1, 0:1, :]))
            pump(1, 0)
            pump(1, 1)
            need(1, 0)

    def gp_copy(layer, m):
        off, n = MATS[m]
        return pltpu.make_async_copy(
            gv.at[pl.ds(off, n)], gp_ref.at[layer, pl.ds(off, n)], gp_l.at[layer, m]
        )

    def grad_tiles(layer, m, left, right):
        off, n = MATS[m]
        if layer == 0:
            gp_copy(1, m).wait()

        def body(i, carry):
            at = pl.ds(pl.multiple_of(off + i * TILE, TILE), TILE)
            gv[at, :] = tm(left[:, cols_of(i)], right[...]).astype(bf16)
            return carry

        lax.fori_loop(0, n // TILE, body, 0)
        gp_copy(layer, m).start()

    cot_copy.wait()
    gg[...] = jnp.zeros_like(gg)

    for layer in (1, 0):
        st = 5 if layer == 1 else 7
        for h in range(HALVES):
            at = rows_of(h)
            if layer == 0:
                ag_wait(5, h, gb.at[1])

            def d_up_tile(j, carry):
                cols = cols_of(j)
                rows = pl.ds(pl.multiple_of(2560 + j * TILE, TILE), TILE)
                d_hidden = mm_t(gb[layer + 1, at, :], wb[layer, rows, :])
                up = upb[layer, at, cols]
                t = jnp.tanh(GELU_A * (up + GELU_B * up * up * up))
                slope = 0.5 * (1.0 + t) + 0.5 * up * (1.0 - t * t) * (
                    GELU_A * (1.0 + 3.0 * GELU_B * up * up)
                )
                du[at, cols] = (d_hidden * slope).astype(bf16)
                return carry

            lax.fori_loop(0, D // TILE, d_up_tile, 0)
            if layer == 1:
                mlp_out(1, h)
            rs_send(
                st, h,
                lambda j, cols: mm_t(
                    du[at, :], wb[layer, pl.ds(pl.multiple_of(1280 + j * TILE, TILE), TILE), :]
                ),
            )
        grad_tiles(layer, 3, hb.at[layer], gb.at[layer + 1])
        for h in range(HALVES):
            dn = rs_take(st, h)
            dx, gain = norm_back(dn, mid[layer, own(h), :], gn[layer, 1:2, :])
            dm = gb[layer + 1, chunk(h, z), :].astype(f32) + dx
            dmid[own(h), :] = dm
            gg[2 * layer + 1 : 2 * layer + 2, :] += gain
            ag_send(st - 1, h, mb.at[layer], dm)
        grad_tiles(layer, 2, nm.at[layer], du)
        for h in range(HALVES):
            ag_wait(st - 1, h, mb.at[layer])
            attention_back(layer, h)
            at = rows_of(h)
            rs_send(
                st + 1, h,
                lambda j, cols: mm(dqb[0, at, :], wb[layer, 0:ATT, cols])
                + mm(dqb[1, at, :], wb[layer, ATT : 2 * ATT, cols])
                + mm(dqb[2, at, :], wb[layer, 2 * ATT : 3 * ATT, cols]),
            )
        if layer == 0:
            gp_copy(1, 0).wait()
            gp_copy(1, 1).wait()
        for i in range(3):
            gv[i * ATT : (i + 1) * ATT, :] = tm(dqb[i], nb[layer]).astype(bf16)
        gp_copy(layer, 0).start()
        gv[960:1280, :] = tm(ct[layer], mb[layer]).astype(bf16)
        gp_copy(layer, 1).start()
        for h in range(HALVES):
            dn = rs_take(st + 1, h)
            dx, gain = norm_back(dn, sx[layer, own(h), :], gn[layer, 0:1, :])
            gg[2 * layer : 2 * layer + 1, :] += gain
            ag_send(st, h, gb.at[layer], dmid[own(h), :] + dx)

    def gg_copy(d):
        return remote(gg, ggr.at[d - 1], gg_s.at[d - 1], gg_r.at[d - 1], z_peer[d])

    for d in (1, 2, 3):
        gg_copy(d).start()

    for h in range(HALVES):
        ag_wait(7, h, gb.at[0])
        at = rows_of(h)
        low = gb[0, at, :]
        before = pre[at, :]
        sig = jax.nn.sigmoid(before)
        d_pre = (
            mm_t(low, w_hid_ref[...]) * (sig * (1.0 + before * (1.0 - sig)))
        ).astype(bf16)
        dctx[at, :] = d_pre
        points = mm_t(d_pre, w_in_ref[...])
        points = points + jnp.where(z == 0, mm_t(low, w_res_ref[...]), 0.0)
        gpad[at, :] = points
    points = gpad[...]
    high = points.astype(bf16)
    low = (points - high.astype(f32)).astype(bf16)
    row = lax.broadcasted_iota(jnp.int32, (ROWS, ROWS), 0)
    col = lax.broadcasted_iota(jnp.int32, (ROWS, ROWS), 1)
    swap = jnp.where(
        ((row >> 4) == (col & 15)) & ((row & 15) == (col >> 4)), 1.0, 0.0
    ).astype(bf16)
    points = mm(swap, high) + mm(swap, low)
    for k in range(8):
        dps[k, :, 0:64] = points[k * 32 : (k + 1) * 32]
        dps[k, :, 64:128] = jnp.zeros((32, 64), f32)
    me = s * 4 + z

    def dp_copy(d):
        to = lax.rem(me + d, 8)
        return remote(
            dps.at[to], dpr.at[me], dp_s.at[d - 1], dp_r.at[d - 1],
            (lax.div(to, 4), dp, lax.rem(to, 4)),
        )

    for d in range(1, 8):
        dp_copy(d).start()
    dpr[me] = dps[me]

    grad_low = gb[0]
    hid = tm(tokh[...], grad_low).astype(bf16)
    res = tm(patch_ref[...], grad_low).astype(bf16)
    inn = tm(patch_ref[...], dctx[...]).astype(bf16)
    for sec in range(2):
        lanes = slice(sec * 640, sec * 640 + 640)
        gt[sec, 0:160, 0:640] = hid[0:160, lanes]
        gt[sec, 0:160, 640:1280] = hid[160:320, lanes]
        gt[sec, 160:192, 0:640] = res[0:32, lanes]
        gt[sec, 160:192, 640:1280] = res[32:64, lanes]
        gt[sec, 192:224, :] = jnp.zeros((32, D), bf16)
        gt[sec, 192:224, 0:320] = inn[sec * 32 : sec * 32 + 32]
    total = gg[...]
    for d in (1, 2, 3):
        gg_copy(d).wait_recv()
        total = total + ggr[d - 1]
    for sec in range(2):
        gt[sec, 224:256, :] = jnp.concatenate(
            [total[2 * sec : 2 * sec + 2], jnp.zeros((30, D), f32)], axis=0
        ).astype(bf16)

    def gt_copy(sec):
        return pltpu.make_async_copy(
            gt.at[sec], gp_ref.at[sec, pl.ds(LAYER_ROWS, PACK_ROWS - LAYER_ROWS)], gp_l.at[sec, 4]
        )

    for sec in range(2):
        gt_copy(sec).start()
    for d in range(1, 8):
        dp_copy(d).wait_recv()
    for sec in range(2):
        points_ref[sec] = dpr[4 * sec] + dpr[4 * sec + 1] + dpr[4 * sec + 2] + dpr[4 * sec + 3]

    for m in range(4):
        for k in range(2):
            w_quarter(m, k).wait_send()
        w_forward(m).wait_send()
        gp_copy(0, m).wait()
    gn_send.wait_send()
    for sec in range(2):
        gt_copy(sec).wait()
    for h in range(HALVES):
        for d in (1, 2, 3):
            rs_copy(7, h, d).wait_send()
            rs_copy(8, h, d).wait_send()
            gathered = [nb.at[0], nm.at[0], nb.at[1], nm.at[1], mb.at[1], gb.at[1], mb.at[0], gb.at[0]]
            for i, ref in enumerate(gathered):
                ag_copy(i, h, d, ref).wait_send()
        for layer in range(2):
            src = ob.at[layer, own(h)]
            dst = lo_ref.at[pl.ds(pl.multiple_of(s * ROWS + h * RH + z * RQ, RQ), RQ)]

            @pl.when(s == layer)
            def _():
                pltpu.make_async_copy(src, dst, lo_l.at[h]).wait()

            @pl.when(s != layer)
            def _():
                remote(src, dst, lo_s.at[layer, 0, h], lo_r.at[s, 0, h], (layer, dp, z)).wait_send()

            for d in (1, 2, 3):
                remote(
                    src, dst, lo_s.at[layer, d, h], lo_r.at[s, d, h], (layer, dp, z_at[d])
                ).wait_send()
        for d in range(4):
            remote(
                ob.at[0, own(h)], lo_ref.at[pl.ds(0, RQ)], lo_s.at[0, d, h],
                lo_r.at[other, d, h], across[d],
            ).wait_recv()
        for d in (1, 2, 3):
            remote(
                ob.at[0, own(h)], lo_ref.at[pl.ds(0, RQ)], lo_s.at[0, d, h],
                lo_r.at[s, d, h], z_peer[d],
            ).wait_recv()
    for d in (1, 2, 3):
        gg_copy(d).wait_send()
    for d in range(1, 8):
        dp_copy(d).wait_send()


def run_layers(patch_in, w_in, w_hid, w_res, gains, wq, wo, wu, wd, cotangent):
    cos, sin, turn = rotary_arrays()
    vm = pl.BlockSpec(memory_space=pltpu.VMEM)
    hbm = pl.BlockSpec(memory_space=pl.ANY)
    dma = pltpu.SemaphoreType.DMA
    scratch = [
        pltpu.VMEM((2, LAYER_ROWS, D), bf16),
        pltpu.VMEM((2, 8, D), f32),
        pltpu.VMEM((ROWS, ATT), bf16),
        pltpu.VMEM((ROWS, ATT), f32),
        pltpu.VMEM((2, ROWS // 4, D), f32),
        pltpu.VMEM((2, ROWS // 4, D), f32),
        pltpu.VMEM((2, ROWS, D), bf16),
        pltpu.VMEM((2, ROWS, D), bf16),
        pltpu.VMEM((2, 3, ROWS, ATT), bf16),
        pltpu.VMEM((2, ROWS // BLOCK, HEADS_HERE * BLOCK, BLOCK), f32),
        pltpu.VMEM((2, ROWS, ATT), bf16),
        pltpu.VMEM((2, ROWS, D), f32),
        pltpu.VMEM((2, ROWS, D), bf16),
        pltpu.VMEM((3, ROWS, D), bf16),
        pltpu.VMEM((2, ROWS, D), bf16),
        pltpu.VMEM((ROWS, D), bf16),
        pltpu.VMEM((3, ROWS, ATT), bf16),
        pltpu.VMEM((ROWS, ATT), bf16),
        pltpu.VMEM((LAYER_ROWS, D), bf16),
        pltpu.VMEM((2, PACK_ROWS - LAYER_ROWS, D), bf16),
        pltpu.VMEM((2, ROWS, D), bf16),
        pltpu.VMEM((9, 3, ROWS // 4, D), bf16),
        pltpu.VMEM((ROWS // 4, D), f32),
        pltpu.VMEM((2, ROWS // 4, D), bf16),
        pltpu.VMEM((8, D), f32),
        pltpu.VMEM((3, 8, D), f32),
        pltpu.VMEM((8, 32, 128), f32),
        pltpu.VMEM((8, 32, 128), f32),
        pltpu.VMEM((ROWS, 64), f32),
        dma((4,)), dma((4, 2)), dma((4, 2)), dma((4,)), dma((4,)),
        dma, dma, dma, dma,
        dma((9, HALVES, 3)), dma((9, HALVES, 3)),
        dma((8, HALVES, 3)), dma((8, HALVES, 3)),
        dma((HALVES,)), dma((2, 4, HALVES)), dma((2, 4, HALVES)),
        dma((3,)), dma((3,)), dma((7,)), dma((7,)),
        dma((2, 5)),
    ]
    return pl.pallas_call(
        layers_kernel,
        out_shape=(
            jax.ShapeDtypeStruct((2 * ROWS, D), bf16),
            jax.ShapeDtypeStruct((2, PACK_ROWS, D), bf16),
            jax.ShapeDtypeStruct((2, 32, 128), f32),
        ),
        in_specs=[vm] * 5 + [hbm] * 5 + [vm] * 3,
        out_specs=(hbm, hbm, vm),
        scratch_shapes=scratch,
        compiler_params=pltpu.CompilerParams(
            collective_id=0, has_side_effects=True, vmem_limit_bytes=62 * 2**20
        ),
        cost_estimate=pl.CostEstimate(
            flops=15_000_000_000, bytes_accessed=50_000_000, transcendentals=4_000_000
        ),
        name="layers",
    )(
        patch_in, w_in, w_hid, w_res, gains, wq, wo, wu, wd, cotangent,
        jnp.asarray(cos, f32), jnp.asarray(sin, f32), jnp.asarray(turn, bf16),
    )


HALF = PACK_ROWS // 2
PART = HALF // 2


def sum_kernel(
    gp_ref, out_ref,
    mine, theirs, ra1, rb1, ca, cb, ra2, rb2,
    in_l, c_s, c_r, a1_s, a1_r, b1_s, b1_r, a2_s, a2_r, b2_s, b2_r,
    a3_s, a3_r, b3_s, b3_r, a4_s, a4_r, b4_s, b4_r, c5_s, c5_r,
):
    s, dp, z, x, yh, c = places()
    y = 2 * yh + s
    core = (s, dp + 1 - 2 * c, z)
    x_at = [x] + [lax.rem(x + d, 4) for d in (1, 2, 3)]
    y_at = [y] + [lax.rem(y + d, 4) for d in (1, 2, 3)]
    x_peer = [None] + [(s, x_at[d] * 4 + 2 * yh + c, z) for d in (1, 2, 3)]
    y_peer = [None] + [
        (lax.rem(y_at[d], 2), x * 4 + 2 * lax.div(y_at[d], 2) + c, z) for d in (1, 2, 3)
    ]

    barrier = pltpu.get_barrier_semaphore()
    peers = x_peer[1:] + y_peer[1:] + [core]
    for peer in peers:
        pl.semaphore_signal(barrier, inc=1, device_id=peer, device_id_type=MESH)
    pl.semaphore_wait(barrier, len(peers))

    def remote(src, dst, ssem, rsem, peer):
        return pltpu.make_async_remote_copy(
            src_ref=src, dst_ref=dst, send_sem=ssem, recv_sem=rsem,
            device_id=peer, device_id_type=MESH,
        )

    def add_into(dst, srcs, rows, step):
        def body(i, carry):
            at = pl.ds(pl.multiple_of(i * step, step), step)
            total = dst[at, :].astype(f32)
            for src in srcs:
                total = total + src[at, :].astype(f32)
            dst[at, :] = total.astype(bf16)
            return carry

        lax.fori_loop(0, rows // step, body, 0)

    keep = pl.ds(pl.multiple_of(c * HALF, HALF), HALF)
    give = pl.ds(pl.multiple_of((1 - c) * HALF, HALF), HALF)
    for layer in range(2):
        remote(
            gp_ref.at[layer, give], theirs.at[layer], c_s.at[layer], c_r.at[layer], core
        ).start()
        pltpu.make_async_copy(gp_ref.at[layer, keep], mine.at[layer], in_l.at[layer]).start()
    for layer in range(2):
        pltpu.make_async_copy(gp_ref.at[layer, keep], mine.at[layer], in_l.at[layer]).wait()
        remote(
            gp_ref.at[layer, give], theirs.at[layer], c_s.at[layer], c_r.at[layer], core
        ).wait()
        add_into(mine.at[layer], [theirs.at[layer]], HALF, 64)

    def a1(d):
        src = mine.at[
            lax.rem(y_at[d], 2), pl.ds(pl.multiple_of(lax.div(y_at[d], 2) * 512, 512), 512)
        ]
        return remote(src, ra1.at[d - 1], a1_s.at[d - 1], a1_r.at[d - 1], y_peer[d])

    def b1(d, layer):
        src = mine.at[layer, pl.ds(pl.multiple_of(PART + x_at[d] * 256, 256), 256)]
        return remote(
            src, rb1.at[d - 1, layer], b1_s.at[d - 1, layer], b1_r.at[d - 1, layer], x_peer[d]
        )

    for d in (2, 1, 3):
        a1(d).start()
        for layer in range(2):
            b1(d, layer).start()
    ca[...] = mine[s, pl.ds(pl.multiple_of(yh * 512, 512), 512), :]
    for layer in range(2):
        cb[layer] = mine[layer, pl.ds(pl.multiple_of(PART + x * 256, 256), 256), :]
    for d in (1, 3, 2):
        a1(d).wait_recv()
        for layer in range(2):
            b1(d, layer).wait_recv()
    add_into(ca, [ra1.at[i] for i in range(3)], 512, 32)
    for layer in range(2):
        add_into(cb.at[layer], [rb1.at[i, layer] for i in range(3)], 256, 32)

    def a2(d):
        src = ca.at[pl.ds(pl.multiple_of(x_at[d] * 128, 128), 128)]
        return remote(src, ra2.at[d - 1], a2_s.at[d - 1], a2_r.at[d - 1], x_peer[d])

    def b2(d):
        src = cb.at[
            lax.rem(y_at[d], 2), pl.ds(pl.multiple_of(lax.div(y_at[d], 2) * 128, 128), 128)
        ]
        return remote(src, rb2.at[d - 1], b2_s.at[d - 1], b2_r.at[d - 1], y_peer[d])

    for d in (2, 1, 3):
        a2(d).start()
        b2(d).start()
    for d in (1, 3, 2):
        a2(d).wait_recv()
        b2(d).wait_recv()
    own_a = pl.ds(pl.multiple_of(c * HALF + yh * 512 + x * 128, 128), 128)
    own_b = pl.ds(pl.multiple_of(c * HALF + PART + x * 256 + yh * 128, 128), 128)

    def finish(dst, chunk_ref, off, parts):
        for i in range(4):
            at = pl.ds(pl.multiple_of(off + 32 * i, 32), 32)
            total = chunk_ref[at, :].astype(f32)
            for k in range(3):
                total = total + parts[k, pl.ds(32 * i, 32), :].astype(f32)
            out_ref[pl.ds(pl.multiple_of(dst + 32 * i, 32), 32), :] = total.astype(bf16)

    finish(c * HALF + yh * 512 + x * 128, ca, x * 128, ra2)
    finish(c * HALF + PART + x * 256 + yh * 128, cb.at[s], yh * 128, rb2)

    def a3(d):
        return remote(
            out_ref.at[own_a], out_ref.at[own_a], a3_s.at[d - 1], a3_r.at[d - 1], x_peer[d]
        )

    b3 = remote(out_ref.at[own_b], out_ref.at[own_b], b3_s, b3_r, y_peer[2])
    for d in (2, 1, 3):
        a3(d).start()
    b3.start()
    for d in (1, 3, 2):
        a3(d).wait_recv()
    b3.wait_recv()
    wide_a = pl.ds(pl.multiple_of(c * HALF + yh * 512, 512), 512)
    wide_b = pl.ds(pl.multiple_of(c * HALF + PART + x * 256, 256), 256)
    a4 = remote(out_ref.at[wide_a], out_ref.at[wide_a], a4_s, a4_r, y_peer[2])

    def b4(d):
        return remote(
            out_ref.at[wide_b], out_ref.at[wide_b], b4_s.at[d - 1], b4_r.at[d - 1], x_peer[d]
        )

    a4.start()
    for d in (2, 1, 3):
        b4(d).start()
    for d in (1, 3, 2):
        b4(d).wait_recv()
    a4.wait_recv()
    c5 = remote(out_ref.at[keep], out_ref.at[keep], c5_s, c5_r, core)
    c5.start()
    c5.wait()
    for d in (1, 2, 3):
        a1(d).wait_send()
        for layer in range(2):
            b1(d, layer).wait_send()
        a2(d).wait_send()
        b2(d).wait_send()
        a3(d).wait_send()
        b4(d).wait_send()
    b3.wait_send()
    a4.wait_send()


def run_sum(packed):
    dma = pltpu.SemaphoreType.DMA
    return pl.pallas_call(
        sum_kernel,
        out_shape=jax.ShapeDtypeStruct((PACK_ROWS, D), bf16),
        in_specs=[pl.BlockSpec(memory_space=pl.ANY)],
        out_specs=pl.BlockSpec(memory_space=pltpu.VMEM),
        scratch_shapes=[
            pltpu.VMEM((2, HALF, D), bf16),
            pltpu.VMEM((2, HALF, D), bf16),
            pltpu.VMEM((3, 512, D), bf16),
            pltpu.VMEM((3, 2, 256, D), bf16),
            pltpu.VMEM((512, D), bf16),
            pltpu.VMEM((2, 256, D), bf16),
            pltpu.VMEM((3, 128, D), bf16),
            pltpu.VMEM((3, 128, D), bf16),
            dma((2,)), dma((2,)), dma((2,)),
            dma((3,)), dma((3,)), dma((3, 2)), dma((3, 2)),
            dma((3,)), dma((3,)), dma((3,)), dma((3,)),
            dma((3,)), dma((3,)), dma, dma,
            dma, dma, dma((3,)), dma((3,)),
            dma, dma,
        ],
        compiler_params=pltpu.CompilerParams(
            collective_id=1, has_side_effects=True, vmem_limit_bytes=56 * 2**20
        ),
        cost_estimate=pl.CostEstimate(
            flops=60_000_000, bytes_accessed=40_000_000, transcendentals=0
        ),
        name="gradient_sum",
    )(packed)


def per_device(
    series, missing, w_in, w_hid, w_res, gain_attn, w_qkv, w_out, gain_mlp, w_up, w_down, cotangent
):
    s = lax.axis_index("section")
    contexts = series.shape[0] // 2
    keep = (1 - missing).astype(f32)
    values = lax.dynamic_slice_in_dim(series * keep, s * contexts, contexts, 0)
    flags = lax.dynamic_slice_in_dim(missing, s * contexts, contexts, 0).astype(f32)
    patch_in = jnp.concatenate(
        [values.reshape(ROWS, PATCH), flags.reshape(ROWS, PATCH)], axis=1
    ).astype(bf16)
    gains = jnp.concatenate([gain_attn, gain_mlp, jnp.zeros((6, D), f32)], axis=0)
    wq = jnp.transpose(w_qkv[0], (1, 2, 0)).reshape(3 * ATT, D)
    layer_out, packed, points = run_layers(
        patch_in, w_in, w_hid, w_res, gains, wq, w_out[0], w_up[0], w_down[0], cotangent
    )
    total = run_sum(packed).astype(f32)
    points = points[:, :, :PATCH].reshape(2, 2, contexts, PATCH)
    points = jnp.transpose(points, (0, 2, 1, 3)).reshape(2 * contexts, 2 * PATCH)
    block = s * 4 + lax.axis_index("tensor")
    keep_here = lax.dynamic_slice_in_dim(keep, block * 2 * PATCH, 2 * PATCH, 1)
    series_grad = points * keep_here
    g_qkv = jnp.transpose(total[0:960].reshape(3, ATT, D), (2, 0, 1))
    hid = total[3840:4000]
    res = total[4000:4032]
    return (
        layer_out[None],
        series_grad,
        total[4032:4064, :ATT],
        jnp.concatenate([hid[:, :640], hid[:, 640:]], axis=0),
        jnp.concatenate([res[:, :640], res[:, 640:]], axis=0),
        total[4064:4065],
        g_qkv[None],
        total[960:1280][None],
        total[4065:4066],
        total[1280:2560][None],
        total[2560:3840][None],
    )


def solution(mesh):
    in_specs = (
        P("dp", None),
        P("dp", None),
        P(None, "tensor"),
        P("tensor", None),
        P(),
        P("section", None),
        P("section", None, None, "tensor"),
        P("section", "tensor", None),
        P("section", None),
        P("section", None, "tensor"),
        P("section", "tensor", None),
        P("dp", None),
    )
    out_specs = (
        P("section", "dp", None),
        P("dp", ("section", "tensor")),
        P("section", "tensor"),
        P("tensor", "section"),
        P(None, "section"),
        P("section", None),
        P("section", None, None, "tensor"),
        P("section", "tensor", None),
        P("section", None),
        P("section", None, "tensor"),
        P("section", "tensor", None),
    )
    return jax.shard_map(
        per_device, mesh=mesh, in_specs=in_specs, out_specs=out_specs, check_vma=False
    )
```

```python
import math

import jax
import jax.numpy as jnp
import numpy as np
from jax import lax
from jax.experimental import pallas as pl
from jax.experimental.pallas import tpu as pltpu
from jax.sharding import PartitionSpec as P

D = 1280
HEADS_HERE = 4
HEAD_DIM = 80
ATT = HEADS_HERE * HEAD_DIM
PATCH = 32
PATCHES = 16
ROWS = 256
HALVES = 2
RH = ROWS // HALVES
RQ = RH // 4
TILE = 256
BLOCK = 128
MATS = ((0, 960), (960, 320), (1280, 1280), (2560, 1280))
PIECES = (
    (0, 512, 0), (512, 448, 0), (960, 320, 1), (1280, 640, 2), (1920, 640, 2), (2560, 640, 3), (3200, 640, 3),
)
N_PIECES = len(PIECES)
LAYER_ROWS = 3840
PACK_ROWS = 4096
MESH = pl.DeviceIdType.MESH
f32 = jnp.float32
bf16 = jnp.bfloat16
eps_norm = 1e-06
masked_score = -1e30
GELU_A = math.sqrt(2.0 / math.pi)
GELU_B = 0.044715


def mm(a, b):
    return lax.dot_general(a, b, (((1,), (0,)), ((), ())), preferred_element_type=f32)


def mm_t(a, b):
    return lax.dot_general(a, b, (((1,), (1,)), ((), ())), preferred_element_type=f32)


def tm(a, b):
    return lax.dot_general(a, b, (((0,), (0,)), ((), ())), preferred_element_type=f32)


def unrolled(count, body):
    for j in range(count):
        body(j, 0)


def rotary_arrays():
    half = HEAD_DIM // 2
    position = (np.arange(BLOCK) % PATCHES).astype(np.float32)
    frequency = np.exp(
        np.arange(half, dtype=np.float32) * np.float32(-2.0 * math.log(10000.0) / HEAD_DIM)
    )
    angles = position[:, None] * frequency[None, :]
    lane = np.arange(ATT) % half
    turn = np.zeros((ATT, ATT), np.float32)
    for j in range(ATT):
        if j % HEAD_DIM < half:
            turn[j + half, j] = -1.0
        else:
            turn[j - half, j] = 1.0
    return np.cos(angles)[:, lane], np.sin(angles)[:, lane], turn


def places():
    s = lax.axis_index("section")
    dp = lax.axis_index("dp")
    z = lax.axis_index("tensor")
    c = lax.rem(dp, 2)
    yh = lax.rem(lax.div(dp, 2), 2)
    x = lax.div(dp, 4)
    return s, dp, z, x, yh, c


def layers_kernel(
    patch_ref, w_in_ref, w_hid_ref, w_res_ref, gains_ref, wq_ref, wo_ref, wu_ref, wd_ref,
    cot_ref, cos_ref, sin_ref, turn_ref,
    lo_ref, go_ref, to_ref, points_ref,
    wb, gn, tokh, pre, sx, mid, nb, nm, qb, pb, ct, upb, hb, gb, mb, du, dqb, dctx, gv, gt,
    sb, rb, dmid, ob, gg, ggr, dps, dpr, gpad,
    th, r1, r2, ra1, ra2, rb3, tt, tx, ty,
    w_loc, w_s, w_r, x_s, x_r, f_s, f_r, gn_l, gn_s, gn_r, cot_l,
    rs_s, rs_r, ag_s, ag_r, lo_l, lo_s, lo_r, gg_s, gg_r, dp_s, dp_r,
    e_s, e_r, e_l, t_s, t_r, t_l, free_th, free_r1, free_r2,
):
    s, dp, z, x, yh, c = places()
    other = 1 - s
    z_peer = [None] + [(s, dp, lax.rem(z + d, 4)) for d in (1, 2, 3)]
    z_at = [z] + [lax.rem(z + d, 4) for d in (1, 2, 3)]
    y_a = (other, dp, z)
    y_b = (other, dp + 2 - 4 * yh, z)
    core = (s, dp + 1 - 2 * c, z)
    across = [(other, dp, z_at[d]) for d in range(4)]
    y = 2 * yh + s
    x_at = [x] + [lax.rem(x + d, 4) for d in (1, 2, 3)]
    y_at = [y] + [lax.rem(y + d, 4) for d in (1, 2, 3)]
    x_peer = [None] + [(s, x_at[d] * 4 + 2 * yh + c, z) for d in (1, 2, 3)]
    y_peer = [None] + [
        (lax.rem(y_at[d], 2), x * 4 + 2 * lax.div(y_at[d], 2) + c, z) for d in (1, 2, 3)
    ]
    x_up, x_down = x_peer[1], x_peer[3]
    w_refs = (wq_ref, wo_ref, wu_ref, wd_ref)

    barrier = pltpu.get_barrier_semaphore()
    peers = z_peer[1:] + across + [y_b, core] + x_peer[1:] + [y_peer[2]]
    for peer in peers:
        pl.semaphore_signal(barrier, inc=1, device_id=peer, device_id_type=MESH)
    pl.semaphore_wait(barrier, len(peers))

    def remote(src, dst, ssem, rsem, peer):
        return pltpu.make_async_remote_copy(
            src_ref=src, dst_ref=dst, send_sem=ssem, recv_sem=rsem,
            device_id=peer, device_id_type=MESH,
        )

    odd = lax.rem(x, 2)

    def w_local(m):
        off, n = MATS[m]
        return pltpu.make_async_copy(w_refs[m], wb.at[s, pl.ds(off, n)], w_loc.at[m])

    def share(i, parity, k):
        off, n, m = PIECES[i]
        first = (n // 4 + 31) // 32 * 16
        size = first if k == 0 else n // 4 - first
        return (2 * c + parity) * (n // 4) + k * first, size

    def w_over_y(i, k):
        off, n, m = PIECES[i]
        at, size = share(i, odd, k)
        src = w_refs[m].at[pl.ds(pl.multiple_of(off - MATS[m][0] + at, 16), size)]
        dst = wb.at[s, pl.ds(pl.multiple_of(off + at, 16), size)]
        return remote(src, dst, w_s.at[i, k], w_r.at[i, k], (y_a, y_b)[k])

    def w_over_x(i, k, parity):
        at, size = share(i, parity, k)
        ref = wb.at[other, pl.ds(pl.multiple_of(PIECES[i][0] + at, 16), size)]
        return remote(ref, ref, x_s.at[i, k], x_r.at[i, k], (x_up, x_down)[k])

    def w_to_core(i, q):
        off, n, m = PIECES[i]
        parity = odd if q == 0 else 1 - odd
        ref = wb.at[other, pl.ds(pl.multiple_of(off + (2 * c + parity) * (n // 4), 16), n // 4)]
        return remote(ref, ref, f_s.at[i, q], f_r.at[i, q], core)

    def weights(layer, steps):
        @pl.when(s != layer)
        def _():
            for step, i in steps:
                if step == "y":
                    for k in range(2):
                        w_over_y(i, k).wait_recv()
                        w_over_x(i, k, odd).start()
                    w_to_core(i, 0).start()
                elif step == "x":
                    for k in range(2):
                        w_over_x(i, k, 1 - odd).wait_recv()
                    w_to_core(i, 1).start()
                else:
                    for q in range(2):
                        w_to_core(i, q).wait_recv()

    gn_copy = pltpu.make_async_copy(gains_ref, gn.at[s], gn_l)
    gn_send = remote(gains_ref, gn.at[s], gn_s, gn_r, y_a)
    cot_copy = pltpu.make_async_copy(
        cot_ref.at[pl.ds(pl.multiple_of(s * ROWS, ROWS), ROWS)], gb.at[0], cot_l
    )
    gn_send.start()
    gn_copy.start()
    for i in range(N_PIECES):
        for k in range(2):
            w_over_y(i, k).start()
    for m in range(4):
        w_local(m).start()
    cot_copy.start()

    def rows_of(h):
        return pl.ds(h * RH, RH)

    def chunk(h, zz):
        return pl.ds(pl.multiple_of(h * RH + zz * RQ, RQ), RQ)

    def cols_of(j):
        return pl.ds(j * TILE, TILE)

    def rs_copy(st, h, d, cols=None):
        src = sb.at[st % 2, chunk(h, z_at[d])]
        dst = rb.at[st % 2, d - 1, pl.ds(h * RQ, RQ)]
        if cols is not None:
            src = sb.at[st % 2, chunk(h, z_at[d]), cols]
            dst = rb.at[st % 2, d - 1, pl.ds(h * RQ, RQ), cols]
        return remote(src, dst, rs_s.at[st, h, d - 1], rs_r.at[st, h, d - 1], z_peer[d])

    def rs_send(st, h, produce):
        if st >= 2:
            for d in (1, 2, 3):
                rs_copy(st - 2, h, d).wait_send()

        def body(j, carry):
            cols = cols_of(j)
            sb[st % 2, rows_of(h), cols] = produce(j, cols).astype(bf16)
            for d in (2, 1, 3):
                rs_copy(st, h, d, cols).start()

        unrolled(D // TILE, body)

    def rs_take(st, h):
        total = sb[st % 2, chunk(h, z), :].astype(f32)
        for d in (1, 3, 2):
            rs_copy(st, h, d).wait_recv()
            total = total + rb[st % 2, d - 1, pl.ds(h * RQ, RQ), :].astype(f32)
        return total

    def ag_copy(st, h, d, dst):
        at = dst.at[chunk(h, z)]
        return remote(at, at, ag_s.at[st, h, d - 1], ag_r.at[st, h, d - 1], z_peer[d])

    def ag_send(st, h, dst, value):
        dst[chunk(h, z), :] = value.astype(bf16)
        for d in (2, 1, 3):
            ag_copy(st, h, d, dst).start()

    def ag_wait(st, h, dst):
        for d in (1, 3, 2):
            ag_copy(st, h, d, dst).wait_recv()

    def own(h):
        return pl.ds(h * RQ, RQ)

    def scale_of(v):
        return lax.rsqrt(jnp.mean(v * v, axis=-1, keepdims=True) + eps_norm)

    def norm(v, g):
        return v * scale_of(v) * g

    def norm_back(dn, v, g):
        r = scale_of(v)
        weighted = g * dn
        inner = jnp.mean(v * weighted, axis=-1, keepdims=True)
        return r * weighted - v * (r * r * r * inner), jnp.sum(dn * v * r, axis=0, keepdims=True)

    head_lane = lax.broadcasted_iota(jnp.int32, (1, ATT), 1)
    head_mask = [
        (head_lane >= HEAD_DIM * h) & (head_lane < HEAD_DIM * (h + 1)) for h in range(HEADS_HERE)
    ]

    def spread(v):
        wide = v.astype(f32)
        return jnp.concatenate(
            [jnp.where(m, wide, 0.0) for m in head_mask], axis=0
        ).astype(bf16)

    def gather(v):
        total = jnp.where(head_mask[0], v[:BLOCK], 0.0)
        for h in range(1, HEADS_HERE):
            total = total + jnp.where(head_mask[h], v[h * BLOCK : (h + 1) * BLOCK], 0.0)
        return total

    def turned(v, sign):
        high = v.astype(bf16)
        low = (v - high.astype(f32)).astype(bf16)
        swapped = mm(high, turn_ref[...]) + mm(low, turn_ref[...])
        if sign < 0:
            swapped = -swapped
        return v * cos_ref[...] + swapped * sin_ref[...]

    inv = 1.0 / math.sqrt(HEAD_DIM)

    def blocks_of(h):
        return range(h * RH // BLOCK, (h + 1) * RH // BLOCK)

    def attention_front(layer, h):
        for b in blocks_of(h):
            at = pl.ds(b * BLOCK, BLOCK)
            normed = nb[layer, at, :]
            q = turned(mm_t(normed, wb[layer, 0:ATT, :]), 1).astype(bf16)
            k = turned(mm_t(normed, wb[layer, ATT : 2 * ATT, :]), 1).astype(bf16)
            v = mm_t(normed, wb[layer, 2 * ATT : 3 * ATT, :]).astype(bf16)
            qb[layer, 0, at, :] = q
            qb[layer, 1, at, :] = k
            qb[layer, 2, at, :] = v
            scores = mm_t(spread(q), k) * inv
            row = lax.broadcasted_iota(jnp.int32, scores.shape, 0) & (BLOCK - 1)
            col = lax.broadcasted_iota(jnp.int32, scores.shape, 1)
            allowed = (col <= row) & (col >= (row & (BLOCK - PATCHES)))
            scores = jnp.where(allowed, scores, masked_score)
            e = jnp.exp(scores - jnp.max(scores, axis=-1, keepdims=True))
            probs = e / jnp.sum(e, axis=-1, keepdims=True)
            pb[layer, b] = probs
            ct[layer, at, :] = gather(mm(probs.astype(bf16), v)).astype(bf16)

    def attention_back(layer, h):
        for b in blocks_of(h):
            at = pl.ds(b * BLOCK, BLOCK)
            spread_d = spread(mm_t(mb[at, :], wb[layer, 960:1280, :]).astype(bf16))
            spread_q = spread(qb[layer, 0, at, :])
            k = qb[layer, 1, at, :]
            v = qb[layer, 2, at, :]
            probs = pb[layer, b]
            d_probs = mm_t(spread_d, v)
            d_scores = (
                probs * (d_probs - jnp.sum(probs * d_probs, axis=-1, keepdims=True))
            ).astype(bf16)
            d_q = gather(mm(d_scores, k)) * inv
            d_k = tm(d_scores, spread_q) * inv
            dqb[0, at, :] = turned(d_q, -1).astype(bf16)
            dqb[1, at, :] = turned(d_k, -1).astype(bf16)
            dqb[2, at, :] = tm(probs.astype(bf16), spread_d).astype(bf16)

    for h in range(HALVES):
        at = rows_of(h)
        before = mm(patch_ref[at, :], w_in_ref[...])
        pre[at, :] = before
        tokh[at, :] = (before * jax.nn.sigmoid(before)).astype(bf16)
        rs_send(0, h, lambda j, cols: mm(tokh[at, :], w_hid_ref[:, cols]))
    gn_copy.wait()
    gn_send.wait_recv()
    for m in range(4):
        w_local(m).wait()
    for h in range(HALVES):
        weights(0, [("y", h)])
        stream = rs_take(0, h) + mm(patch_ref[chunk(h, z), :], w_res_ref[...])
        sx[0, own(h), :] = stream
        ag_send(0, h, nb.at[0], norm(stream, gn[0, 0:1, :]))
    weights(0, [("y", 2), ("x", 0), ("x", 1), ("core", 0), ("core", 1)])

    def send_out(layer, h):
        dst = lo_ref.at[pl.ds(pl.multiple_of(s * ROWS + h * RH + z * RQ, RQ), RQ)]
        src = ob.at[layer, own(h)]

        @pl.when(s == layer)
        def _():
            pltpu.make_async_copy(src, dst, lo_l.at[h]).start()

        @pl.when(s != layer)
        def _():
            remote(src, dst, lo_s.at[layer, 0, h], lo_r.at[s, 0, h], (layer, dp, z)).start()

        for d in (1, 2, 3):
            remote(
                src, dst, lo_s.at[layer, d, h], lo_r.at[s, d, h], (layer, dp, z_at[d])
            ).start()

    def mlp_out(layer, h):
        out = (mid[layer, own(h), :] + rs_take(2 + 2 * layer, h)).astype(bf16)
        ob[layer, own(h), :] = out
        return out

    for layer in range(2):
        for h in range(HALVES):
            ag_wait(2 * layer, h, nb.at[layer])
            attention_front(layer, h)
            if h == 0 and layer == 0:
                weights(0, [("y", 3), ("x", 2), ("core", 2)])
            if h == 0 and layer == 1:
                weights(1, [("core", 2)])
            at = rows_of(h)
            rs_send(
                1 + 2 * layer, h, lambda j, cols: mm(ct[layer, at, :], wb[layer, 960:1280, cols])
            )
        if layer == 0:
            weights(0, [("y", 4), ("x", 3)])
            weights(1, [("y", 0), ("y", 1), ("y", 2)])
        for h in range(HALVES):
            middle = sx[layer, own(h), :] + rs_take(1 + 2 * layer, h)
            mid[layer, own(h), :] = middle
            ag_send(1 + 2 * layer, h, nm.at[layer], norm(middle, gn[layer, 1:2, :]))
        if layer == 0:
            weights(0, [("y", 5), ("x", 4), ("core", 3), ("core", 4)])
            weights(1, [("y", 3), ("x", 0), ("x", 1), ("x", 2)])
        else:
            weights(1, [("core", 3), ("core", 4)])
        for h in range(HALVES):
            ag_wait(1 + 2 * layer, h, nm.at[layer])
            at = rows_of(h)

            def up_tile(j, carry):
                cols = cols_of(j)
                up = mm(nm[layer, at, :], wb[layer, 1280:2560, cols])
                upb[layer, at, cols] = up
                t = jnp.tanh(GELU_A * (up + GELU_B * up * up * up))
                hb[at, cols] = (0.5 * up * (1.0 + t)).astype(bf16)

            unrolled(D // TILE, up_tile)
            if h == 0 and layer == 0:
                weights(0, [("y", 6), ("x", 5), ("x", 6), ("core", 5), ("core", 6)])
            if h == 0 and layer == 1:
                weights(1, [("core", 5), ("core", 6)])
            rs_send(
                2 + 2 * layer, h, lambda j, cols: mm(hb[at, :], wb[layer, 2560:3840, cols])
            )
        if layer == 0:
            weights(1, [("y", 4), ("y", 5), ("y", 6), ("x", 3)])
            for h in range(HALVES):
                out = mlp_out(0, h)
                stream = out.astype(f32)
                sx[1, own(h), :] = stream
                ag_send(2, h, nb.at[1], norm(stream, gn[1, 0:1, :]))
            weights(1, [("x", 4), ("x", 5), ("x", 6), ("core", 0), ("core", 1)])

    xa = x + 1 - 2 * lax.rem(x, 2)
    xb = 3 - x
    to_xa = (s, xa * 4 + 2 * yh + c, z)
    to_xb = (s, xb * 4 + 2 * yh + c, z)
    j1 = lax.rem(lax.div(x + 1, 2), 2)
    j2 = lax.div(x, 2)
    i1 = lax.div(x, 2)
    i2 = lax.rem(x, 2)
    half_at = (128 + 128 * j1, 384 + 128 * i1)
    half_off = (128 + 128 * (1 - j1), 384 + 128 * (1 - i1))
    quarter_at = (half_at[0] + 64 * j2, half_at[1] + 64 * i2)
    quarter_off = (half_at[0] + 64 * (1 - j2), half_at[1] + 64 * (1 - i2))
    first_peer = (to_xa, to_xb)
    second_peer = (to_xb, to_xa)

    class Group:
        def __init__(self, layer, k):
            self.layer, self.k = layer, k
            self.buf = gv if layer == 1 else wb.at[1]
            self.mine = k * 1280 + c * 640
            self.theirs = k * 1280 + (1 - c) * 640
            self.home = s == layer

        def rows(self, at, n):
            return self.buf.at[pl.ds(pl.multiple_of(self.mine + at, 16), n)]

        def result(self, at, n):
            return go_ref.at[pl.ds(pl.multiple_of(self.mine + at, 16), n)]

        def move(self, i, src, dst, peer):
            return remote(src, dst, e_s.at[self.layer, self.k, i], e_r.at[self.layer, self.k, i], peer)

        def add(self, at, n, sources):
            def body(i, carry):
                here = pl.ds(pl.multiple_of(self.mine + at + i * 16, 16), 16)
                there = pl.ds(pl.multiple_of(i * 16, 16), 16)
                total = self.buf[here, :].astype(f32)
                for source in sources:
                    total = total + source[there, :].astype(f32)
                self.buf[here, :] = total.astype(bf16)
                return carry

            lax.fori_loop(0, n // 16, body, 0)

        def core(self):
            src = self.buf.at[pl.ds(pl.multiple_of(self.theirs, 16), 640)]
            return self.move(0, src, th.at[self.k], core)

        def first(self, b):
            return self.move(1 + b, self.rows(half_off[b], 128), r1.at[self.k, b], first_peer[b])

        def second(self, b):
            return self.move(3 + b, self.rows(quarter_off[b], 64), r2.at[self.k, b], second_peer[b])

        def a_over_y(self, d):
            src = self.rows(64 * lax.div(y_at[d], 2), 64)
            return self.move(4 + d, src, ra1.at[self.k, d - 1], y_peer[d])

        def a_over_x(self, d):
            src = self.rows(64 * yh + 16 * x_at[d], 16)
            return self.move(7 + d, src, ra2.at[self.k, d - 1], x_peer[d])

        def b_over_y(self, d, b):
            src = self.rows(quarter_at[b] + 32 * lax.div(y_at[d], 2), 32)
            return self.move(9 + 2 * d + b, src, rb3.at[self.k, d - 1, b], y_peer[d])

        def a_back_x(self, d):
            at = 64 * yh + 16 * x
            return self.move(16 + d, self.rows(at, 16), self.result(at, 16), x_peer[d])

        def a_back_y(self):
            ref = self.result(64 * yh, 64)
            return self.move(20, ref, ref, y_peer[2])

        def b_back_y(self, b):
            at = quarter_at[b] + 32 * yh
            return self.move(21 + b, self.rows(at, 32), self.result(at, 32), y_peer[2])

        def back_second(self, b):
            ref = self.result(quarter_at[b], 64)
            return self.move(23 + b, ref, ref, second_peer[b])

        def back_first(self, b):
            ref = self.result(half_at[b], 128)
            return self.move(25 + b, ref, ref, first_peer[b])

        def back_core(self):
            ref = self.result(0, 640)
            return self.move(27, ref, ref, core)

        def keep_a(self):
            at = 64 * yh + 16 * x
            return pltpu.make_async_copy(
                self.rows(at, 16), self.result(at, 16), e_l.at[self.layer, self.k, 0]
            )

        def keep_b(self, b):
            at = quarter_at[b] + 32 * yh
            return pltpu.make_async_copy(
                self.rows(at, 32), self.result(at, 32), e_l.at[self.layer, self.k, 1 + b]
            )

        def to_homes(self, copies, act):
            @pl.when(self.home)
            def _():
                for copy in copies(2):
                    act(copy)

            @pl.when(jnp.logical_not(self.home))
            def _():
                for d in (1, 3):
                    for copy in copies(d):
                        act(copy)

        def s0(self):
            if self.layer == 0:
                pl.semaphore_wait(free_th.at[self.k], 1)
            self.core().start()

        def s1(self):
            self.core().wait_recv()
            self.add(0, 640, [th.at[self.k]])
            if self.layer == 1:
                pl.semaphore_signal(free_th.at[self.k], inc=1, device_id=core, device_id_type=MESH)
            else:
                pl.semaphore_wait(free_r1.at[self.k], 2)
            for b in range(2):
                self.first(b).start()
            self.to_homes(lambda d: [self.a_over_y(d)], lambda copy: copy.start())

        def s2(self):
            for b in range(2):
                self.first(b).wait_recv()
                self.add(half_at[b], 128, [r1.at[self.k, b]])
            if self.layer == 1:
                for peer in (to_xa, to_xb):
                    pl.semaphore_signal(
                        free_r1.at[self.k], inc=1, device_id=peer, device_id_type=MESH
                    )
            else:
                pl.semaphore_wait(free_r2.at[self.k], 2)
            for b in range(2):
                self.second(b).start()

            @pl.when(self.home)
            def _():
                for d in (1, 2, 3):
                    self.a_over_y(d).wait_recv()
                self.add(64 * yh, 64, [ra1.at[self.k, i] for i in range(3)])
                for d in (2, 1, 3):
                    self.a_over_x(d).start()

        def s3(self):
            for b in range(2):
                self.second(b).wait_recv()
                self.add(quarter_at[b], 64, [r2.at[self.k, b]])
            if self.layer == 1:
                for peer in (to_xa, to_xb):
                    pl.semaphore_signal(
                        free_r2.at[self.k], inc=1, device_id=peer, device_id_type=MESH
                    )
            self.to_homes(
                lambda d: [self.b_over_y(d, b) for b in range(2)], lambda copy: copy.start()
            )

            @pl.when(self.home)
            def _():
                for d in (1, 2, 3):
                    self.a_over_x(d).wait_recv()
                self.add(64 * yh + 16 * x, 16, [ra2.at[self.k, i] for i in range(3)])
                self.keep_a().start()
                for d in (2, 1, 3):
                    self.a_back_x(d).start()

        def s4(self):
            @pl.when(self.home)
            def _():
                for b in range(2):
                    for d in (1, 2, 3):
                        self.b_over_y(d, b).wait_recv()
                    self.add(
                        quarter_at[b] + 32 * yh, 32, [rb3.at[self.k, i, b] for i in range(3)]
                    )
                    self.keep_b(b).start()
                    self.b_back_y(b).start()
                self.keep_a().wait()
                for d in (1, 2, 3):
                    self.a_back_x(d).wait_recv()
                self.a_back_y().start()

        def s5(self):
            @pl.when(self.home)
            def _():
                for b in range(2):
                    self.keep_b(b).wait()
                    self.b_back_y(b).wait_recv()
                    self.back_second(b).start()

        def s6(self):
            @pl.when(self.home)
            def _():
                for b in range(2):
                    self.back_second(b).wait_recv()
                    self.back_first(b).start()

        def s7(self):
            @pl.when(self.home)
            def _():
                self.a_back_y().wait_recv()
                for b in range(2):
                    self.back_first(b).wait_recv()
                self.back_core().start()

        def drain(self):
            self.core().wait_send()
            for b in range(2):
                self.first(b).wait_send()
                self.second(b).wait_send()
            self.to_homes(lambda d: [self.a_over_y(d)], lambda copy: copy.wait_send())
            self.to_homes(
                lambda d: [self.b_over_y(d, b) for b in range(2)], lambda copy: copy.wait_send()
            )

            @pl.when(self.home)
            def _():
                for d in (1, 2, 3):
                    self.a_over_x(d).wait_send()
                    self.a_back_x(d).wait_send()
                self.a_back_y().wait_send()
                for b in range(2):
                    self.b_back_y(b).wait_send()
                    self.back_second(b).wait_send()
                    self.back_first(b).wait_send()
                self.back_core().wait()

    groups = {(layer, k): Group(layer, k) for layer in range(2) for k in range(3)}
    att1, up1, down1 = (groups[1, k] for k in range(3))
    att0, up0, down0 = (groups[0, k] for k in range(3))

    def put(layer, at, value):
        if layer == 1:
            gv[at, :] = value.astype(bf16)
        else:
            wb[1, at, :] = value.astype(bf16)

    def grad_tiles(layer, k, left, right):
        for i in range(D // TILE):
            put(layer, pl.ds(k * 1280 + i * TILE, TILE), tm(left[:, cols_of(i)], right[...]))
        groups[layer, k].s0()

    def t_move(i, src, dst, peer):
        return remote(src, dst, t_s.at[i], t_r.at[i], peer)

    def t_rows(sec, at, n):
        return gt.at[sec, pl.ds(pl.multiple_of(at, 16), n)]

    def t_result(at, n):
        return to_ref.at[pl.ds(pl.multiple_of(at, 16), n)]

    def t_core(sec):
        return t_move(sec, t_rows(sec, 128 * (1 - c), 128), tt.at[sec], core)

    def t_over_x(d, sec):
        src = t_rows(sec, 128 * c + 32 * x_at[d], 32)
        return t_move(2 * d + sec, src, tx.at[d - 1, sec], x_peer[d])

    def t_over_y(d):
        src = t_rows(lax.rem(y_at[d], 2), 128 * c + 32 * x + 16 * lax.div(y_at[d], 2), 16)
        return t_move(7 + d, src, ty.at[d - 1], y_peer[d])

    t_own = 128 * c + 32 * x + 16 * yh

    def t_back_y():
        return t_move(11, t_rows(s, t_own, 16), t_result(t_own, 16), y_peer[2])

    def t_keep():
        return pltpu.make_async_copy(t_rows(s, t_own, 16), t_result(t_own, 16), t_l)

    def t_back_x(d):
        ref = t_result(128 * c + 32 * x, 32)
        return t_move(11 + d, ref, ref, x_peer[d])

    def t_back_core():
        ref = t_result(128 * c, 128)
        return t_move(15, ref, ref, core)

    def t_add(sec, at, n, sources):
        here = pl.ds(pl.multiple_of(at, 16), n)
        total = gt[sec, here, :].astype(f32)
        for source in sources:
            total = total + source[...].astype(f32)
        gt[sec, here, :] = total.astype(bf16)

    def t1():
        for sec in range(2):
            t_core(sec).wait_recv()
            for i in range(4):
                t_add(sec, 128 * c + 32 * i, 32, [tt.at[sec, pl.ds(32 * i, 32)]])
            for d in (2, 1, 3):
                t_over_x(d, sec).start()

    def t2():
        for sec in range(2):
            for d in (1, 2, 3):
                t_over_x(d, sec).wait_recv()
            t_add(sec, 128 * c + 32 * x, 32, [tx.at[i, sec] for i in range(3)])
        for d in (2, 1, 3):
            t_over_y(d).start()

    def t3():
        for d in (1, 2, 3):
            t_over_y(d).wait_recv()
        t_add(s, t_own, 16, [ty.at[i] for i in range(3)])
        t_keep().start()
        t_back_y().start()

    def t4():
        t_keep().wait()
        t_back_y().wait_recv()
        for d in (2, 1, 3):
            t_back_x(d).start()

    def t5():
        for d in (1, 2, 3):
            t_back_x(d).wait_recv()
        t_back_core().start()

    cot_copy.wait()
    gg[...] = jnp.zeros_like(gg)

    for layer in (1, 0):
        st = 5 if layer == 1 else 7
        for h in range(HALVES):
            at = rows_of(h)
            if layer == 0:
                ag_wait(5, h, gb.at[1])

            def d_up_tile(j, carry):
                cols = cols_of(j)
                rows = pl.ds(2560 + j * TILE, TILE)
                d_hidden = mm_t(gb[1 - layer, at, :], wb[layer, rows, :])
                up = upb[layer, at, cols]
                t = jnp.tanh(GELU_A * (up + GELU_B * up * up * up))
                slope = 0.5 * (1.0 + t) + 0.5 * up * (1.0 - t * t) * (
                    GELU_A * (1.0 + 3.0 * GELU_B * up * up)
                )
                du[at, cols] = (d_hidden * slope).astype(bf16)
                if layer == 0:
                    hb[at, cols] = (0.5 * up * (1.0 + t)).astype(bf16)

            unrolled(D // TILE, d_up_tile)
            if layer == 1:
                mlp_out(1, h)
            if layer == 0 and h == 1:
                att1.s1()
                up1.s2()
            rs_send(
                st, h,
                lambda j, cols: mm_t(
                    du[at, :], wb[layer, pl.ds(1280 + j * TILE, TILE), :]
                ),
            )
        if layer == 0:
            for i in range(N_PIECES):
                for k in range(2):
                    w_over_x(i, k, odd).wait_send()
                    w_to_core(i, k).wait_send()
        grad_tiles(layer, 2, hb, gb.at[1 - layer])
        if layer == 0:
            down1.s3()
            att1.s2()
        for h in range(HALVES):
            dn = rs_take(st, h)
            dx, gain = norm_back(dn, mid[layer, own(h), :], gn[layer, 1:2, :])
            dm = gb[1 - layer, chunk(h, z), :].astype(f32) + dx
            dmid[own(h), :] = dm
            gg[2 * layer + 1 : 2 * layer + 2, :] += gain
            if layer == 0:
                for d in (1, 2, 3):
                    ag_copy(4, h, d, mb).wait_send()
            ag_send(st - 1, h, mb, dm)
        if layer == 0:
            up1.s3()
        grad_tiles(layer, 1, nm.at[layer], du)
        if layer == 1:
            down1.s1()
        else:
            down0.s1()
            down1.s4()
        for h in range(HALVES):
            ag_wait(st - 1, h, mb)
            attention_back(layer, h)
            if h == 1 and layer == 1:
                up1.s1()
            if h == 1 and layer == 0:
                up0.s1()
                up1.s4()
                att1.s3()
            at = rows_of(h)
            rs_send(
                st + 1, h,
                lambda j, cols: mm(dqb[0, at, :], wb[layer, 0:ATT, cols])
                + mm(dqb[1, at, :], wb[layer, ATT : 2 * ATT, cols])
                + mm(dqb[2, at, :], wb[layer, 2 * ATT : 3 * ATT, cols]),
            )
        for i in range(3):
            put(layer, pl.ds(i * ATT, ATT), tm(dqb[i], nb[layer]))
        put(layer, pl.ds(960, 320), tm(ct[layer], mb[...]))
        groups[layer, 0].s0()
        if layer == 1:
            down1.s2()
        else:
            down0.s2()
            down1.s5()
        for h in range(HALVES):
            dn = rs_take(st + 1, h)
            dx, gain = norm_back(dn, sx[layer, own(h), :], gn[layer, 0:1, :])
            gg[2 * layer : 2 * layer + 1, :] += gain
            ag_send(st, h, gb.at[layer], dmid[own(h), :] + dx)

    att0.s1()
    up1.s5()
    att1.s4()

    def gg_copy(d):
        return remote(gg, ggr.at[d - 1], gg_s.at[d - 1], gg_r.at[d - 1], z_peer[d])

    for d in (1, 2, 3):
        gg_copy(d).start()

    for h in range(HALVES):
        ag_wait(7, h, gb.at[0])
        at = rows_of(h)
        low = gb[0, at, :]
        before = pre[at, :]
        sig = jax.nn.sigmoid(before)
        d_pre = (
            mm_t(low, w_hid_ref[...]) * (sig * (1.0 + before * (1.0 - sig)))
        ).astype(bf16)
        dctx[at, :] = d_pre
        if h == 0:
            for layer in (1, 0):
                for k in range(HALVES):
                    send_out(layer, k)
            up0.s2()
            down1.s6()
        points = mm_t(d_pre, w_in_ref[...])
        points = points + jnp.where(z == 0, mm_t(low, w_res_ref[...]), 0.0)
        gpad[at, :] = points
    points = gpad[...]
    high = points.astype(bf16)
    low = (points - high.astype(f32)).astype(bf16)
    row = lax.broadcasted_iota(jnp.int32, (ROWS, ROWS), 0)
    col = lax.broadcasted_iota(jnp.int32, (ROWS, ROWS), 1)
    swap = jnp.where(
        ((row >> 4) == (col & 15)) & ((row & 15) == (col >> 4)), 1.0, 0.0
    ).astype(bf16)
    points = mm(swap, high) + mm(swap, low)
    for k in range(8):
        dps[k, :, 0:64] = points[k * 32 : (k + 1) * 32]
        dps[k, :, 64:128] = jnp.zeros((32, 64), f32)
    me = s * 4 + z

    def dp_copy(d):
        to = lax.rem(me + d, 8)
        return remote(
            dps.at[to], dpr.at[me], dp_s.at[d - 1], dp_r.at[d - 1],
            (lax.div(to, 4), dp, lax.rem(to, 4)),
        )

    for d in range(1, 8):
        dp_copy(d).start()
    dpr[me] = dps[me]

    grad_low = gb[0]
    hid = tm(tokh[...], grad_low).astype(bf16)
    res = tm(patch_ref[...], grad_low).astype(bf16)
    inn = tm(patch_ref[...], dctx[...]).astype(bf16)
    for sec in range(2):
        lanes = slice(sec * 640, sec * 640 + 640)
        gt[sec, 0:160, 0:640] = hid[0:160, lanes]
        gt[sec, 0:160, 640:1280] = hid[160:320, lanes]
        gt[sec, 160:192, 0:640] = res[0:32, lanes]
        gt[sec, 160:192, 640:1280] = res[32:64, lanes]
        gt[sec, 192:224, :] = jnp.zeros((32, D), bf16)
        gt[sec, 192:224, 0:320] = inn[sec * 32 : sec * 32 + 32]
    total = gg[...]
    for d in (1, 2, 3):
        gg_copy(d).wait_recv()
        total = total + ggr[d - 1]
    for sec in range(2):
        gt[sec, 224:256, :] = jnp.concatenate(
            [total[2 * sec : 2 * sec + 2], jnp.zeros((30, D), f32)], axis=0
        ).astype(bf16)

    for sec in range(2):
        t_core(sec).start()
    down0.s3()
    att0.s2()
    up1.s6()
    att1.s5()
    t1()
    up0.s3()
    down1.s7()
    down0.s4()
    t2()
    att0.s3()
    up1.s7()
    att1.s6()
    up0.s4()
    down0.s5()
    t3()
    att0.s4()
    up0.s5()
    down0.s6()
    t4()
    att1.s7()
    att0.s5()
    up0.s6()
    down0.s7()
    t5()
    att0.s6()
    up0.s7()
    att0.s7()
    for d in range(1, 8):
        dp_copy(d).wait_recv()
    for sec in range(2):
        points_ref[sec] = dpr[4 * sec] + dpr[4 * sec + 1] + dpr[4 * sec + 2] + dpr[4 * sec + 3]

    for i in range(N_PIECES):
        for k in range(2):
            w_over_y(i, k).wait_send()
    for group in groups.values():
        group.drain()
    for sec in range(2):
        t_core(sec).wait_send()
    for d in (1, 2, 3):
        for sec in range(2):
            t_over_x(d, sec).wait_send()
        t_over_y(d).wait_send()
        t_back_x(d).wait_send()
    t_back_y().wait_send()
    t_back_core().wait()
    gn_send.wait_send()
    for h in range(HALVES):
        for d in (1, 2, 3):
            rs_copy(7, h, d).wait_send()
            rs_copy(8, h, d).wait_send()
            gathered = [nb.at[0], nm.at[0], nb.at[1], nm.at[1], None, gb.at[1], mb, gb.at[0]]
            for i, ref in enumerate(gathered):
                if ref is not None:
                    ag_copy(i, h, d, ref).wait_send()
        for layer in range(2):
            src = ob.at[layer, own(h)]
            dst = lo_ref.at[pl.ds(pl.multiple_of(s * ROWS + h * RH + z * RQ, RQ), RQ)]

            @pl.when(s == layer)
            def _():
                pltpu.make_async_copy(src, dst, lo_l.at[h]).wait()

            @pl.when(s != layer)
            def _():
                remote(src, dst, lo_s.at[layer, 0, h], lo_r.at[s, 0, h], (layer, dp, z)).wait_send()

            for d in (1, 2, 3):
                remote(
                    src, dst, lo_s.at[layer, d, h], lo_r.at[s, d, h], (layer, dp, z_at[d])
                ).wait_send()
        for d in range(4):
            remote(
                ob.at[0, own(h)], lo_ref.at[pl.ds(0, RQ)], lo_s.at[0, d, h],
                lo_r.at[other, d, h], across[d],
            ).wait_recv()
        for d in (1, 2, 3):
            remote(
                ob.at[0, own(h)], lo_ref.at[pl.ds(0, RQ)], lo_s.at[0, d, h],
                lo_r.at[s, d, h], z_peer[d],
            ).wait_recv()
    for d in (1, 2, 3):
        gg_copy(d).wait_send()
    for d in range(1, 8):
        dp_copy(d).wait_send()


def run_layers(patch_in, w_in, w_hid, w_res, gains, wq, wo, wu, wd, cotangent):
    cos, sin, turn = rotary_arrays()
    vm = pl.BlockSpec(memory_space=pltpu.VMEM)
    hbm = pl.BlockSpec(memory_space=pl.ANY)
    dma = pltpu.SemaphoreType.DMA
    scratch = [
        pltpu.VMEM((2, LAYER_ROWS, D), bf16),
        pltpu.VMEM((2, 8, D), f32),
        pltpu.VMEM((ROWS, ATT), bf16),
        pltpu.VMEM((ROWS, ATT), f32),
        pltpu.VMEM((2, ROWS // 4, D), f32),
        pltpu.VMEM((2, ROWS // 4, D), f32),
        pltpu.VMEM((2, ROWS, D), bf16),
        pltpu.VMEM((2, ROWS, D), bf16),
        pltpu.VMEM((2, 3, ROWS, ATT), bf16),
        pltpu.VMEM((2, ROWS // BLOCK, HEADS_HERE * BLOCK, BLOCK), f32),
        pltpu.VMEM((2, ROWS, ATT), bf16),
        pltpu.VMEM((2, ROWS, D), f32),
        pltpu.VMEM((ROWS, D), bf16),
        pltpu.VMEM((2, ROWS, D), bf16),
        pltpu.VMEM((ROWS, D), bf16),
        pltpu.VMEM((ROWS, D), bf16),
        pltpu.VMEM((3, ROWS, ATT), bf16),
        pltpu.VMEM((ROWS, ATT), bf16),
        pltpu.VMEM((LAYER_ROWS, D), bf16),
        pltpu.VMEM((2, PACK_ROWS - LAYER_ROWS, D), bf16),
        pltpu.VMEM((2, ROWS, D), bf16),
        pltpu.VMEM((2, 3, ROWS // 4, D), bf16),
        pltpu.VMEM((ROWS // 4, D), f32),
        pltpu.VMEM((2, ROWS // 4, D), bf16),
        pltpu.VMEM((8, D), f32),
        pltpu.VMEM((3, 8, D), f32),
        pltpu.VMEM((8, 32, 128), f32),
        pltpu.VMEM((8, 32, 128), f32),
        pltpu.VMEM((ROWS, 64), f32),
        pltpu.VMEM((3, 640, D), bf16),
        pltpu.VMEM((3, 2, 128, D), bf16),
        pltpu.VMEM((3, 2, 64, D), bf16),
        pltpu.VMEM((3, 3, 64, D), bf16),
        pltpu.VMEM((3, 3, 16, D), bf16),
        pltpu.VMEM((3, 3, 2, 32, D), bf16),
        pltpu.VMEM((2, 128, D), bf16),
        pltpu.VMEM((3, 2, 32, D), bf16),
        pltpu.VMEM((3, 16, D), bf16),
        dma((4,)), *[dma((N_PIECES, 2))] * 6,
        dma, dma, dma, dma,
        dma((9, HALVES, 3)), dma((9, HALVES, 3)),
        dma((8, HALVES, 3)), dma((8, HALVES, 3)),
        dma((HALVES,)), dma((2, 4, HALVES)), dma((2, 4, HALVES)),
        dma((3,)), dma((3,)), dma((7,)), dma((7,)),
        dma((2, 3, 28)), dma((2, 3, 28)), dma((2, 3, 3)),
        dma((16,)), dma((16,)), dma,
        *[pltpu.SemaphoreType.REGULAR((3,))] * 3,
    ]
    return pl.pallas_call(
        layers_kernel,
        out_shape=(
            jax.ShapeDtypeStruct((2 * ROWS, D), bf16),
            jax.ShapeDtypeStruct((LAYER_ROWS, D), bf16),
            jax.ShapeDtypeStruct((PACK_ROWS - LAYER_ROWS, D), bf16),
            jax.ShapeDtypeStruct((2, 32, 128), f32),
        ),
        in_specs=[vm] * 5 + [hbm] * 5 + [vm] * 3,
        out_specs=(hbm, hbm, hbm, vm),
        scratch_shapes=scratch,
        compiler_params=pltpu.CompilerParams(
            collective_id=0, has_side_effects=True, vmem_limit_bytes=62 * 2**20
        ),
        cost_estimate=pl.CostEstimate(
            flops=15_000_000_000, bytes_accessed=50_000_000, transcendentals=4_000_000
        ),
        name="layers",
    )(
        patch_in, w_in, w_hid, w_res, gains, wq, wo, wu, wd, cotangent,
        jnp.asarray(cos, f32), jnp.asarray(sin, f32), jnp.asarray(turn, bf16),
    )


STEP = 320


def widen_kernel(big_ref, small_ref, qkv, out, up, down, hid, res, inn, gain_a, gain_m):
    i = pl.program_id(0)
    for first, last, ref in ((0, 3, qkv), (3, 4, out), (4, 8, up), (8, 12, down)):

        @pl.when((i >= first) & (i < last))
        def _(ref=ref):
            ref[...] = big_ref[...].astype(f32)

    @pl.when(i == 0)
    def _():
        small = small_ref[...].astype(f32)
        hid[0:160, :] = small[0:160, 0:640]
        hid[160:320, :] = small[0:160, 640:1280]
        res[0:32, :] = small[160:192, 0:640]
        res[32:64, :] = small[160:192, 640:1280]
        inn[...] = small[192:224, 0:320]
        gain_a[...] = small[224:225]
        gain_m[...] = small[225:226]


def widen(big, small):
    def tall(first, count):
        return pl.BlockSpec((STEP, D), lambda i: (jnp.clip(i - first, 0, count - 1), 0))

    def whole(rows, columns):
        return pl.BlockSpec((rows, columns), lambda i: (0, 0))

    shapes = ((960, D), (320, D), (1280, D), (1280, D), (320, 640), (64, 640), (32, 320), (1, D), (1, D))
    return pl.pallas_call(
        widen_kernel,
        grid=(LAYER_ROWS // STEP,),
        out_shape=[jax.ShapeDtypeStruct(shape, f32) for shape in shapes],
        in_specs=[
            pl.BlockSpec((STEP, D), lambda i: (i, 0)),
            pl.BlockSpec((256, D), lambda i: (0, 0)),
        ],
        out_specs=[tall(0, 3), tall(3, 1), tall(4, 4), tall(8, 4)]
        + [whole(*shape) for shape in shapes[4:]],
        compiler_params=pltpu.CompilerParams(vmem_limit_bytes=40 * 2**20),
        cost_estimate=pl.CostEstimate(flops=0, bytes_accessed=32_000_000, transcendentals=0),
        name="widen",
    )(big, small)


def per_device(
    series, missing, w_in, w_hid, w_res, gain_attn, w_qkv, w_out, gain_mlp, w_up, w_down, cotangent
):
    s = lax.axis_index("section")
    contexts = series.shape[0] // 2
    keep = (1 - missing).astype(f32)
    values = lax.dynamic_slice_in_dim(series * keep, s * contexts, contexts, 0)
    flags = lax.dynamic_slice_in_dim(missing, s * contexts, contexts, 0).astype(f32)
    patch_in = jnp.concatenate(
        [values.reshape(ROWS, PATCH), flags.reshape(ROWS, PATCH)], axis=1
    ).astype(bf16)
    gains = jnp.concatenate([gain_attn, gain_mlp, jnp.zeros((6, D), f32)], axis=0)
    wq = jnp.transpose(w_qkv[0], (1, 2, 0)).reshape(3 * ATT, D)
    layer_out, big, small, points = run_layers(
        patch_in, w_in, w_hid, w_res, gains, wq, w_out[0], w_up[0], w_down[0], cotangent
    )
    g_qkv, g_out, g_up, g_down, g_hid, g_res, g_in, gain_a, gain_m = widen(big, small)
    points = points[:, :, :PATCH].reshape(2, 2, contexts, PATCH)
    points = jnp.transpose(points, (0, 2, 1, 3)).reshape(2 * contexts, 2 * PATCH)
    block = s * 4 + lax.axis_index("tensor")
    keep_here = lax.dynamic_slice_in_dim(keep, block * 2 * PATCH, 2 * PATCH, 1)
    series_grad = points * keep_here
    g_qkv = jnp.transpose(g_qkv.reshape(3, ATT, D), (2, 0, 1))
    return (
        layer_out[None],
        series_grad,
        g_in,
        g_hid,
        g_res,
        gain_a,
        g_qkv[None],
        g_out[None],
        gain_m,
        g_up[None],
        g_down[None],
    )


def solution(mesh):
    in_specs = (
        P("dp", None),
        P("dp", None),
        P(None, "tensor"),
        P("tensor", None),
        P(),
        P("section", None),
        P("section", None, None, "tensor"),
        P("section", "tensor", None),
        P("section", None),
        P("section", None, "tensor"),
        P("section", "tensor", None),
        P("dp", None),
    )
    out_specs = (
        P("section", "dp", None),
        P("dp", ("section", "tensor")),
        P("section", "tensor"),
        P("tensor", "section"),
        P(None, "section"),
        P("section", None),
        P("section", None, None, "tensor"),
        P("section", "tensor", None),
        P("section", None),
        P("section", None, "tensor"),
        P("section", "tensor", None),
    )
    return jax.shard_map(
        per_device, mesh=mesh, in_specs=in_specs, out_specs=out_specs, check_vma=False
    )
```

```python
import math

import jax
import jax.numpy as jnp
import numpy as np
from jax import lax
from jax.experimental import pallas as pl
from jax.experimental.pallas import tpu as pltpu
from jax.sharding import PartitionSpec as P

D = 1280
HEADS_HERE = 4
HEAD_DIM = 80
ATT = HEADS_HERE * HEAD_DIM
PATCH = 32
PATCHES = 16
ROWS = 256
HALVES = 2
RH = ROWS // HALVES
RQ = RH // 4
TILE = 256
BLOCK = 128
MATS = ((0, 960), (960, 320), (1280, 1280), (2560, 1280))
PIECES = (
    (0, 512, 0), (512, 448, 0), (960, 320, 1), (1280, 640, 2), (1920, 640, 2), (2560, 640, 3), (3200, 640, 3),
)
N_PIECES = len(PIECES)
LAYER_ROWS = 3840
PACK_ROWS = 4096
RS_BEFORE = {2: 0, 3: 1, 5: 3, 6: 2, 7: 5, 8: 6, 4: 8}
MESH = pl.DeviceIdType.MESH
f32 = jnp.float32
bf16 = jnp.bfloat16
eps_norm = 1e-06
masked_score = -1e30
GELU_A = math.sqrt(2.0 / math.pi)
GELU_B = 0.044715


def mm(a, b):
    return lax.dot_general(a, b, (((1,), (0,)), ((), ())), preferred_element_type=f32)


def mm_t(a, b):
    return lax.dot_general(a, b, (((1,), (1,)), ((), ())), preferred_element_type=f32)


def tm(a, b):
    return lax.dot_general(a, b, (((0,), (0,)), ((), ())), preferred_element_type=f32)


def unrolled(count, body):
    for j in range(count):
        body(j, 0)


def rotary_arrays():
    half = HEAD_DIM // 2
    position = (np.arange(BLOCK) % PATCHES).astype(np.float32)
    frequency = np.exp(
        np.arange(half, dtype=np.float32) * np.float32(-2.0 * math.log(10000.0) / HEAD_DIM)
    )
    angles = position[:, None] * frequency[None, :]
    lane = np.arange(ATT) % half
    turn = np.zeros((ATT, ATT), np.float32)
    for j in range(ATT):
        if j % HEAD_DIM < half:
            turn[j + half, j] = -1.0
        else:
            turn[j - half, j] = 1.0
    return np.cos(angles)[:, lane], np.sin(angles)[:, lane], turn


def places():
    s = lax.axis_index("section")
    dp = lax.axis_index("dp")
    z = lax.axis_index("tensor")
    c = lax.rem(dp, 2)
    yh = lax.rem(lax.div(dp, 2), 2)
    x = lax.div(dp, 4)
    return s, dp, z, x, yh, c


def layers_kernel(
    patch_ref, w_in_ref, w_hid_ref, w_res_ref, gain_a_ref, gain_m_ref, wq_ref, wo_ref, wu_ref, wd_ref,
    cot_ref, cos_ref, sin_ref, turn_ref,
    lo_ref, go_ref, to_ref, points_ref,
    wb, gn, tokh, pre, sx, mid, nb, nm, qb, pb, ct, upb, hb, gb, mb, du, dqb, dctx, gv, gt,
    sb, rb, dmid, ob, gg, ggr, dps, dpr, gpad,
    th, r1, r2, ra1, ra2, ra3, rb3, tt, tx, ty, pd,
    w_loc, w_s, w_r, x_s, x_r, f_s, f_r, gn_s, gn_r, cot_l,
    rs_s, rs_r, ag_s, ag_r, lo_l, lo_s, lo_r, gg_s, gg_r, dp_s, dp_r,
    e_s, e_r, e_l, t_s, t_r, t_l, free_th, free_r1, free_r2,
):
    s, dp, z, x, yh, c = places()
    other = 1 - s
    z_peer = [None] + [(s, dp, lax.rem(z + d, 4)) for d in (1, 2, 3)]
    z_at = [z] + [lax.rem(z + d, 4) for d in (1, 2, 3)]
    y_a = (other, dp, z)
    y_b = (other, dp + 2 - 4 * yh, z)
    core = (s, dp + 1 - 2 * c, z)
    across = [(other, dp, z_at[d]) for d in range(4)]
    y = 2 * yh + s
    x_at = [x] + [lax.rem(x + d, 4) for d in (1, 2, 3)]
    y_at = [y] + [lax.rem(y + d, 4) for d in (1, 2, 3)]
    x_peer = [None] + [(s, x_at[d] * 4 + 2 * yh + c, z) for d in (1, 2, 3)]
    y_peer = [None] + [
        (lax.rem(y_at[d], 2), x * 4 + 2 * lax.div(y_at[d], 2) + c, z) for d in (1, 2, 3)
    ]
    x_up, x_down = x_peer[1], x_peer[3]
    w_refs = (wq_ref, wo_ref, wu_ref, wd_ref)

    barrier = pltpu.get_barrier_semaphore()
    peers = z_peer[1:] + across + [y_b, core] + x_peer[1:] + [y_peer[2]]
    for peer in peers:
        pl.semaphore_signal(barrier, inc=1, device_id=peer, device_id_type=MESH)
    pl.semaphore_wait(barrier, len(peers))

    def remote(src, dst, ssem, rsem, peer):
        return pltpu.make_async_remote_copy(
            src_ref=src, dst_ref=dst, send_sem=ssem, recv_sem=rsem,
            device_id=peer, device_id_type=MESH,
        )

    odd = lax.rem(x, 2)

    def w_local(m):
        off, n = MATS[m]
        return pltpu.make_async_copy(w_refs[m], wb.at[s, pl.ds(off, n)], w_loc)

    def share(i, parity, k):
        off, n, m = PIECES[i]
        first = (n // 4 + 31) // 32 * 16
        size = first if k == 0 else n // 4 - first
        return (2 * c + parity) * (n // 4) + k * first, size

    def w_over_y(i, k):
        off, n, m = PIECES[i]
        at, size = share(i, odd, k)
        src = w_refs[m].at[pl.ds(pl.multiple_of(off - MATS[m][0] + at, 16), size)]
        dst = wb.at[s, pl.ds(pl.multiple_of(off + at, 16), size)]
        return remote(src, dst, w_s.at[i], w_r.at[i], (y_a, y_b)[k])

    def w_over_x(i, k, parity):
        at, size = share(i, parity, k)
        ref = wb.at[other, pl.ds(pl.multiple_of(PIECES[i][0] + at, 16), size)]
        return remote(ref, ref, x_s.at[i], x_r.at[i], (x_up, x_down)[k])

    def w_to_core(i, q):
        off, n, m = PIECES[i]
        parity = odd if q == 0 else 1 - odd
        ref = wb.at[other, pl.ds(pl.multiple_of(off + (2 * c + parity) * (n // 4), 16), n // 4)]
        return remote(ref, ref, f_s.at[i], f_r.at[i], core)

    def w_total(i, part, ssem, rsem):
        ref = wb.at[0, pl.ds(0, PIECES[i][1] // part)]
        return remote(ref, ref, ssem.at[i], rsem.at[i], core)

    def weights(layer, steps):
        @pl.when(s != layer)
        def _():
            for step, i in steps:
                if step == "y":
                    w_total(i, 4, w_s, w_r).wait_recv()
                    for k in range(2):
                        w_over_x(i, k, odd).start()
                    w_to_core(i, 0).start()
                elif step == "x":
                    w_total(i, 4, x_s, x_r).wait_recv()
                    w_to_core(i, 1).start()
                else:
                    w_total(i, 2, f_s, f_r).wait_recv()

    gains = gn.at[s]
    gains[0:1, :] = gain_a_ref[...]
    gains[1:2, :] = gain_m_ref[...]
    gn_send = remote(gn.at[s], gn.at[s], gn_s, gn_r, y_a)
    cot_copy = pltpu.make_async_copy(
        cot_ref.at[pl.ds(pl.multiple_of(s * ROWS, ROWS), ROWS)], gb.at[0], cot_l
    )
    gn_send.start()
    def start_weights(first, last):
        for i in range(first, last):
            for k in range(2):
                w_over_y(i, k).start()

    start_weights(0, 3)
    for m in range(4):
        w_local(m).start()
    cot_copy.start()

    def rows_of(h):
        return pl.ds(h * RH, RH)

    def chunk(h, zz):
        return pl.ds(pl.multiple_of(h * RH + zz * RQ, RQ), RQ)

    def cols_of(j):
        return pl.ds(j * TILE, TILE)

    def rs_copy(st, h, d, cols=None):
        src = sb.at[st % 2, chunk(h, z_at[d])]
        dst = rb.at[st % 2, d - 1, pl.ds(h * RQ, RQ)]
        if cols is not None:
            src = sb.at[st % 2, chunk(h, z_at[d]), cols]
            dst = rb.at[st % 2, d - 1, pl.ds(h * RQ, RQ), cols]
        return remote(src, dst, rs_s.at[st, h], rs_r.at[st, h], z_peer[d])

    def rs_total(st, h):
        ref = rb.at[st % 2, pl.ds(0, 3), pl.ds(h * RQ, RQ)]
        return remote(ref, ref, rs_s.at[st, h], rs_r.at[st, h], core)

    def rs_send(st, h, produce):
        if st in RS_BEFORE:
            rs_total(RS_BEFORE[st], h).wait_send()

        if produce is None:
            sb[st % 2, rows_of(h), :] = pd[rows_of(h), :]
            for d in (2, 1, 3):
                rs_copy(st, h, d).start()
            return

        def body(j, carry):
            cols = cols_of(j)
            sb[st % 2, rows_of(h), cols] = produce(j, cols).astype(bf16)
            if j in (2, 4):
                part = pl.ds(0, 768) if j == 2 else pl.ds(768, 512)
                for d in (2, 1, 3):
                    rs_copy(st, h, d, part).start()

        unrolled(D // TILE, body)

    def rs_take(st, h):
        total = sb[st % 2, chunk(h, z), :].astype(f32)
        rs_total(st, h).wait_recv()
        for d in (1, 2, 3):
            total = total + rb[st % 2, d - 1, pl.ds(h * RQ, RQ), :].astype(f32)
        return total

    def ag_copy(st, h, d, dst):
        at = dst.at[chunk(h, z)]
        return remote(at, at, ag_s.at[st, h], ag_r.at[st, h], z_peer[d])

    def ag_send(st, h, dst, value):
        dst[chunk(h, z), :] = value.astype(bf16)
        for d in (2, 1, 3):
            ag_copy(st, h, d, dst).start()

    def ag_total(st, h):
        ref = pd.at[pl.ds(0, 3 * RQ)]
        return remote(ref, ref, ag_s.at[st, h], ag_r.at[st, h], core)

    def ag_wait(st, h, dst):
        ag_total(st, h).wait_recv()

    def own(h):
        return pl.ds(h * RQ, RQ)

    def scale_of(v):
        return lax.rsqrt(jnp.mean(v * v, axis=-1, keepdims=True) + eps_norm)

    def norm(v, g):
        return v * scale_of(v) * g

    def norm_back(dn, v, g):
        r = scale_of(v)
        weighted = g * dn
        inner = jnp.mean(v * weighted, axis=-1, keepdims=True)
        return r * weighted - v * (r * r * r * inner), jnp.sum(dn * v * r, axis=0, keepdims=True)

    head_lane = lax.broadcasted_iota(jnp.int32, (1, ATT), 1)
    head_mask = [
        (head_lane >= HEAD_DIM * h) & (head_lane < HEAD_DIM * (h + 1)) for h in range(HEADS_HERE)
    ]

    def spread(v):
        wide = v.astype(f32)
        return jnp.concatenate(
            [jnp.where(m, wide, 0.0) for m in head_mask], axis=0
        ).astype(bf16)

    def gather(v):
        total = jnp.where(head_mask[0], v[:BLOCK], 0.0)
        for h in range(1, HEADS_HERE):
            total = total + jnp.where(head_mask[h], v[h * BLOCK : (h + 1) * BLOCK], 0.0)
        return total

    def turned(v, sign):
        high = v.astype(bf16)
        low = (v - high.astype(f32)).astype(bf16)
        swapped = mm(high, turn_ref[...]) + mm(low, turn_ref[...])
        if sign < 0:
            swapped = -swapped
        return v * cos_ref[...] + swapped * sin_ref[...]

    inv = 1.0 / math.sqrt(HEAD_DIM)

    def blocks_of(h):
        return range(h * RH // BLOCK, (h + 1) * RH // BLOCK)

    def attention_front(layer, h):
        for b in blocks_of(h):
            at = pl.ds(b * BLOCK, BLOCK)
            normed = nb[layer, at, :]
            q = turned(mm_t(normed, wb[layer, 0:ATT, :]), 1).astype(bf16)
            k = turned(mm_t(normed, wb[layer, ATT : 2 * ATT, :]), 1).astype(bf16)
            v = mm_t(normed, wb[layer, 2 * ATT : 3 * ATT, :]).astype(bf16)
            qb[layer, 0, at, :] = q
            qb[layer, 1, at, :] = k
            qb[layer, 2, at, :] = v
            scores = mm_t(spread(q), k) * inv
            row = lax.broadcasted_iota(jnp.int32, scores.shape, 0) & (BLOCK - 1)
            col = lax.broadcasted_iota(jnp.int32, scores.shape, 1)
            allowed = (col <= row) & (col >= (row & (BLOCK - PATCHES)))
            scores = jnp.where(allowed, scores, masked_score)
            e = jnp.exp(scores - jnp.max(scores, axis=-1, keepdims=True))
            probs = e / jnp.sum(e, axis=-1, keepdims=True)
            pb[layer, b] = probs
            ct[layer, at, :] = gather(mm(probs.astype(bf16), v)).astype(bf16)

    def attention_back(layer, h):
        for b in blocks_of(h):
            at = pl.ds(b * BLOCK, BLOCK)
            spread_d = spread(mm_t(mb[at, :], wb[layer, 960:1280, :]).astype(bf16))
            spread_q = spread(qb[layer, 0, at, :])
            k = qb[layer, 1, at, :]
            v = qb[layer, 2, at, :]
            probs = pb[layer, b]
            d_probs = mm_t(spread_d, v)
            d_scores = (
                probs * (d_probs - jnp.sum(probs * d_probs, axis=-1, keepdims=True))
            ).astype(bf16)
            d_q = gather(mm(d_scores, k)) * inv
            d_k = tm(d_scores, spread_q) * inv
            dqb[0, at, :] = turned(d_q, -1).astype(bf16)
            dqb[1, at, :] = turned(d_k, -1).astype(bf16)
            dqb[2, at, :] = tm(probs.astype(bf16), spread_d).astype(bf16)

    for h in range(HALVES):
        at = rows_of(h)
        before = mm(patch_ref[at, :], w_in_ref[...])
        pre[at, :] = before
        tokh[at, :] = (before * jax.nn.sigmoid(before)).astype(bf16)
        rs_send(0, h, lambda j, cols: mm(tokh[at, :], w_hid_ref[:, cols]))
    gn_send.wait_recv()
    pltpu.make_async_copy(wb.at[s], wb.at[s], w_loc).wait()
    start_weights(3, 4)
    for h in range(HALVES):
        weights(0, [("y", h)])
        start_weights(4 + h, 5 + h)
        stream = rs_take(0, h) + mm(patch_ref[chunk(h, z), :], w_res_ref[...])
        sx[0, own(h), :] = stream
        ag_send(0, h, nb.at[0], norm(stream, gn[0, 0:1, :]))
    start_weights(6, 7)
    weights(0, [("y", 2), ("x", 0), ("x", 1), ("core", 0), ("core", 1)])

    def lo_rows(sec, h):
        return lo_ref.at[pl.ds(pl.multiple_of(sec * ROWS + h * RH + z * RQ, RQ), RQ)]

    def lo_keep(h):
        return pltpu.make_async_copy(ob.at[s, own(h)], lo_rows(s, h), lo_l.at[h])

    def lo_cross(h):
        return remote(ob.at[other, own(h)], lo_rows(s, h), lo_s.at[0, h], lo_r.at[0, h], y_a)

    def lo_arrive(h):
        return remote(ob.at[other, own(h)], lo_rows(other, h), lo_s.at[0, h], lo_r.at[0, h], y_a)

    def lo_own(h, d):
        return remote(ob.at[s, own(h)], lo_rows(s, h), lo_s.at[1, h], lo_r.at[1, h], z_peer[d])

    def lo_pass(h, d):
        ref = lo_rows(other, h)
        return remote(ref, ref, lo_s.at[2, h], lo_r.at[2, h], z_peer[d])

    def lo_total(i, h):
        ref = pd.at[pl.ds(0, 3 * RQ)]
        return remote(ref, ref, lo_s.at[i, h], lo_r.at[i, h], core)

    def cross_out(layer, h):
        @pl.when(s != layer)
        def _():
            lo_cross(h).start()

    def own_out(h):
        lo_keep(h).start()
        for d in (2, 1, 3):
            lo_own(h, d).start()

    def pass_out(h):
        lo_arrive(h).wait_recv()
        for d in (2, 1, 3):
            lo_pass(h, d).start()

    def mlp_out(layer, h):
        out = (mid[layer, own(h), :] + rs_take(2 + 2 * layer, h)).astype(bf16)
        ob[layer, own(h), :] = out
        cross_out(layer, h)
        return out

    for layer in range(2):
        for h in range(HALVES):
            ag_wait(2 * layer, h, nb.at[layer])
            attention_front(layer, h)
            if h == 0 and layer == 0:
                weights(0, [("y", 3), ("x", 2), ("core", 2)])
            if h == 0 and layer == 1:
                weights(1, [("core", 2), ("x", 4), ("x", 5)])
            at = rows_of(h)
            rs_send(
                1 + 2 * layer, h, lambda j, cols: mm(ct[layer, at, :], wb[layer, 960:1280, cols])
            )
        if layer == 0:
            weights(0, [("y", 4), ("x", 3), ("y", 5)])
            weights(1, [("y", 0), ("y", 1), ("y", 2), ("y", 3)])
        for h in range(HALVES):
            if layer == 0 and h == 1:
                weights(0, [("y", 6)])
            middle = sx[layer, own(h), :] + rs_take(1 + 2 * layer, h)
            mid[layer, own(h), :] = middle
            ag_send(1 + 2 * layer, h, nm.at[layer], norm(middle, gn[layer, 1:2, :]))
        if layer == 0:
            weights(0, [("x", 4), ("core", 3), ("x", 5), ("core", 4)])
            weights(1, [("y", 4), ("y", 5)])
        else:
            weights(1, [("core", 3), ("core", 4), ("x", 6)])
        for h in range(HALVES):
            ag_wait(1 + 2 * layer, h, nm.at[layer])
            at = rows_of(h)

            def up_tile(j, carry):
                cols = cols_of(j)
                up = mm(nm[layer, at, :], wb[layer, 1280:2560, cols])
                upb[layer, at, cols] = up
                t = jnp.tanh(GELU_A * (up + GELU_B * up * up * up))
                hb[at, cols] = (0.5 * up * (1.0 + t)).astype(bf16)

            unrolled(D // TILE, up_tile)
            if layer == 1:
                continue
            if h == 0 and layer == 0:
                weights(0, [("x", 6), ("core", 5), ("core", 6)])
                weights(1, [("y", 6)])
            rs_send(
                2 + 2 * layer, h, lambda j, cols: mm(hb[at, :], wb[layer, 2560:3840, cols])
            )
        if layer == 0:
            weights(1, [("x", 0), ("x", 1), ("x", 2)])
            for h in range(HALVES):
                out = mlp_out(0, h)
                stream = out.astype(f32)
                sx[1, own(h), :] = stream
                ag_send(2, h, nb.at[1], norm(stream, gn[1, 0:1, :]))
            weights(1, [("x", 3), ("core", 0), ("core", 1)])

    xa = x + 1 - 2 * lax.rem(x, 2)
    xb = 3 - x
    to_xa = (s, xa * 4 + 2 * yh + c, z)
    to_xb = (s, xb * 4 + 2 * yh + c, z)
    j1 = lax.rem(lax.div(x + 1, 2), 2)
    j2 = lax.div(x, 2)
    i1 = lax.div(x, 2)
    i2 = lax.rem(x, 2)
    b_rows = (256, 128)
    half_at = (256 + 128 * j1, 512 + 64 * i1)
    half_off = (256 + 128 * (1 - j1), 512 + 64 * (1 - i1))
    quarter_at = (half_at[0] + 64 * j2, half_at[1] + 32 * i2)
    quarter_off = (half_at[0] + 64 * (1 - j2), half_at[1] + 32 * (1 - i2))
    a_half_at = 128 * yh + 64 * i1
    a_half_off = 128 * yh + 64 * (1 - i1)
    a_at = a_half_at + 32 * i2
    a_off = a_half_at + 32 * (1 - i2)
    first_peer = (to_xa, to_xb)
    second_peer = (to_xb, to_xa)

    class Group:
        def __init__(self, layer, k):
            self.layer, self.k = layer, k
            self.buf = gv if layer == 1 else wb.at[1]
            self.mine = k * 1280 + c * 640
            self.theirs = k * 1280 + (1 - c) * 640
            self.home = s == layer

        def rows(self, at, n):
            return self.buf.at[pl.ds(pl.multiple_of(self.mine + at, 16), n)]

        def result(self, at, n):
            return go_ref.at[pl.ds(pl.multiple_of(self.mine + at, 16), n)]

        def move(self, i, src, dst, peer):
            return remote(src, dst, e_s.at[self.layer, self.k, i], e_r.at[self.layer, self.k, i], peer)

        def add(self, at, n, sources):
            def body(i, carry):
                here = pl.ds(pl.multiple_of(self.mine + at + i * 16, 16), 16)
                there = pl.ds(pl.multiple_of(i * 16, 16), 16)
                total = self.buf[here, :].astype(f32)
                for source in sources:
                    total = total + source[there, :].astype(f32)
                self.buf[here, :] = total.astype(bf16)
                return carry

            lax.fori_loop(0, n // 16, body, 0)

        def total(self, i, n):
            ref = th.at[self.k, pl.ds(0, n)]
            return self.move(i, ref, ref, core)

        def core(self):
            src = self.buf.at[pl.ds(pl.multiple_of(self.theirs, 16), 640)]
            return self.move(0, src, th.at[self.k], core)

        def first(self, b):
            n = b_rows[b] // 2
            dst = r1.at[self.k, pl.ds(128 * b, n)]
            return self.move(1, self.rows(half_off[b], n), dst, first_peer[b])

        def second(self, b):
            n = b_rows[b] // 4
            dst = r2.at[self.k, pl.ds(64 * b, n)]
            return self.move(2, self.rows(quarter_off[b], n), dst, second_peer[b])

        def a_over_y(self, d):
            src = self.rows(128 * lax.div(y_at[d], 2), 128)
            return self.move(3, src, ra1.at[self.k, d - 1], y_peer[d])

        def a_first(self):
            return self.move(4, self.rows(a_half_off, 64), ra2.at[self.k], to_xb)

        def a_second(self):
            return self.move(5, self.rows(a_off, 32), ra3.at[self.k], to_xa)

        def b_over_y(self, d, b):
            n = b_rows[b] // 8
            src = self.rows(quarter_at[b] + n * lax.div(y_at[d], 2), n)
            return self.move(6, src, rb3.at[self.k, d - 1, pl.ds(32 * b, n)], y_peer[d])

        def a_back_second(self):
            return self.move(7, self.rows(a_at, 32), self.result(a_at, 32), to_xa)

        def a_back_first(self):
            ref = self.result(a_half_at, 64)
            return self.move(8, ref, ref, to_xb)

        def a_back_y(self):
            ref = self.result(128 * yh, 128)
            return self.move(9, ref, ref, y_peer[2])

        def b_back_y(self, b):
            n = b_rows[b] // 8
            at = quarter_at[b] + n * yh
            return self.move(10, self.rows(at, n), self.result(at, n), y_peer[2])

        def back_second(self, b):
            ref = self.result(quarter_at[b], b_rows[b] // 4)
            return self.move(11, ref, ref, second_peer[b])

        def back_first(self, b):
            ref = self.result(half_at[b], b_rows[b] // 2)
            return self.move(12, ref, ref, first_peer[b])

        def back_core(self):
            ref = self.result(0, 640)
            return self.move(13, ref, ref, core)

        def keep(self, at, n):
            return pltpu.make_async_copy(
                self.rows(at, n), self.result(at, n), e_l.at[self.layer, self.k]
            )

        def to_homes(self, copies):
            @pl.when(self.home)
            def _():
                for copy in copies(2):
                    copy.start()

            @pl.when(jnp.logical_not(self.home))
            def _():
                for d in (1, 3):
                    for copy in copies(d):
                        copy.start()

        def s0(self):
            if self.layer == 0:
                pl.semaphore_wait(free_th.at[self.k], 1)
            self.core().start()

        def s1(self):
            self.core().wait_recv()
            self.add(0, 640, [th.at[self.k]])
            if self.layer == 1:
                pl.semaphore_signal(free_th.at[self.k], inc=1, device_id=core, device_id_type=MESH)
            else:
                pl.semaphore_wait(free_r1.at[self.k], 2)
            for b in range(2):
                self.first(b).start()
            self.to_homes(lambda d: [self.a_over_y(d)])

        def s2(self):
            self.total(1, 192).wait_recv()
            for b in range(2):
                n = b_rows[b] // 2
                self.add(half_at[b], n, [r1.at[self.k, pl.ds(128 * b, n)]])
            if self.layer == 1:
                for peer in (to_xa, to_xb):
                    pl.semaphore_signal(
                        free_r1.at[self.k], inc=1, device_id=peer, device_id_type=MESH
                    )
            else:
                pl.semaphore_wait(free_r2.at[self.k], 2)
            for b in range(2):
                self.second(b).start()

            @pl.when(self.home)
            def _():
                self.total(3, 384).wait_recv()
                self.add(128 * yh, 128, [ra1.at[self.k, i] for i in range(3)])
                self.a_first().start()

        def s3(self):
            self.total(2, 96).wait_recv()
            for b in range(2):
                n = b_rows[b] // 4
                self.add(quarter_at[b], n, [r2.at[self.k, pl.ds(64 * b, n)]])
            if self.layer == 1:
                for peer in (to_xa, to_xb):
                    pl.semaphore_signal(
                        free_r2.at[self.k], inc=1, device_id=peer, device_id_type=MESH
                    )
            self.to_homes(lambda d: [self.b_over_y(d, b) for b in range(2)])

            @pl.when(self.home)
            def _():
                self.a_first().wait_recv()
                self.add(a_half_at, 64, [ra2.at[self.k]])
                self.a_second().start()

        def s4(self):
            @pl.when(self.home)
            def _():
                self.total(6, 144).wait_recv()
                for b in range(2):
                    n = b_rows[b] // 8
                    at = quarter_at[b] + n * yh
                    self.add(at, n, [rb3.at[self.k, i, pl.ds(32 * b, n)] for i in range(3)])
                    self.keep(at, n).start()
                    self.b_back_y(b).start()
                self.a_second().wait_recv()
                self.add(a_at, 32, [ra3.at[self.k]])
                self.keep(a_at, 32).start()
                self.a_back_second().start()

        def s5(self):
            @pl.when(self.home)
            def _():
                self.keep(0, 80).wait()
                self.total(10, 48).wait_recv()
                for b in range(2):
                    self.back_second(b).start()
                self.a_back_second().wait_recv()
                self.a_back_first().start()

        def s6(self):
            @pl.when(self.home)
            def _():
                self.total(11, 96).wait_recv()
                for b in range(2):
                    self.back_first(b).start()
                self.a_back_first().wait_recv()
                self.a_back_y().start()

        def s7(self):
            @pl.when(self.home)
            def _():
                self.a_back_y().wait_recv()
                self.total(12, 192).wait_recv()
                self.back_core().start()

        def drain(self):
            for i, n in ((0, 640), (1, 192), (2, 96)):
                self.total(i, n).wait_send()

            @pl.when(self.home)
            def _():
                for i, n in (
                    (3, 128), (4, 64), (5, 32), (6, 48), (7, 32), (8, 64), (9, 128), (10, 48),
                    (11, 96), (12, 192),
                ):
                    self.total(i, n).wait_send()
                self.back_core().wait()

            @pl.when(jnp.logical_not(self.home))
            def _():
                for i, n in ((3, 256), (6, 96)):
                    self.total(i, n).wait_send()

    groups = {(layer, k): Group(layer, k) for layer in range(2) for k in range(3)}
    att1, up1, down1 = (groups[1, k] for k in range(3))
    att0, up0, down0 = (groups[0, k] for k in range(3))

    def put(layer, at, value):
        if layer == 1:
            gv[at, :] = value.astype(bf16)
        else:
            wb[1, at, :] = value.astype(bf16)

    def grad_tiles(layer, k, left, right):
        for i in range(D // TILE):
            put(layer, pl.ds(k * 1280 + i * TILE, TILE), tm(left[:, cols_of(i)], right[...]))
        groups[layer, k].s0()

    def t_move(i, src, dst, peer):
        return remote(src, dst, t_s.at[i], t_r.at[i], peer)

    def t_rows(sec, at, n):
        return gt.at[sec, pl.ds(pl.multiple_of(at, 16), n)]

    def t_result(at, n):
        return to_ref.at[pl.ds(pl.multiple_of(at, 16), n)]

    def t_core(sec):
        return t_move(0, t_rows(sec, 128 * (1 - c), 128), tt.at[sec], core)

    def t_over_x(d, sec):
        src = t_rows(sec, 128 * c + 32 * x_at[d], 32)
        return t_move(1, src, tx.at[d - 1, sec], x_peer[d])

    def t_over_y(d):
        src = t_rows(lax.rem(y_at[d], 2), 128 * c + 32 * x + 16 * lax.div(y_at[d], 2), 16)
        return t_move(2, src, ty.at[d - 1], y_peer[d])

    t_own = 128 * c + 32 * x + 16 * yh

    def t_back_y():
        return t_move(3, t_rows(s, t_own, 16), t_result(t_own, 16), y_peer[2])

    def t_keep():
        return pltpu.make_async_copy(t_rows(s, t_own, 16), t_result(t_own, 16), t_l)

    def t_back_x(d):
        ref = t_result(128 * c + 32 * x, 32)
        return t_move(4, ref, ref, x_peer[d])

    def t_back_core():
        ref = t_result(128 * c, 128)
        return t_move(5, ref, ref, core)

    def t_total(i, n):
        ref = gt.at[0, pl.ds(0, n)]
        return t_move(i, ref, ref, core)

    def t_add(sec, at, n, sources):
        here = pl.ds(pl.multiple_of(at, 16), n)
        total = gt[sec, here, :].astype(f32)
        for source in sources:
            total = total + source[...].astype(f32)
        gt[sec, here, :] = total.astype(bf16)

    def t1():
        t_total(0, 256).wait_recv()
        for sec in range(2):
            for i in range(4):
                t_add(sec, 128 * c + 32 * i, 32, [tt.at[sec, pl.ds(32 * i, 32)]])
            for d in (2, 1, 3):
                t_over_x(d, sec).start()

    def t2():
        t_total(1, 192).wait_recv()
        for sec in range(2):
            t_add(sec, 128 * c + 32 * x, 32, [tx.at[i, sec] for i in range(3)])
        for d in (2, 1, 3):
            t_over_y(d).start()

    def t3():
        t_total(2, 48).wait_recv()
        t_add(s, t_own, 16, [ty.at[i] for i in range(3)])
        t_keep().start()
        t_back_y().start()

    def t4():
        t_keep().wait()
        t_back_y().wait_recv()
        for d in (2, 1, 3):
            t_back_x(d).start()

    def t5():
        t_total(4, 96).wait_recv()
        t_back_core().start()

    weights(1, [("core", 5), ("core", 6)])
    cot_copy.wait()
    grad_tiles(1, 2, hb, gb.at[0])
    gg[...] = jnp.zeros_like(gg)

    for layer in (1, 0):
        st = 5 if layer == 1 else 7
        for h in range(HALVES):
            at = rows_of(h)
            if layer == 0:
                ag_wait(5, h, gb.at[1])

            def d_up_tile(j, carry):
                cols = cols_of(j)
                rows = pl.ds(2560 + j * TILE, TILE)
                d_hidden = mm_t(gb[1 - layer, at, :], wb[layer, rows, :])
                up = upb[layer, at, cols]
                t = jnp.tanh(GELU_A * (up + GELU_B * up * up * up))
                slope = 0.5 * (1.0 + t) + 0.5 * up * (1.0 - t * t) * (
                    GELU_A * (1.0 + 3.0 * GELU_B * up * up)
                )
                du[at, cols] = (d_hidden * slope).astype(bf16)
                if layer == 0:
                    hb[at, cols] = (0.5 * up * (1.0 + t)).astype(bf16)

            unrolled(D // TILE, d_up_tile)
            if layer == 0 and h == 1:
                up1.s3()
            if layer == 1 and h == 1:
                down1.s1()
            rs_send(
                st, h,
                lambda j, cols: mm_t(
                    du[at, :], wb[layer, pl.ds(1280 + j * TILE, TILE), :]
                ),
            )
        if layer == 0:
            for i in range(N_PIECES):
                w_total(i, 4, x_s, x_r).wait_send()
                w_total(i, 2, f_s, f_r).wait_send()
        if layer == 0:
            grad_tiles(0, 2, hb, gb.at[1])
            att1.s2()
        for h in range(HALVES):
            dn = rs_take(st, h)
            dx, gain = norm_back(dn, mid[layer, own(h), :], gn[layer, 1:2, :])
            dm = gb[1 - layer, chunk(h, z), :].astype(f32) + dx
            dmid[own(h), :] = dm
            gg[2 * layer + 1 : 2 * layer + 2, :] += gain
            if layer == 0:
                ag_total(4, h).wait_send()
            ag_send(st - 1, h, mb, dm)
        grad_tiles(layer, 1, nm.at[layer], du)
        if layer == 1:
            for j in range(D // TILE):
                pd[:, cols_of(j)] = mm(hb[...], wb[1, 2560:3840, cols_of(j)]).astype(bf16)
            down1.s2()
        else:
            down0.s1()
            down1.s4()
        for h in range(HALVES):
            ag_wait(st - 1, h, mb)
            attention_back(layer, h)
            if h == 1 and layer == 1:
                up1.s1()
            if h == 1 and layer == 0:
                up0.s1()
                att1.s3()
                up1.s4()
                down1.s5()
            at = rows_of(h)
            rs_send(
                st + 1, h,
                lambda j, cols: mm(dqb[0, at, :], wb[layer, 0:ATT, cols])
                + mm(dqb[1, at, :], wb[layer, ATT : 2 * ATT, cols])
                + mm(dqb[2, at, :], wb[layer, 2 * ATT : 3 * ATT, cols]),
            )
        for i in range(3):
            put(layer, pl.ds(i * ATT, ATT), tm(dqb[i], nb[layer]))
        put(layer, pl.ds(960, 320), tm(ct[layer], mb[...]))
        groups[layer, 0].s0()
        if layer == 1:
            up1.s2()
            down1.s3()
        else:
            down0.s2()
        for h in range(HALVES):
            dn = rs_take(st + 1, h)
            dx, gain = norm_back(dn, sx[layer, own(h), :], gn[layer, 0:1, :])
            gg[2 * layer : 2 * layer + 1, :] += gain
            ag_send(st, h, gb.at[layer], dmid[own(h), :] + dx)
        if layer == 1:
            att1.s1()
        else:
            att0.s1()
            up0.s2()

    def gg_copy(d):
        return remote(gg, ggr.at[d - 1], gg_s, gg_r, z_peer[d])

    for d in (1, 2, 3):
        gg_copy(d).start()

    for h in range(HALVES):
        ag_wait(7, h, gb.at[0])
        rs_send(4, h, None)
        at = rows_of(h)
        low = gb[0, at, :]
        before = pre[at, :]
        sig = jax.nn.sigmoid(before)
        d_pre = (
            mm_t(low, w_hid_ref[...]) * (sig * (1.0 + before * (1.0 - sig)))
        ).astype(bf16)
        dctx[at, :] = d_pre
        if h == 0:
            down0.s3()
            att1.s4()
        points = mm_t(d_pre, w_in_ref[...])
        points = points + jnp.where(z == 0, mm_t(low, w_res_ref[...]), 0.0)
        gpad[at, :] = points
    points = gpad[...]
    high = points.astype(bf16)
    low = (points - high.astype(f32)).astype(bf16)
    row = lax.broadcasted_iota(jnp.int32, (ROWS, ROWS), 0)
    col = lax.broadcasted_iota(jnp.int32, (ROWS, ROWS), 1)
    swap = jnp.where(
        ((row >> 4) == (col & 15)) & ((row & 15) == (col >> 4)), 1.0, 0.0
    ).astype(bf16)
    points = mm(swap, high) + mm(swap, low)
    for k in range(8):
        dps[k, :, 0:64] = points[k * 32 : (k + 1) * 32]
        dps[k, :, 64:128] = jnp.zeros((32, 64), f32)
    me = s * 4 + z

    def dp_copy(d):
        to = lax.rem(me + d, 8)
        return remote(
            dps.at[to], dpr.at[me], dp_s, dp_r,
            (lax.div(to, 4), dp, lax.rem(to, 4)),
        )

    for d in range(1, 8):
        dp_copy(d).start()
    dpr[me] = dps[me]

    grad_low = gb[0]
    hid = tm(tokh[...], grad_low).astype(bf16)
    res = tm(patch_ref[...], grad_low).astype(bf16)
    inn = tm(patch_ref[...], dctx[...]).astype(bf16)
    for sec in range(2):
        lanes = slice(sec * 640, sec * 640 + 640)
        gt[sec, 0:160, 0:640] = hid[0:160, lanes]
        gt[sec, 0:160, 640:1280] = hid[160:320, lanes]
        gt[sec, 160:192, 0:640] = res[0:32, lanes]
        gt[sec, 160:192, 640:1280] = res[32:64, lanes]
        gt[sec, 192:224, :] = jnp.zeros((32, D), bf16)
        gt[sec, 192:224, 0:320] = inn[sec * 32 : sec * 32 + 32]
    total = gg[...]
    remote(ggr, ggr, gg_s, gg_r, core).wait_recv()
    for d in (1, 2, 3):
        total = total + ggr[d - 1]
    for sec in range(2):
        gt[sec, 224:256, :] = jnp.concatenate(
            [total[2 * sec : 2 * sec + 2], jnp.zeros((30, D), f32)], axis=0
        ).astype(bf16)

    for sec in range(2):
        t_core(sec).start()
    up0.s3()
    att0.s2()
    t1()
    att0.s3()
    down0.s4()
    down1.s6()
    t2()
    up0.s4()
    up1.s5()
    for h in range(HALVES):
        mlp_out(1, h)
        own_out(h)
    down0.s5()
    att1.s5()
    att0.s4()
    t3()
    up0.s5()
    up1.s6()
    down1.s7()
    for h in range(HALVES):
        pass_out(h)
    down0.s6()
    att1.s6()
    t4()
    att0.s5()
    up0.s6()
    up1.s7()
    down0.s7()
    att1.s7()
    t5()
    att0.s6()
    up0.s7()
    att0.s7()
    seven = dps.at[pl.ds(0, 7)]
    remote(seven, seven, dp_s, dp_r, core).wait_recv()
    for sec in range(2):
        points_ref[sec] = dpr[4 * sec] + dpr[4 * sec + 1] + dpr[4 * sec + 2] + dpr[4 * sec + 3]

    for i in range(N_PIECES):
        w_total(i, 4, w_s, w_r).wait_send()
    for group in groups.values():
        group.drain()
    for i, n in ((0, 256), (1, 192), (2, 48), (3, 16), (4, 96)):
        t_total(i, n).wait_send()
    t_back_core().wait()
    gn_send.wait_send()
    for h in range(HALVES):
        rs_total(7, h).wait_send()
        rs_total(4, h).wait_send()
        for st in (0, 1, 2, 3, 5, 6, 7):
            ag_total(st, h).wait_send()
        lo_cross(h).wait_send()
        lo_keep(h).wait()
        for i in (1, 2):
            lo_total(i, h).wait()
    remote(ggr, ggr, gg_s, gg_r, core).wait_send()
    remote(seven, seven, dp_s, dp_r, core).wait_send()


def run_layers(patch_in, w_in, w_hid, w_res, gain_a, gain_m, wq, wo, wu, wd, cotangent):
    cos, sin, turn = rotary_arrays()
    vm = pl.BlockSpec(memory_space=pltpu.VMEM)
    hbm = pl.BlockSpec(memory_space=pl.ANY)
    dma = pltpu.SemaphoreType.DMA
    scratch = [
        pltpu.VMEM((2, LAYER_ROWS, D), bf16),
        pltpu.VMEM((2, 2, D), f32),
        pltpu.VMEM((ROWS, ATT), bf16),
        pltpu.VMEM((ROWS, ATT), f32),
        pltpu.VMEM((2, ROWS // 4, D), f32),
        pltpu.VMEM((2, ROWS // 4, D), f32),
        pltpu.VMEM((2, ROWS, D), bf16),
        pltpu.VMEM((2, ROWS, D), bf16),
        pltpu.VMEM((2, 3, ROWS, ATT), bf16),
        pltpu.VMEM((2, ROWS // BLOCK, HEADS_HERE * BLOCK, BLOCK), f32),
        pltpu.VMEM((2, ROWS, ATT), bf16),
        pltpu.VMEM((2, ROWS, D), f32),
        pltpu.VMEM((ROWS, D), bf16),
        pltpu.VMEM((2, ROWS, D), bf16),
        pltpu.VMEM((ROWS, D), bf16),
        pltpu.VMEM((ROWS, D), bf16),
        pltpu.VMEM((3, ROWS, ATT), bf16),
        pltpu.VMEM((ROWS, ATT), bf16),
        pltpu.VMEM((LAYER_ROWS, D), bf16),
        pltpu.VMEM((2, PACK_ROWS - LAYER_ROWS, D), bf16),
        pltpu.VMEM((2, ROWS, D), bf16),
        pltpu.VMEM((2, 3, ROWS // 4, D), bf16),
        pltpu.VMEM((ROWS // 4, D), f32),
        pltpu.VMEM((2, ROWS // 4, D), bf16),
        pltpu.VMEM((8, D), f32),
        pltpu.VMEM((3, 8, D), f32),
        pltpu.VMEM((8, 32, 128), f32),
        pltpu.VMEM((8, 32, 128), f32),
        pltpu.VMEM((ROWS, 64), f32),
        pltpu.VMEM((3, 640, D), bf16),
        pltpu.VMEM((3, 192, D), bf16),
        pltpu.VMEM((3, 96, D), bf16),
        pltpu.VMEM((3, 3, 128, D), bf16),
        pltpu.VMEM((3, 64, D), bf16),
        pltpu.VMEM((3, 32, D), bf16),
        pltpu.VMEM((3, 3, 48, D), bf16),
        pltpu.VMEM((2, 128, D), bf16),
        pltpu.VMEM((3, 2, 32, D), bf16),
        pltpu.VMEM((3, 16, D), bf16),
        pltpu.VMEM((ROWS, D), bf16),
        dma, *[dma((N_PIECES,))] * 6,
        dma, dma, dma,
        dma((9, HALVES)), dma((9, HALVES)),
        dma((8, HALVES)), dma((8, HALVES)),
        dma((HALVES,)), dma((3, HALVES)), dma((3, HALVES)),
        dma, dma, dma, dma,
        dma((2, 3, 14)), dma((2, 3, 14)), dma((2, 3)),
        dma((6,)), dma((6,)), dma,
        *[pltpu.SemaphoreType.REGULAR((3,))] * 3,
    ]
    return pl.pallas_call(
        layers_kernel,
        out_shape=(
            jax.ShapeDtypeStruct((2 * ROWS, D), bf16),
            jax.ShapeDtypeStruct((LAYER_ROWS, D), bf16),
            jax.ShapeDtypeStruct((PACK_ROWS - LAYER_ROWS, D), bf16),
            jax.ShapeDtypeStruct((2, 32, 128), f32),
        ),
        in_specs=[vm] * 6 + [hbm] * 5 + [vm] * 3,
        out_specs=(hbm, hbm, hbm, vm),
        scratch_shapes=scratch,
        compiler_params=pltpu.CompilerParams(
            collective_id=0, has_side_effects=True, vmem_limit_bytes=62 * 2**20
        ),
        cost_estimate=pl.CostEstimate(
            flops=15_000_000_000, bytes_accessed=50_000_000, transcendentals=4_000_000
        ),
        name="layers",
    )(
        patch_in, w_in, w_hid, w_res, gain_a, gain_m, wq, wo, wu, wd, cotangent,
        jnp.asarray(cos, f32), jnp.asarray(sin, f32), jnp.asarray(turn, bf16),
    )


STEP = 320


def widen_kernel(big_ref, small_ref, qkv, out, up, down, hid, res, inn, gain_a, gain_m):
    i = pl.program_id(0)
    for first, last, ref in ((0, 3, qkv), (3, 4, out), (4, 8, up), (8, 12, down)):

        @pl.when((i >= first) & (i < last))
        def _(ref=ref):
            ref[...] = big_ref[...].astype(f32)

    @pl.when(i == 0)
    def _():
        small = small_ref[...].astype(f32)
        hid[0:160, :] = small[0:160, 0:640]
        hid[160:320, :] = small[0:160, 640:1280]
        res[0:32, :] = small[160:192, 0:640]
        res[32:64, :] = small[160:192, 640:1280]
        inn[...] = small[192:224, 0:320]
        gain_a[...] = small[224:225]
        gain_m[...] = small[225:226]


def widen(big, small):
    def tall(first, count):
        return pl.BlockSpec((STEP, D), lambda i: (jnp.clip(i - first, 0, count - 1), 0))

    def whole(rows, columns):
        return pl.BlockSpec((rows, columns), lambda i: (0, 0))

    shapes = ((960, D), (320, D), (1280, D), (1280, D), (320, 640), (64, 640), (32, 320), (1, D), (1, D))
    return pl.pallas_call(
        widen_kernel,
        grid=(LAYER_ROWS // STEP,),
        out_shape=[jax.ShapeDtypeStruct(shape, f32) for shape in shapes],
        in_specs=[
            pl.BlockSpec((STEP, D), lambda i: (i, 0)),
            pl.BlockSpec((256, D), lambda i: (0, 0)),
        ],
        out_specs=[tall(0, 3), tall(3, 1), tall(4, 4), tall(8, 4)]
        + [whole(*shape) for shape in shapes[4:]],
        compiler_params=pltpu.CompilerParams(vmem_limit_bytes=40 * 2**20),
        cost_estimate=pl.CostEstimate(flops=0, bytes_accessed=32_000_000, transcendentals=0),
        name="widen",
    )(big, small)


def per_device(
    series, missing, w_in, w_hid, w_res, gain_attn, w_qkv, w_out, gain_mlp, w_up, w_down, cotangent
):
    s = lax.axis_index("section")
    contexts = series.shape[0] // 2
    keep = (1 - missing).astype(f32)
    values = lax.dynamic_slice_in_dim(series * keep, s * contexts, contexts, 0)
    flags = lax.dynamic_slice_in_dim(missing, s * contexts, contexts, 0).astype(f32)
    patch_in = jnp.concatenate(
        [values.reshape(ROWS, PATCH), flags.reshape(ROWS, PATCH)], axis=1
    ).astype(bf16)
    wq = jnp.transpose(w_qkv[0], (1, 2, 0)).reshape(3 * ATT, D)
    layer_out, big, small, points = run_layers(
        patch_in, w_in, w_hid, w_res, gain_attn, gain_mlp, wq, w_out[0], w_up[0], w_down[0], cotangent
    )
    g_qkv, g_out, g_up, g_down, g_hid, g_res, g_in, gain_a, gain_m = widen(big, small)
    points = points[:, :, :PATCH].reshape(2, 2, contexts, PATCH)
    points = jnp.transpose(points, (0, 2, 1, 3)).reshape(2 * contexts, 2 * PATCH)
    block = s * 4 + lax.axis_index("tensor")
    keep_here = lax.dynamic_slice_in_dim(keep, block * 2 * PATCH, 2 * PATCH, 1)
    series_grad = points * keep_here
    g_qkv = jnp.transpose(g_qkv.reshape(3, ATT, D), (2, 0, 1))
    return (
        layer_out[None],
        series_grad,
        g_in,
        g_hid,
        g_res,
        gain_a,
        g_qkv[None],
        g_out[None],
        gain_m,
        g_up[None],
        g_down[None],
    )


def solution(mesh):
    in_specs = (
        P("dp", None),
        P("dp", None),
        P(None, "tensor"),
        P("tensor", None),
        P(),
        P("section", None),
        P("section", None, None, "tensor"),
        P("section", "tensor", None),
        P("section", None),
        P("section", None, "tensor"),
        P("section", "tensor", None),
        P("dp", None),
    )
    out_specs = (
        P("section", "dp", None),
        P("dp", ("section", "tensor")),
        P("section", "tensor"),
        P("tensor", "section"),
        P(None, "section"),
        P("section", None),
        P("section", None, None, "tensor"),
        P("section", "tensor", None),
        P("section", None),
        P("section", None, "tensor"),
        P("section", "tensor", None),
    )
    return jax.shard_map(
        per_device, mesh=mesh, in_specs=in_specs, out_specs=out_specs, check_vma=False
    )
```

```python
import math

import jax
import jax.numpy as jnp
import numpy as np
from jax import lax
from jax.experimental import pallas as pl
from jax.experimental.pallas import tpu as pltpu
from jax.sharding import PartitionSpec as P

D = 1280
HEADS_HERE = 4
HEAD_DIM = 80
ATT = HEADS_HERE * HEAD_DIM
PATCH = 32
PATCHES = 16
ROWS = 256
HALVES = 2
RH = ROWS // HALVES
RQ = RH // 4
TILE = 256
BLOCK = 128
MATS = ((0, 960), (960, 320), (1280, 1280), (2560, 1280))
PIECES = tuple((320 * i, 320, 0 if i < 3 else 1 if i < 4 else 2 if i < 8 else 3) for i in range(12))
N_PIECES = len(PIECES)
LAYER_ROWS = 3840
PACK_ROWS = 4096
RS_BEFORE = {2: 0, 3: 1, 5: 3, 6: 2, 7: 5, 8: 6, 4: 8}
MESH = pl.DeviceIdType.MESH
f32 = jnp.float32
bf16 = jnp.bfloat16
eps_norm = 1e-06
masked_score = -1e30
GELU_A = math.sqrt(2.0 / math.pi)
GELU_B = 0.044715


def mm(a, b):
    return lax.dot_general(a, b, (((1,), (0,)), ((), ())), preferred_element_type=f32)


def mm_t(a, b):
    return lax.dot_general(a, b, (((1,), (1,)), ((), ())), preferred_element_type=f32)


def tm(a, b):
    return lax.dot_general(a, b, (((0,), (0,)), ((), ())), preferred_element_type=f32)


def unrolled(count, body):
    for j in range(count):
        body(j, 0)


def rotary_arrays():
    half = HEAD_DIM // 2
    position = (np.arange(BLOCK) % PATCHES).astype(np.float32)
    frequency = np.exp(
        np.arange(half, dtype=np.float32) * np.float32(-2.0 * math.log(10000.0) / HEAD_DIM)
    )
    angles = position[:, None] * frequency[None, :]
    lane = np.arange(ATT) % half
    turn = np.zeros((ATT, ATT), np.float32)
    for j in range(ATT):
        if j % HEAD_DIM < half:
            turn[j + half, j] = -1.0
        else:
            turn[j - half, j] = 1.0
    return np.cos(angles)[:, lane], np.sin(angles)[:, lane], turn


def places():
    s = lax.axis_index("section")
    dp = lax.axis_index("dp")
    z = lax.axis_index("tensor")
    c = lax.rem(dp, 2)
    yh = lax.rem(lax.div(dp, 2), 2)
    x = lax.div(dp, 4)
    return s, dp, z, x, yh, c


def layers_kernel(
    series_ref, missing_ref, w_in_in, w_hid_in, w_res_in, gain_a_ref, gain_m_ref, wq_ref, wo_ref, wu_ref, wd_ref,
    cot_ref, cos_in, sin_in, turn_in,
    lo_ref, go_ref, points_ref,
    w_in_ref, w_hid_ref, w_res_ref, cos_ref, sin_ref, turn_ref, in_l,
    patch_ref, wb, gn, tokh, pre, sx, mid, nb, nm, qb, pb, ct, upb, hb, gb, mb, du, dqb, dctx, gv, gt,
    sb, rb, dmid, ob, gg, ggr, dps, dpr, gpad,
    th, r1, r2, ra1, ra2, rb3, tt, tx, ty, pd,
    w_loc, w_s, w_r, x_s, x_r, f_s, f_r, gn_s, gn_r, cot_l,
    rs_s, rs_r, ag_s, ag_r, lo_l, lo_s, lo_r, gg_s, gg_r, dp_s, dp_r,
    e_s, e_r, e_l, t_s, t_r, t_l, free_th, free_r1, free_r2,
):
    s, dp, z, x, yh, c = places()
    other = 1 - s
    z_peer = [None] + [(s, dp, lax.rem(z + d, 4)) for d in (1, 2, 3)]
    z_at = [z] + [lax.rem(z + d, 4) for d in (1, 2, 3)]
    y_a = (other, dp, z)
    y_b = (other, dp + 2 - 4 * yh, z)
    core = (s, dp + 1 - 2 * c, z)
    across = [(other, dp, z_at[d]) for d in range(4)]
    y = 2 * yh + s
    x_at = [x] + [lax.rem(x + d, 4) for d in (1, 2, 3)]
    y_at = [y] + [lax.rem(y + d, 4) for d in (1, 2, 3)]
    x_peer = [None] + [(s, x_at[d] * 4 + 2 * yh + c, z) for d in (1, 2, 3)]
    y_peer = [None] + [
        (lax.rem(y_at[d], 2), x * 4 + 2 * lax.div(y_at[d], 2) + c, z) for d in (1, 2, 3)
    ]
    x_up, x_down = x_peer[1], x_peer[3]
    w_refs = (wq_ref, wo_ref, wu_ref, wd_ref)

    small_inputs = [
        pltpu.make_async_copy(src, dst, in_l.at[i])
        for i, (src, dst) in enumerate((
            (w_in_in, w_in_ref), (w_hid_in, w_hid_ref), (w_res_in, w_res_ref),
            (cos_in, cos_ref), (sin_in, sin_ref), (turn_in, turn_ref),
        ))
    ]
    for copy in small_inputs:
        copy.start()
    barrier = pltpu.get_barrier_semaphore()
    peers = z_peer[1:] + across + [y_b, core] + x_peer[1:] + [y_peer[2]]
    for peer in peers:
        pl.semaphore_signal(barrier, inc=1, device_id=peer, device_id_type=MESH)
    pl.semaphore_wait(barrier, len(peers))

    def remote(src, dst, ssem, rsem, peer):
        return pltpu.make_async_remote_copy(
            src_ref=src, dst_ref=dst, send_sem=ssem, recv_sem=rsem,
            device_id=peer, device_id_type=MESH,
        )

    odd = lax.rem(x, 2)

    def w_local(m):
        off, n = MATS[m]
        return pltpu.make_async_copy(w_refs[m], wb.at[s, pl.ds(off, n)], w_loc)

    def share(i, parity, k):
        off, n, m = PIECES[i]
        first = (n // 4 + 31) // 32 * 16 if i % 2 == 0 else n // 4 // 32 * 16
        size = first if k == 0 else n // 4 - first
        return (2 * c + parity) * (n // 4) + k * first, size

    def w_over_y(i, k):
        off, n, m = PIECES[i]
        at, size = share(i, odd, k)
        src = w_refs[m].at[pl.ds(pl.multiple_of(off - MATS[m][0] + at, 16), size)]
        dst = wb.at[s, pl.ds(pl.multiple_of(off + at, 16), size)]
        return remote(src, dst, w_s, w_r.at[i], (y_a, y_b)[k])

    def w_over_x(i, k, parity):
        at, size = share(i, parity, k)
        ref = wb.at[other, pl.ds(pl.multiple_of(PIECES[i][0] + at, 16), size)]
        return remote(ref, ref, x_s, x_r.at[i], (x_up, x_down)[k])

    def w_to_core(i, q):
        off, n, m = PIECES[i]
        parity = odd if q == 0 else 1 - odd
        ref = wb.at[other, pl.ds(pl.multiple_of(off + (2 * c + parity) * (n // 4), 16), n // 4)]
        return remote(ref, ref, f_s, f_r.at[i], core)

    def w_total(i, part, ssem, rsem):
        ref = wb.at[0, pl.ds(0, PIECES[i][1] // part)]
        return remote(ref, ref, ssem, rsem.at[i], core)

    def w_sent(part, ssem, rsem):
        ref = wb.at[0, pl.ds(0, LAYER_ROWS // part)]
        return remote(ref, ref, ssem, rsem.at[0], core)

    def weights(layer, steps):
        @pl.when(s != layer)
        def _():
            for step, i in steps:
                if step == "y":
                    w_total(i, 4, w_s, w_r).wait_recv()
                    for k in range(2):
                        w_over_x(i, k, odd).start()
                    w_to_core(i, 0).start()
                elif step == "x":
                    w_total(i, 4, x_s, x_r).wait_recv()
                    w_to_core(i, 1).start()
                else:
                    w_total(i, 2, f_s, f_r).wait_recv()

    gains = gn.at[s]
    gains[0:1, :] = gain_a_ref[...]
    gains[1:2, :] = gain_m_ref[...]
    gn_send = remote(gn.at[s], gn.at[s], gn_s, gn_r, y_a)
    cot_copy = pltpu.make_async_copy(
        cot_ref.at[pl.ds(pl.multiple_of(s * ROWS, ROWS), ROWS)], gb.at[0], cot_l
    )
    gn_send.start()
    def start_weights(first, last):
        for i in range(first, last):
            for k in range(2):
                w_over_y(i, k).start()

    start_weights(0, 4)
    for m in range(4):
        w_local(m).start()
    cot_copy.start()

    def rows_of(h):
        return pl.ds(h * RH, RH)

    def chunk(h, zz):
        return pl.ds(pl.multiple_of(h * RH + zz * RQ, RQ), RQ)

    def cols_of(j):
        return pl.ds(j * TILE, TILE)

    def rs_copy(st, h, d, cols=None):
        src = sb.at[st % 2, chunk(h, z_at[d])]
        dst = rb.at[st % 2, d - 1, pl.ds(h * RQ, RQ)]
        if cols is not None:
            src = sb.at[st % 2, chunk(h, z_at[d]), cols]
            dst = rb.at[st % 2, d - 1, pl.ds(h * RQ, RQ), cols]
        return remote(src, dst, rs_s.at[st, h], rs_r.at[st, h], z_peer[d])

    def rs_total(st, h):
        ref = rb.at[st % 2, pl.ds(0, 3), pl.ds(h * RQ, RQ)]
        return remote(ref, ref, rs_s.at[st, h], rs_r.at[st, h], core)

    def rs_send(st, h, produce):
        if st in RS_BEFORE:
            rs_total(RS_BEFORE[st], h).wait_send()

        if produce is None:
            sb[st % 2, rows_of(h), :] = pd[rows_of(h), :]
            for d in (2, 1, 3):
                rs_copy(st, h, d).start()
            return

        def body(j, carry):
            cols = cols_of(j)
            sb[st % 2, rows_of(h), cols] = produce(j, cols).astype(bf16)
            if j in (2, 4):
                part = pl.ds(0, 768) if j == 2 else pl.ds(768, 512)
                for d in (2, 1, 3):
                    rs_copy(st, h, d, part).start()

        unrolled(D // TILE, body)

    def rs_take(st, h):
        total = sb[st % 2, chunk(h, z), :].astype(f32)
        rs_total(st, h).wait_recv()
        for d in (1, 2, 3):
            total = total + rb[st % 2, d - 1, pl.ds(h * RQ, RQ), :].astype(f32)
        return total

    def ag_copy(st, h, d, dst):
        at = dst.at[chunk(h, z)]
        return remote(at, at, ag_s.at[st, h], ag_r.at[st, h], z_peer[d])

    def ag_send(st, h, dst, value):
        dst[chunk(h, z), :] = value.astype(bf16)
        for d in (2, 1, 3):
            ag_copy(st, h, d, dst).start()

    def ag_total(st, h):
        ref = pd.at[pl.ds(0, 3 * RQ)]
        return remote(ref, ref, ag_s.at[st, h], ag_r.at[st, h], core)

    def ag_wait(st, h, dst):
        ag_total(st, h).wait_recv()

    def own(h):
        return pl.ds(h * RQ, RQ)

    def scale_of(v):
        return lax.rsqrt(jnp.mean(v * v, axis=-1, keepdims=True) + eps_norm)

    def norm(v, g):
        return v * scale_of(v) * g

    def norm_back(dn, v, g):
        r = scale_of(v)
        weighted = g * dn
        inner = jnp.mean(v * weighted, axis=-1, keepdims=True)
        return r * weighted - v * (r * r * r * inner), jnp.sum(dn * v * r, axis=0, keepdims=True)

    head_lane = lax.broadcasted_iota(jnp.int32, (1, ATT), 1)
    head_mask = [
        (head_lane >= HEAD_DIM * h) & (head_lane < HEAD_DIM * (h + 1)) for h in range(HEADS_HERE)
    ]

    def spread(v):
        wide = v.astype(f32)
        return jnp.concatenate(
            [jnp.where(m, wide, 0.0) for m in head_mask], axis=0
        ).astype(bf16)

    def gather(v):
        total = jnp.where(head_mask[0], v[:BLOCK], 0.0)
        for h in range(1, HEADS_HERE):
            total = total + jnp.where(head_mask[h], v[h * BLOCK : (h + 1) * BLOCK], 0.0)
        return total

    def turned(v, sign):
        high = v.astype(bf16)
        low = (v - high.astype(f32)).astype(bf16)
        swapped = mm(high, turn_ref[...]) + mm(low, turn_ref[...])
        if sign < 0:
            swapped = -swapped
        return v * cos_ref[...] + swapped * sin_ref[...]

    inv = 1.0 / math.sqrt(HEAD_DIM)

    def blocks_of(h):
        return range(h * RH // BLOCK, (h + 1) * RH // BLOCK)

    def attention_front(layer, h):
        for b in blocks_of(h):
            at = pl.ds(b * BLOCK, BLOCK)
            normed = nb[layer, at, :]
            first = b == 0
            if first:
                weights(layer, [("core", 0)])
            q = turned(mm_t(normed, wb[layer, 0:ATT, :]), 1).astype(bf16)
            if first:
                weights(layer, [("core", 1)])
            k = turned(mm_t(normed, wb[layer, ATT : 2 * ATT, :]), 1).astype(bf16)
            if first:
                weights(layer, [("core", 2)])
            v = mm_t(normed, wb[layer, 2 * ATT : 3 * ATT, :]).astype(bf16)
            qb[layer, 0, at, :] = q
            qb[layer, 1, at, :] = k
            qb[layer, 2, at, :] = v
            scores = mm_t(spread(q), k) * inv
            row = lax.broadcasted_iota(jnp.int32, scores.shape, 0) & (BLOCK - 1)
            col = lax.broadcasted_iota(jnp.int32, scores.shape, 1)
            allowed = (col <= row) & (col >= (row & (BLOCK - PATCHES)))
            scores = jnp.where(allowed, scores, masked_score)
            e = jnp.exp(scores - jnp.max(scores, axis=-1, keepdims=True))
            probs = e / jnp.sum(e, axis=-1, keepdims=True)
            pb[layer, b] = probs
            ct[layer, at, :] = gather(mm(probs.astype(bf16), v)).astype(bf16)

    def attention_back(layer, h):
        for b in blocks_of(h):
            at = pl.ds(b * BLOCK, BLOCK)
            spread_d = spread(mm_t(mb[at, :], wb[layer, 960:1280, :]).astype(bf16))
            spread_q = spread(qb[layer, 0, at, :])
            k = qb[layer, 1, at, :]
            v = qb[layer, 2, at, :]
            probs = pb[layer, b]
            d_probs = mm_t(spread_d, v)
            d_scores = (
                probs * (d_probs - jnp.sum(probs * d_probs, axis=-1, keepdims=True))
            ).astype(bf16)
            d_q = gather(mm(d_scores, k)) * inv
            d_k = tm(d_scores, spread_q) * inv
            dqb[0, at, :] = turned(d_q, -1).astype(bf16)
            dqb[1, at, :] = turned(d_k, -1).astype(bf16)
            dqb[2, at, :] = tm(probs.astype(bf16), spread_d).astype(bf16)

    contexts = pl.ds(pl.multiple_of(s * PATCHES, PATCHES), PATCHES)
    flags = missing_ref[contexts, :].astype(f32)
    values = series_ref[contexts, :] * (1.0 - flags)
    for j in range(PATCHES):
        at = pl.ds(j, PATCHES, stride=PATCHES)
        own_points = slice(j * PATCH, (j + 1) * PATCH)
        gpad[at, :] = jnp.concatenate(
            [values[:, own_points], flags[:, own_points], jnp.zeros((PATCHES, 64), f32)], axis=1
        )
    patch_ref[...] = gpad[:, 0:64].astype(bf16)
    for copy in small_inputs:
        copy.wait()
    for h in range(HALVES):
        at = rows_of(h)
        before = mm(patch_ref[at, :], w_in_ref[...])
        pre[at, :] = before
        tokh[at, :] = (before * jax.nn.sigmoid(before)).astype(bf16)
        rs_send(0, h, lambda j, cols: mm(tokh[at, :], w_hid_ref[:, cols]))
    gn_send.wait_recv()
    pltpu.make_async_copy(wb.at[s], wb.at[s], w_loc).wait()
    for h in range(HALVES):
        start_weights(4 + 2 * h, 6 + 2 * h)
        weights(0, [("y", 0)] if h == 0 else [("y", 1), ("y", 2)])
        stream = rs_take(0, h) + mm(patch_ref[chunk(h, z), :], w_res_ref[...])
        sx[0, own(h), :] = stream
        ag_send(0, h, nb.at[0], norm(stream, gn[0, 0:1, :]))
    start_weights(8, 10)
    weights(0, [("x", 0), ("y", 3), ("x", 1), ("x", 2), ("y", 4)])
    weights(1, [("y", 0), ("y", 1), ("y", 2)])

    def lo_rows(sec, h):
        return lo_ref.at[pl.ds(pl.multiple_of(sec * ROWS + h * RH + z * RQ, RQ), RQ)]

    def lo_keep(h):
        return pltpu.make_async_copy(ob.at[s, own(h)], lo_rows(s, h), lo_l.at[h])

    def lo_cross(h):
        return remote(ob.at[other, own(h)], lo_rows(s, h), lo_s.at[0, h], lo_r.at[0, h], y_a)

    def lo_arrive(h):
        return remote(ob.at[other, own(h)], lo_rows(other, h), lo_s.at[0, h], lo_r.at[0, h], y_a)

    def lo_own(h, d):
        return remote(ob.at[s, own(h)], lo_rows(s, h), lo_s.at[1, h], lo_r.at[1, h], z_peer[d])

    def lo_pass(h, d):
        ref = lo_rows(other, h)
        return remote(ref, ref, lo_s.at[2, h], lo_r.at[2, h], z_peer[d])

    def lo_total(i, h):
        ref = pd.at[pl.ds(0, 3 * RQ)]
        return remote(ref, ref, lo_s.at[i, h], lo_r.at[i, h], core)

    def cross_out(layer, h):
        @pl.when(s != layer)
        def _():
            lo_cross(h).start()

    def own_out(h):
        lo_keep(h).start()
        for d in (2, 1, 3):
            lo_own(h, d).start()

    def pass_out(h):
        lo_arrive(h).wait_recv()
        for d in (2, 1, 3):
            lo_pass(h, d).start()

    def mlp_out(layer, h):
        out = (mid[layer, own(h), :] + rs_take(2 + 2 * layer, h)).astype(bf16)
        ob[layer, own(h), :] = out
        cross_out(layer, h)
        return out

    for layer in range(2):
        for h in range(HALVES):
            ag_wait(2 * layer, h, nb.at[layer])
            attention_front(layer, h)
            if h == 0 and layer == 0:
                start_weights(10, 12)
                weights(0, [("y", 5), ("x", 3), ("x", 4), ("y", 6), ("core", 3)])
                weights(1, [("y", 3), ("y", 4), ("y", 5)])
            if h == 0 and layer == 1:
                weights(1, [("core", 3)])
            if h == 1 and layer == 0:
                weights(0, [("y", 7)])
            at = rows_of(h)
            rs_send(
                1 + 2 * layer, h, lambda j, cols: mm(ct[layer, at, :], wb[layer, 960:1280, cols])
            )
        if layer == 0:
            weights(0, [("y", 8), ("x", 5), ("x", 6)])
            weights(1, [("y", 6), ("x", 0), ("x", 1), ("x", 2), ("x", 3)])
        for h in range(HALVES):
            if layer == 0 and h == 1:
                weights(0, [("y", 9), ("x", 7), ("y", 10), ("y", 11)])
                weights(1, [("y", 7)])
            middle = sx[layer, own(h), :] + rs_take(1 + 2 * layer, h)
            mid[layer, own(h), :] = middle
            ag_send(1 + 2 * layer, h, nm.at[layer], norm(middle, gn[layer, 1:2, :]))
        if layer == 0:
            weights(0, [("x", 8)] + [("core", i) for i in range(4, 8)])
            weights(1, [("y", 8), ("y", 9), ("x", 4), ("x", 5)])
        else:
            weights(1, [("core", i) for i in range(4, 8)])
        for h in range(HALVES):
            ag_wait(1 + 2 * layer, h, nm.at[layer])
            at = rows_of(h)

            def up_tile(j, carry):
                cols = cols_of(j)
                up = mm(nm[layer, at, :], wb[layer, 1280:2560, cols])
                upb[layer, at, cols] = up
                t = jnp.tanh(GELU_A * (up + GELU_B * up * up * up))
                hb[at, cols] = (0.5 * up * (1.0 + t)).astype(bf16)

            unrolled(D // TILE, up_tile)
            if layer == 1:
                continue
            if h == 0 and layer == 0:
                weights(0, [("x", 9), ("x", 10), ("x", 11)] + [("core", i) for i in range(8, 12)])
                weights(1, [("y", 10), ("y", 11), ("x", 6), ("x", 7)])
            rs_send(
                2 + 2 * layer, h, lambda j, cols: mm(hb[at, :], wb[layer, 2560:3840, cols])
            )
        if layer == 0:
            weights(1, [("x", 8), ("x", 9)])
            for h in range(HALVES):
                out = mlp_out(0, h)
                stream = out.astype(f32)
                sx[1, own(h), :] = stream
                ag_send(2, h, nb.at[1], norm(stream, gn[1, 0:1, :]))
            weights(1, [("x", 10), ("x", 11)])

    xa = x + 1 - 2 * lax.rem(x, 2)
    xb = 3 - x
    to_xa = (s, xa * 4 + 2 * yh + c, z)
    to_xb = (s, xb * 4 + 2 * yh + c, z)
    j1 = lax.rem(lax.div(x + 1, 2), 2)
    j2 = lax.div(x, 2)
    i1 = lax.div(x, 2)
    i2 = lax.rem(x, 2)
    half_at = (64 + 64 * j1, 192 + 64 * i1)
    half_off = (64 + 64 * (1 - j1), 192 + 64 * (1 - i1))
    quarter_at = (half_at[0] + 32 * j2, half_at[1] + 32 * i2)
    quarter_off = (half_at[0] + 32 * (1 - j2), half_at[1] + 32 * (1 - i2))
    first_peer = (to_xa, to_xb)
    second_peer = (to_xb, to_xa)

    class Group:
        def __init__(self, layer, k):
            self.layer, self.k = layer, k
            self.buf = gv if layer == 1 else wb.at[1]
            self.mine = k * 1280 + c * 640
            self.theirs = k * 1280 + (1 - c) * 640
            self.home = s == layer

        def rows(self, at, n):
            return self.buf.at[pl.ds(pl.multiple_of(self.mine + at, 16), n)]

        def result(self, at, n):
            return go_ref.at[pl.ds(pl.multiple_of(self.mine + at, 16), n)]

        def move(self, i, src, dst, peer):
            return remote(src, dst, e_s.at[self.layer, self.k], e_r.at[self.layer, self.k, i], peer)

        def add(self, at, n, sources):
            def body(i, carry):
                here = pl.ds(pl.multiple_of(self.mine + at + i * 16, 16), 16)
                there = pl.ds(pl.multiple_of(i * 16, 16), 16)
                total = self.buf[here, :].astype(f32)
                for source in sources:
                    total = total + source[there, :].astype(f32)
                self.buf[here, :] = total.astype(bf16)
                return carry

            lax.fori_loop(0, n // 16, body, 0)

        def total(self, i, n):
            ref = th.at[self.k, pl.ds(0, n)]
            return self.move(i, ref, ref, core)

        def core(self):
            src = self.buf.at[pl.ds(pl.multiple_of(self.theirs, 16), 640)]
            return self.move(0, src, th.at[self.k], core)

        def first(self, b, hf):
            dst = r1.at[self.k, pl.ds(128 * b + 64 * hf, 64)]
            return self.move(1, self.rows(320 * hf + half_off[b], 64), dst, first_peer[b])

        def second(self, b, hf):
            dst = r2.at[self.k, pl.ds(64 * b + 32 * hf, 32)]
            return self.move(2, self.rows(320 * hf + quarter_off[b], 32), dst, second_peer[b])

        def a_over_y(self, d):
            src = self.rows(320 * lax.div(y_at[d], 2), 64)
            return self.move(3, src, ra1.at[self.k, d - 1], y_peer[d])

        def a_over_x(self, d):
            src = self.rows(320 * yh + 16 * x_at[d], 16)
            return self.move(4, src, ra2.at[self.k, d - 1], x_peer[d])

        def b_over_y(self, d, b):
            src = self.rows(320 * lax.div(y_at[d], 2) + quarter_at[b], 32)
            return self.move(5, src, rb3.at[self.k, d - 1, pl.ds(32 * b, 32)], y_peer[d])

        def a_back_x(self, d):
            at = 320 * yh + 16 * x
            return self.move(6, self.rows(at, 16), self.result(at, 16), x_peer[d])

        def b_back_y(self, b):
            at = 320 * yh + quarter_at[b]
            return self.move(7, self.rows(at, 32), self.result(at, 32), y_peer[2])

        def back_second(self, b, hf):
            ref = self.result(320 * hf + quarter_at[b], 32)
            return self.move(8, ref, ref, second_peer[b])

        def back_first(self, b, hf):
            ref = self.result(320 * hf + half_at[b], 64)
            return self.move(9, ref, ref, first_peer[b])

        def a_back_y(self):
            ref = self.result(320 * yh, 64)
            return self.move(10, ref, ref, y_peer[2])

        def back_core(self, at, n=640):
            ref = self.result(at, n)
            return self.move(11, ref, ref, core)

        def keep(self, at, n):
            return pltpu.make_async_copy(
                self.rows(at, n), self.result(at, n), e_l.at[self.layer, self.k]
            )

        def to_homes(self, copies):
            @pl.when(self.home)
            def _():
                for copy in copies(2):
                    copy.start()

            @pl.when(jnp.logical_not(self.home))
            def _():
                for d in (1, 3):
                    for copy in copies(d):
                        copy.start()

        def s0(self):
            if self.layer == 0:
                pl.semaphore_wait(free_th.at[self.k], 1)
            self.core().start()

        def s1(self):
            self.core().wait_recv()
            self.add(0, 640, [th.at[self.k]])
            if self.layer == 1:
                pl.semaphore_signal(free_th.at[self.k], inc=1, device_id=core, device_id_type=MESH)
            else:
                pl.semaphore_wait(free_r1.at[self.k], 2)
            for b in range(2):
                for hf in range(2):
                    self.first(b, hf).start()
            self.to_homes(lambda d: [self.a_over_y(d)])

        def s2(self):
            self.total(1, 256).wait_recv()
            for b in range(2):
                for hf in range(2):
                    self.add(
                        320 * hf + half_at[b], 64, [r1.at[self.k, pl.ds(128 * b + 64 * hf, 64)]]
                    )
            if self.layer == 1:
                for peer in (to_xa, to_xb):
                    pl.semaphore_signal(
                        free_r1.at[self.k], inc=1, device_id=peer, device_id_type=MESH
                    )
            else:
                pl.semaphore_wait(free_r2.at[self.k], 2)
            for b in range(2):
                for hf in range(2):
                    self.second(b, hf).start()

        def s3(self):
            self.total(2, 128).wait_recv()
            for b in range(2):
                for hf in range(2):
                    self.add(
                        320 * hf + quarter_at[b], 32, [r2.at[self.k, pl.ds(64 * b + 32 * hf, 32)]]
                    )
            if self.layer == 1:
                for peer in (to_xa, to_xb):
                    pl.semaphore_signal(
                        free_r2.at[self.k], inc=1, device_id=peer, device_id_type=MESH
                    )
            self.to_homes(lambda d: [self.b_over_y(d, b) for b in range(2)])

            @pl.when(self.home)
            def _():
                self.total(3, 192).wait_recv()
                self.add(320 * yh, 64, [ra1.at[self.k, i] for i in range(3)])
                for d in (2, 1, 3):
                    self.a_over_x(d).start()

        def s4(self):
            @pl.when(self.home)
            def _():
                self.total(5, 192).wait_recv()
                for b in range(2):
                    at = 320 * yh + quarter_at[b]
                    self.add(at, 32, [rb3.at[self.k, i, pl.ds(32 * b, 32)] for i in range(3)])
                    self.keep(at, 32).start()
                    self.b_back_y(b).start()
                self.total(4, 48).wait_recv()
                at = 320 * yh + 16 * x
                self.add(at, 16, [ra2.at[self.k, i] for i in range(3)])
                self.keep(at, 16).start()
                for d in (2, 1, 3):
                    self.a_back_x(d).start()

        def s5(self):
            @pl.when(self.home)
            def _():
                self.keep(0, 80).wait()
                self.total(7, 64).wait_recv()
                for b in range(2):
                    for hf in range(2):
                        self.back_second(b, hf).start()
                self.total(6, 48).wait_recv()
                self.a_back_y().start()

        def s6(self):
            @pl.when(self.home)
            def _():
                self.total(8, 128).wait_recv()
                for b in range(2):
                    for hf in range(2):
                        self.back_first(b, hf).start()
                for b in range(2):
                    for hf in range(2):
                        self.back_core(320 * hf + half_at[b], 64).start()

        def s7(self):
            @pl.when(self.home)
            def _():
                self.a_back_y().wait_recv()
                for hf in range(2):
                    self.back_core(320 * hf, 64).start()
                self.total(9, 256).wait_recv()
                for b in range(2):
                    for hf in range(2):
                        self.back_core(320 * hf + half_off[b], 64).start()

        def sent(self, n):
            ref = wb.at[0, pl.ds(0, n)]
            return remote(ref, ref, e_s.at[self.layer, self.k], e_r.at[self.layer, self.k, 0], core)

        def drain(self):
            @pl.when(self.home)
            def _():
                self.back_core(0).wait_recv()
                self.sent(1760 + 640).wait_send()

            @pl.when(jnp.logical_not(self.home))
            def _():
                self.sent(1280).wait_send()

    groups = {(layer, k): Group(layer, k) for layer in range(2) for k in range(3)}
    att1, up1, down1 = (groups[1, k] for k in range(3))
    att0, up0, down0 = (groups[0, k] for k in range(3))

    def put(layer, at, value):
        if layer == 1:
            gv[at, :] = value.astype(bf16)
        else:
            wb[1, at, :] = value.astype(bf16)

    def grad_tiles(layer, k, left, right):
        for i in range(D // TILE):
            put(layer, pl.ds(k * 1280 + i * TILE, TILE), tm(left[:, cols_of(i)], right[...]))
        groups[layer, k].s0()

    def t_move(i, src, dst, peer):
        return remote(src, dst, t_s.at[i], t_r.at[i], peer)

    def t_rows(sec, at, n):
        return gt.at[sec, pl.ds(pl.multiple_of(at, 16), n)]

    def t_result(at, n):
        return go_ref.at[pl.ds(pl.multiple_of(LAYER_ROWS + at, 16), n)]

    def t_core(sec):
        return t_move(0, t_rows(sec, 128 * (1 - c), 128), tt.at[sec], core)

    def t_over_x(d, sec):
        src = t_rows(sec, 128 * c + 32 * x_at[d], 32)
        return t_move(1, src, tx.at[d - 1, sec], x_peer[d])

    def t_over_y(d):
        src = t_rows(lax.rem(y_at[d], 2), 128 * c + 32 * x + 16 * lax.div(y_at[d], 2), 16)
        return t_move(2, src, ty.at[d - 1], y_peer[d])

    t_own = 128 * c + 32 * x + 16 * yh

    def t_back_y():
        return t_move(3, t_rows(s, t_own, 16), t_result(t_own, 16), y_peer[2])

    def t_keep():
        return pltpu.make_async_copy(t_rows(s, t_own, 16), t_result(t_own, 16), t_l)

    def t_back_x(d):
        ref = t_result(128 * c + 32 * x, 32)
        return t_move(4, ref, ref, x_peer[d])

    def t_back_core():
        ref = t_result(128 * c, 128)
        return t_move(5, ref, ref, core)

    def t_total(i, n):
        ref = gt.at[0, pl.ds(0, n)]
        return t_move(i, ref, ref, core)

    def t_add(sec, at, n, sources):
        here = pl.ds(pl.multiple_of(at, 16), n)
        total = gt[sec, here, :].astype(f32)
        for source in sources:
            total = total + source[...].astype(f32)
        gt[sec, here, :] = total.astype(bf16)

    def t1():
        t_total(0, 256).wait_recv()
        for sec in range(2):
            for i in range(4):
                t_add(sec, 128 * c + 32 * i, 32, [tt.at[sec, pl.ds(32 * i, 32)]])
            for d in (2, 1, 3):
                t_over_x(d, sec).start()

    def t2():
        t_total(1, 192).wait_recv()
        for sec in range(2):
            t_add(sec, 128 * c + 32 * x, 32, [tx.at[i, sec] for i in range(3)])
        for d in (2, 1, 3):
            t_over_y(d).start()

    def t3():
        t_total(2, 48).wait_recv()
        t_add(s, t_own, 16, [ty.at[i] for i in range(3)])
        t_keep().start()
        t_back_y().start()

    def t4():
        t_keep().wait()
        t_back_y().wait_recv()
        for d in (2, 1, 3):
            t_back_x(d).start()

    def t5():
        t_total(4, 96).wait_recv()
        t_back_core().start()

    weights(1, [("core", i) for i in range(8, 12)])
    cot_copy.wait()
    grad_tiles(1, 2, hb, gb.at[0])
    gg[...] = jnp.zeros_like(gg)

    for layer in (1, 0):
        st = 5 if layer == 1 else 7
        for h in range(HALVES):
            at = rows_of(h)
            if layer == 0:
                ag_wait(5, h, gb.at[1])

            def d_up_tile(j, carry):
                cols = cols_of(j)
                rows = pl.ds(2560 + j * TILE, TILE)
                d_hidden = mm_t(gb[1 - layer, at, :], wb[layer, rows, :])
                up = upb[layer, at, cols]
                t = jnp.tanh(GELU_A * (up + GELU_B * up * up * up))
                slope = 0.5 * (1.0 + t) + 0.5 * up * (1.0 - t * t) * (
                    GELU_A * (1.0 + 3.0 * GELU_B * up * up)
                )
                du[at, cols] = (d_hidden * slope).astype(bf16)
                if layer == 0:
                    hb[at, cols] = (0.5 * up * (1.0 + t)).astype(bf16)

            unrolled(D // TILE, d_up_tile)
            if layer == 0 and h == 1:
                up1.s2()
            if layer == 1 and h == 1:
                down1.s1()
            rs_send(
                st, h,
                lambda j, cols: mm_t(
                    du[at, :], wb[layer, pl.ds(1280 + j * TILE, TILE), :]
                ),
            )
        if layer == 0:
            w_sent(4, x_s, x_r).wait_send()
            w_sent(2, f_s, f_r).wait_send()
        if layer == 0:
            grad_tiles(0, 2, hb, gb.at[1])
        for h in range(HALVES):
            dn = rs_take(st, h)
            dx, gain = norm_back(dn, mid[layer, own(h), :], gn[layer, 1:2, :])
            dm = gb[1 - layer, chunk(h, z), :].astype(f32) + dx
            dmid[own(h), :] = dm
            gg[2 * layer + 1 : 2 * layer + 2, :] += gain
            if layer == 0:
                ag_total(4, h).wait_send()
            ag_send(st - 1, h, mb, dm)
        grad_tiles(layer, 1, nm.at[layer], du)
        if layer == 1:
            for j in range(D // TILE):
                pd[:, cols_of(j)] = mm(hb[...], wb[1, 2560:3840, cols_of(j)]).astype(bf16)
            down1.s2()
        else:
            down0.s1()
        for h in range(HALVES):
            ag_wait(st - 1, h, mb)
            attention_back(layer, h)
            if h == 1 and layer == 1:
                up1.s1()
            if h == 1 and layer == 0:
                up0.s1()
                up1.s3()
                att1.s2()
            at = rows_of(h)
            rs_send(
                st + 1, h,
                lambda j, cols: mm(dqb[0, at, :], wb[layer, 0:ATT, cols])
                + mm(dqb[1, at, :], wb[layer, ATT : 2 * ATT, cols])
                + mm(dqb[2, at, :], wb[layer, 2 * ATT : 3 * ATT, cols]),
            )
        for i in range(3):
            put(layer, pl.ds(i * ATT, ATT), tm(dqb[i], nb[layer]))
        put(layer, pl.ds(960, 320), tm(ct[layer], mb[...]))
        groups[layer, 0].s0()
        if layer == 1:
            down1.s3()
        else:
            down0.s2()
        for h in range(HALVES):
            dn = rs_take(st + 1, h)
            dx, gain = norm_back(dn, sx[layer, own(h), :], gn[layer, 0:1, :])
            gg[2 * layer : 2 * layer + 1, :] += gain
            ag_send(st, h, gb.at[layer], dmid[own(h), :] + dx)
        if layer == 1:
            att1.s1()
        else:
            att0.s1()
            up0.s2()
            down1.s4()

    def gg_copy(d):
        return remote(gg, ggr.at[d - 1], gg_s, gg_r, z_peer[d])

    for d in (1, 2, 3):
        gg_copy(d).start()

    for h in range(HALVES):
        ag_wait(7, h, gb.at[0])
        rs_send(4, h, None)
        at = rows_of(h)
        low = gb[0, at, :]
        before = pre[at, :]
        sig = jax.nn.sigmoid(before)
        d_pre = (
            mm_t(low, w_hid_ref[...]) * (sig * (1.0 + before * (1.0 - sig)))
        ).astype(bf16)
        dctx[at, :] = d_pre
        points = mm_t(d_pre, w_in_ref[...])
        points = points + jnp.where(z == 0, mm_t(low, w_res_ref[...]), 0.0)
        keep = 1.0 - patch_ref[at, :].astype(f32)
        gpad[at, 0:PATCH] = points[:, 0:PATCH] * keep[:, PATCH : 2 * PATCH]
    down0.s3()
    points = gpad[:, 0:64]
    high = points.astype(bf16)
    low = (points - high.astype(f32)).astype(bf16)
    row = lax.broadcasted_iota(jnp.int32, (ROWS, ROWS), 0)
    col = lax.broadcasted_iota(jnp.int32, (ROWS, ROWS), 1)
    swap = jnp.where(
        ((row >> 4) == (col & 15)) & ((row & 15) == (col >> 4)), 1.0, 0.0
    ).astype(bf16)
    points = mm(swap, high) + mm(swap, low)
    for k in range(8):
        dps[k, :, 0:64] = points[k * 32 : (k + 1) * 32]
        dps[k, :, 64:128] = jnp.zeros((32, 64), f32)
    me = s * 4 + z

    def dp_copy(d):
        to = lax.rem(me + d, 8)
        return remote(
            dps.at[to], dpr.at[me], dp_s, dp_r,
            (lax.div(to, 4), dp, lax.rem(to, 4)),
        )

    for d in range(1, 8):
        dp_copy(d).start()
    dpr[me] = dps[me]

    grad_low = gb[0]
    hid = tm(tokh[...], grad_low).astype(bf16)
    res = tm(patch_ref[...], grad_low).astype(bf16)
    inn = tm(patch_ref[...], dctx[...]).astype(bf16)
    for sec in range(2):
        lanes = slice(sec * 640, sec * 640 + 640)
        gt[sec, 0:160, 0:640] = hid[0:160, lanes]
        gt[sec, 0:160, 640:1280] = hid[160:320, lanes]
        gt[sec, 160:192, 0:640] = res[0:32, lanes]
        gt[sec, 160:192, 640:1280] = res[32:64, lanes]
        gt[sec, 192:224, :] = jnp.zeros((32, D), bf16)
        gt[sec, 192:224, 0:320] = inn[sec * 32 : sec * 32 + 32]
    total = gg[...]
    remote(ggr, ggr, gg_s, gg_r, core).wait_recv()
    for d in (1, 2, 3):
        total = total + ggr[d - 1]
    for sec in range(2):
        gt[sec, 224:256, :] = jnp.concatenate(
            [total[2 * sec : 2 * sec + 2], jnp.zeros((30, D), f32)], axis=0
        ).astype(bf16)

    for sec in range(2):
        t_core(sec).start()
    up0.s3()
    att1.s3()
    att0.s2()
    t1()
    down0.s4()
    att0.s3()
    t2()
    up0.s4()
    up1.s4()
    down0.s5()
    down1.s5()
    for h in range(HALVES):
        mlp_out(1, h)
        own_out(h)
    att0.s4()
    att1.s4()
    t3()
    up0.s5()
    up1.s5()
    down0.s6()
    down1.s6()
    att0.s5()
    att1.s5()
    t4()
    up0.s6()
    up1.s6()
    for h in range(HALVES):
        pass_out(h)
    down0.s7()
    down1.s7()
    att0.s6()
    att1.s6()
    up0.s7()
    up1.s7()
    t5()
    att0.s7()
    att1.s7()
    seven = dps.at[pl.ds(0, 7)]
    remote(seven, seven, dp_s, dp_r, core).wait_recv()
    for sec in range(2):
        points_ref[sec] = dpr[4 * sec] + dpr[4 * sec + 1] + dpr[4 * sec + 2] + dpr[4 * sec + 3]

    w_sent(4, w_s, w_r).wait_send()
    for group in groups.values():
        group.drain()
    for i, n in ((0, 256), (1, 192), (2, 48), (3, 16), (4, 96)):
        t_total(i, n).wait_send()
    t_back_core().wait()
    gn_send.wait_send()
    for h in range(HALVES):
        rs_total(7, h).wait_send()
        rs_total(4, h).wait_send()
        for st in (0, 1, 2, 3, 5, 6, 7):
            ag_total(st, h).wait_send()
        lo_cross(h).wait_send()
        lo_keep(h).wait()
        for i in (1, 2):
            lo_total(i, h).wait()
    remote(ggr, ggr, gg_s, gg_r, core).wait_send()
    remote(seven, seven, dp_s, dp_r, core).wait_send()


def run_layers(series, missing, w_in, w_hid, w_res, gain_a, gain_m, wq, wo, wu, wd, cotangent):
    cos, sin, turn = rotary_arrays()
    vm = pl.BlockSpec(memory_space=pltpu.VMEM)
    hbm = pl.BlockSpec(memory_space=pl.ANY)
    dma = pltpu.SemaphoreType.DMA
    scratch = [
        pltpu.VMEM((2 * PATCH, ATT), bf16),
        pltpu.VMEM((ATT, D), bf16),
        pltpu.VMEM((2 * PATCH, D), bf16),
        pltpu.VMEM((BLOCK, ATT), f32),
        pltpu.VMEM((BLOCK, ATT), f32),
        pltpu.VMEM((ATT, ATT), bf16),
        dma((6,)),
        pltpu.VMEM((ROWS, 2 * PATCH), bf16),
        pltpu.VMEM((2, LAYER_ROWS, D), bf16),
        pltpu.VMEM((2, 2, D), f32),
        pltpu.VMEM((ROWS, ATT), bf16),
        pltpu.VMEM((ROWS, ATT), f32),
        pltpu.VMEM((2, ROWS // 4, D), f32),
        pltpu.VMEM((2, ROWS // 4, D), f32),
        pltpu.VMEM((2, ROWS, D), bf16),
        pltpu.VMEM((2, ROWS, D), bf16),
        pltpu.VMEM((2, 3, ROWS, ATT), bf16),
        pltpu.VMEM((2, ROWS // BLOCK, HEADS_HERE * BLOCK, BLOCK), f32),
        pltpu.VMEM((2, ROWS, ATT), bf16),
        pltpu.VMEM((2, ROWS, D), f32),
        pltpu.VMEM((ROWS, D), bf16),
        pltpu.VMEM((2, ROWS, D), bf16),
        pltpu.VMEM((ROWS, D), bf16),
        pltpu.VMEM((ROWS, D), bf16),
        pltpu.VMEM((3, ROWS, ATT), bf16),
        pltpu.VMEM((ROWS, ATT), bf16),
        pltpu.VMEM((LAYER_ROWS, D), bf16),
        pltpu.VMEM((2, PACK_ROWS - LAYER_ROWS, D), bf16),
        pltpu.VMEM((2, ROWS, D), bf16),
        pltpu.VMEM((2, 3, ROWS // 4, D), bf16),
        pltpu.VMEM((ROWS // 4, D), f32),
        pltpu.VMEM((2, ROWS // 4, D), bf16),
        pltpu.VMEM((8, D), f32),
        pltpu.VMEM((3, 8, D), f32),
        pltpu.VMEM((8, 32, 128), f32),
        pltpu.VMEM((8, 32, 128), f32),
        pltpu.VMEM((ROWS, 128), f32),
        pltpu.VMEM((3, 640, D), bf16),
        pltpu.VMEM((3, 256, D), bf16),
        pltpu.VMEM((3, 128, D), bf16),
        pltpu.VMEM((3, 3, 64, D), bf16),
        pltpu.VMEM((3, 3, 16, D), bf16),
        pltpu.VMEM((3, 3, 64, D), bf16),
        pltpu.VMEM((2, 128, D), bf16),
        pltpu.VMEM((3, 2, 32, D), bf16),
        pltpu.VMEM((3, 16, D), bf16),
        pltpu.VMEM((ROWS, D), bf16),
        dma, *[dma, dma((N_PIECES,))] * 3,
        dma, dma, dma,
        dma((9, HALVES)), dma((9, HALVES)),
        dma((8, HALVES)), dma((8, HALVES)),
        dma((HALVES,)), dma((3, HALVES)), dma((3, HALVES)),
        dma, dma, dma, dma,
        dma((2, 3)), dma((2, 3, 12)), dma((2, 3)),
        dma((6,)), dma((6,)), dma,
        *[pltpu.SemaphoreType.REGULAR((3,))] * 3,
    ]
    return pl.pallas_call(
        layers_kernel,
        out_shape=(
            jax.ShapeDtypeStruct((2 * ROWS, D), bf16),
            jax.ShapeDtypeStruct((PACK_ROWS, D), bf16),
            jax.ShapeDtypeStruct((2, 32, 128), f32),
        ),
        in_specs=[vm] * 2 + [hbm] * 3 + [vm] * 2 + [hbm] * 8,
        out_specs=(hbm, hbm, vm),
        scratch_shapes=scratch,
        compiler_params=pltpu.CompilerParams(
            collective_id=0, has_side_effects=True, vmem_limit_bytes=62 * 2**20
        ),
        cost_estimate=pl.CostEstimate(
            flops=15_000_000_000, bytes_accessed=50_000_000, transcendentals=4_000_000
        ),
        name="layers",
    )(
        series, missing, w_in, w_hid, w_res, gain_a, gain_m, wq, wo, wu, wd, cotangent,
        jnp.asarray(cos, f32), jnp.asarray(sin, f32), jnp.asarray(turn, bf16),
    )


STEP = 320
STEPS = LAYER_ROWS // STEP


def widen_kernel(
    total_ref, lo_ref, points_ref,
    qkv, out, up, down, hid, res, inn, gain_a, gain_m, series_grad, lo_out,
    low, wide, small, kept, in_sem, out_sem, small_sem, lo_sem,
):
    places_of = [(qkv, i) for i in range(3)] + [(out, 0)]
    places_of += [(up, i) for i in range(4)] + [(down, i) for i in range(4)]

    def rows(i):
        return pl.ds(i * STEP, STEP)

    def load(i):
        return pltpu.make_async_copy(total_ref.at[rows(i)], low.at[rows(i)], in_sem.at[i])

    def store(i):
        ref, k = places_of[i]
        return pltpu.make_async_copy(wide.at[rows(i)], ref.at[rows(k)], out_sem.at[i])

    load_small = pltpu.make_async_copy(
        total_ref.at[pl.ds(LAYER_ROWS, PACK_ROWS - LAYER_ROWS)], small, small_sem
    )
    load_lo = pltpu.make_async_copy(lo_ref, kept, lo_sem)
    store_lo = pltpu.make_async_copy(kept, lo_out, lo_sem)
    for i in range(STEPS):
        load(i).start()
    load_small.start()
    load_lo.start()
    for i in range(STEPS):
        load(i).wait()

        def body(j, carry, i=i):
            at = pl.ds(pl.multiple_of(i * STEP + j * 32, 32), 32)
            wide[at, :] = low[at, :].astype(f32)
            return carry

        lax.fori_loop(0, STEP // 32, body, 0, unroll=2)
        store(i).start()
    load_lo.wait()
    store_lo.start()
    load_small.wait()
    values = small[...].astype(f32)
    hid[0:160, :] = values[0:160, 0:640]
    hid[160:320, :] = values[0:160, 640:1280]
    res[0:32, :] = values[160:192, 0:640]
    res[32:64, :] = values[160:192, 640:1280]
    inn[...] = values[192:224, 0:320]
    gain_a[...] = values[224:225]
    gain_m[...] = values[225:226]
    for sec in range(2):
        for j in range(2):
            series_grad[16 * sec : 16 * sec + 16, 32 * j : 32 * j + 32] = points_ref[
                sec, 16 * j : 16 * j + 16, 0:32
            ]
    for i in range(STEPS):
        store(i).wait()
    store_lo.wait()


def widen(total, layer_out, points):
    shapes = ((960, D), (320, D), (1280, D), (1280, D), (320, 640), (64, 640), (32, 320), (1, D), (1, D), (32, 64))
    hbm = pl.BlockSpec(memory_space=pl.ANY)
    vm = pl.BlockSpec(memory_space=pltpu.VMEM)
    dma = pltpu.SemaphoreType.DMA
    return pl.pallas_call(
        widen_kernel,
        out_shape=[jax.ShapeDtypeStruct(shape, f32) for shape in shapes]
        + [jax.ShapeDtypeStruct((2 * ROWS, D), bf16)],
        in_specs=[hbm, hbm, vm],
        out_specs=[hbm] * 4 + [vm] * 6 + [hbm],
        scratch_shapes=[
            pltpu.VMEM((LAYER_ROWS, D), bf16),
            pltpu.VMEM((LAYER_ROWS, D), f32),
            pltpu.VMEM((PACK_ROWS - LAYER_ROWS, D), bf16),
            pltpu.VMEM((2 * ROWS, D), bf16),
            dma((STEPS,)), dma((STEPS,)), dma, dma,
        ],
        compiler_params=pltpu.CompilerParams(vmem_limit_bytes=60 * 2**20),
        cost_estimate=pl.CostEstimate(flops=0, bytes_accessed=32_000_000, transcendentals=0),
        name="widen",
    )(total, layer_out, points)


def per_device(
    series, missing, w_in, w_hid, w_res, gain_attn, w_qkv, w_out, gain_mlp, w_up, w_down, cotangent
):
    wq = jnp.transpose(w_qkv[0], (1, 2, 0)).reshape(3 * ATT, D)
    layer_out, total, points = run_layers(
        series, missing, w_in, w_hid, w_res, gain_attn, gain_mlp, wq, w_out[0], w_up[0], w_down[0],
        cotangent,
    )
    g_qkv, g_out, g_up, g_down, g_hid, g_res, g_in, gain_a, gain_m, series_grad, layer_out = widen(
        total, layer_out, points
    )
    g_qkv = jnp.transpose(g_qkv.reshape(3, ATT, D), (2, 0, 1))
    return (
        layer_out[None],
        series_grad,
        g_in,
        g_hid,
        g_res,
        gain_a,
        g_qkv[None],
        g_out[None],
        gain_m,
        g_up[None],
        g_down[None],
    )


def solution(mesh):
    in_specs = (
        P("dp", None),
        P("dp", None),
        P(None, "tensor"),
        P("tensor", None),
        P(),
        P("section", None),
        P("section", None, None, "tensor"),
        P("section", "tensor", None),
        P("section", None),
        P("section", None, "tensor"),
        P("section", "tensor", None),
        P("dp", None),
    )
    out_specs = (
        P("section", "dp", None),
        P("dp", ("section", "tensor")),
        P("section", "tensor"),
        P("tensor", "section"),
        P(None, "section"),
        P("section", None),
        P("section", None, None, "tensor"),
        P("section", "tensor", None),
        P("section", None),
        P("section", None, "tensor"),
        P("section", "tensor", None),
    )
    return jax.shard_map(
        per_device, mesh=mesh, in_specs=in_specs, out_specs=out_specs, check_vma=False
    )
```

```python
import math

import jax
import jax.numpy as jnp
import numpy as np
from jax import lax
from jax.experimental import pallas as pl
from jax.experimental.pallas import tpu as pltpu
from jax.sharding import PartitionSpec as P

D = 1280
HEADS_HERE = 4
HEAD_DIM = 80
ATT = HEADS_HERE * HEAD_DIM
PATCH = 32
PATCHES = 16
ROWS = 256
HALVES = 2
RH = ROWS // HALVES
RQ = RH // 4
TILE = 256
BLOCK = 128
MATS = ((0, 960), (960, 320), (1280, 1280), (2560, 1280))
PIECES = tuple((320 * i, 320, 0 if i < 3 else 1 if i < 4 else 2 if i < 8 else 3) for i in range(12))
N_PIECES = len(PIECES)
LAYER_ROWS = 3840
PACK_ROWS = 4096
RS_BEFORE = {2: 0, 3: 1, 5: 3, 6: 2, 7: 5, 8: 6, 4: 8}
MESH = pl.DeviceIdType.MESH
f32 = jnp.float32
bf16 = jnp.bfloat16
eps_norm = 1e-06
masked_score = -1e30
GELU_A = math.sqrt(2.0 / math.pi)
GELU_B = 0.044715


def mm(a, b):
    return lax.dot_general(a, b, (((1,), (0,)), ((), ())), preferred_element_type=f32)


def mm_t(a, b):
    return lax.dot_general(a, b, (((1,), (1,)), ((), ())), preferred_element_type=f32)


def tm(a, b):
    return lax.dot_general(a, b, (((0,), (0,)), ((), ())), preferred_element_type=f32)


def unrolled(count, body):
    for j in range(count):
        body(j, 0)


def rotary_arrays():
    half = HEAD_DIM // 2
    position = (np.arange(BLOCK) % PATCHES).astype(np.float32)
    frequency = np.exp(
        np.arange(half, dtype=np.float32) * np.float32(-2.0 * math.log(10000.0) / HEAD_DIM)
    )
    angles = position[:, None] * frequency[None, :]
    lane = np.arange(ATT) % half
    turn = np.zeros((ATT, ATT), np.float32)
    for j in range(ATT):
        if j % HEAD_DIM < half:
            turn[j + half, j] = -1.0
        else:
            turn[j - half, j] = 1.0
    return np.cos(angles)[:, lane], np.sin(angles)[:, lane], turn


def places():
    s = lax.axis_index("section")
    dp = lax.axis_index("dp")
    z = lax.axis_index("tensor")
    c = lax.rem(dp, 2)
    yh = lax.rem(lax.div(dp, 2), 2)
    x = lax.div(dp, 4)
    return s, dp, z, x, yh, c


def layers_kernel(
    series_ref, missing_ref, w_in_in, w_hid_in, w_res_in, gain_a_ref, gain_m_ref, wq_ref, wo_ref, wu_ref, wd_ref,
    cot_ref, cos_in, sin_in, turn_in,
    lo_ref, go_ref, points_ref,
    w_in_ref, w_hid_ref, w_res_ref, cos_ref, sin_ref, turn_ref, in_l,
    patch_ref, wb, gn, tokh, pre, sx, mid, nb, nm, qb, pb, ct, upb, hb, gb, mb, du, dqb, dctx, gv, gt,
    sb, rb, dmid, ob, gg, ggr, dps, dpr, gpad,
    th, r1, r2, ra1, ra2, rb3, tt, tx, ty, pd,
    w_loc, w_s, w_r, x_s, x_r, f_s, f_r, gn_s, gn_r, cot_l,
    rs_s, rs_r, ag_s, ag_r, lo_l, lo_s, lo_r, gg_s, gg_r, dp_s, dp_r,
    e_s, e_r, e_l, t_s, t_r, t_l, free_th, free_r1, free_r2,
):
    s, dp, z, x, yh, c = places()
    other = 1 - s
    z_peer = [None] + [(s, dp, lax.rem(z + d, 4)) for d in (1, 2, 3)]
    z_at = [z] + [lax.rem(z + d, 4) for d in (1, 2, 3)]
    y_a = (other, dp, z)
    y_b = (other, dp + 2 - 4 * yh, z)
    core = (s, dp + 1 - 2 * c, z)
    across = [(other, dp, z_at[d]) for d in range(4)]
    y = 2 * yh + s
    x_at = [x] + [lax.rem(x + d, 4) for d in (1, 2, 3)]
    y_at = [y] + [lax.rem(y + d, 4) for d in (1, 2, 3)]
    x_peer = [None] + [(s, x_at[d] * 4 + 2 * yh + c, z) for d in (1, 2, 3)]
    y_peer = [None] + [
        (lax.rem(y_at[d], 2), x * 4 + 2 * lax.div(y_at[d], 2) + c, z) for d in (1, 2, 3)
    ]
    x_up, x_down = x_peer[1], x_peer[3]
    w_refs = (wq_ref, wo_ref, wu_ref, wd_ref)

    small_inputs = [
        pltpu.make_async_copy(src, dst, in_l.at[i])
        for i, (src, dst) in enumerate((
            (w_in_in, w_in_ref), (w_hid_in, w_hid_ref), (w_res_in, w_res_ref),
            (cos_in, cos_ref), (sin_in, sin_ref), (turn_in, turn_ref),
        ))
    ]
    for copy in small_inputs:
        copy.start()
    barrier = pltpu.get_barrier_semaphore()
    peers = z_peer[1:] + across + [y_b, core] + x_peer[1:] + [y_peer[2]]
    for peer in peers:
        pl.semaphore_signal(barrier, inc=1, device_id=peer, device_id_type=MESH)
    pl.semaphore_wait(barrier, len(peers))

    def remote(src, dst, ssem, rsem, peer):
        return pltpu.make_async_remote_copy(
            src_ref=src, dst_ref=dst, send_sem=ssem, recv_sem=rsem,
            device_id=peer, device_id_type=MESH,
        )

    odd = lax.rem(x, 2)

    def w_local(m):
        off, n = MATS[m]
        return pltpu.make_async_copy(w_refs[m], wb.at[s, pl.ds(off, n)], w_loc)

    def share(i, parity, k):
        off, n, m = PIECES[i]
        first = (n // 4 + 31) // 32 * 16 if i % 2 == 0 else n // 4 // 32 * 16
        size = first if k == 0 else n // 4 - first
        return (2 * c + parity) * (n // 4) + k * first, size

    def w_over_y(i, k):
        off, n, m = PIECES[i]
        at, size = share(i, odd, k)
        src = w_refs[m].at[pl.ds(pl.multiple_of(off - MATS[m][0] + at, 16), size)]
        dst = wb.at[s, pl.ds(pl.multiple_of(off + at, 16), size)]
        return remote(src, dst, w_s, w_r.at[i], (y_a, y_b)[k])

    def w_over_x(i, k, parity):
        at, size = share(i, parity, k)
        ref = wb.at[other, pl.ds(pl.multiple_of(PIECES[i][0] + at, 16), size)]
        return remote(ref, ref, x_s, x_r.at[i], (x_up, x_down)[k])

    def w_to_core(i, q):
        off, n, m = PIECES[i]
        parity = odd if q == 0 else 1 - odd
        ref = wb.at[other, pl.ds(pl.multiple_of(off + (2 * c + parity) * (n // 4), 16), n // 4)]
        return remote(ref, ref, f_s, f_r.at[i], core)

    def w_total(i, part, ssem, rsem):
        ref = wb.at[0, pl.ds(0, PIECES[i][1] // part)]
        return remote(ref, ref, ssem, rsem.at[i], core)

    def w_sent(part, ssem, rsem):
        ref = wb.at[0, pl.ds(0, LAYER_ROWS // part)]
        return remote(ref, ref, ssem, rsem.at[0], core)

    def weights(layer, steps):
        @pl.when(s != layer)
        def _():
            for step, i in steps:
                if step == "y":
                    w_total(i, 4, w_s, w_r).wait_recv()
                    for k in range(2):
                        w_over_x(i, k, odd).start()
                    w_to_core(i, 0).start()
                elif step == "x":
                    w_total(i, 4, x_s, x_r).wait_recv()
                    w_to_core(i, 1).start()
                else:
                    w_total(i, 2, f_s, f_r).wait_recv()

    gains = gn.at[s]
    gains[0:1, :] = gain_a_ref[...]
    gains[1:2, :] = gain_m_ref[...]
    gn_send = remote(gn.at[s], gn.at[s], gn_s, gn_r, y_a)
    cot_copy = pltpu.make_async_copy(
        cot_ref.at[pl.ds(pl.multiple_of(s * ROWS, ROWS), ROWS)], gb.at[0], cot_l
    )
    gn_send.start()
    def start_weights(first, last):
        for i in range(first, last):
            for k in range(2):
                w_over_y(i, k).start()

    start_weights(0, 4)
    for m in range(4):
        w_local(m).start()
    cot_copy.start()

    def rows_of(h):
        return pl.ds(h * RH, RH)

    def chunk(h, zz):
        return pl.ds(pl.multiple_of(h * RH + zz * RQ, RQ), RQ)

    def cols_of(j):
        return pl.ds(j * TILE, TILE)

    def rs_copy(st, h, d, cols=None):
        src = sb.at[st % 2, chunk(h, z_at[d])]
        dst = rb.at[st % 2, d - 1, pl.ds(h * RQ, RQ)]
        if cols is not None:
            src = sb.at[st % 2, chunk(h, z_at[d]), cols]
            dst = rb.at[st % 2, d - 1, pl.ds(h * RQ, RQ), cols]
        return remote(src, dst, rs_s.at[st, h], rs_r.at[st, h], z_peer[d])

    def rs_total(st, h):
        ref = rb.at[st % 2, pl.ds(0, 3), pl.ds(h * RQ, RQ)]
        return remote(ref, ref, rs_s.at[st, h], rs_r.at[st, h], core)

    def rs_send(st, h, produce):
        if st in RS_BEFORE:
            rs_total(RS_BEFORE[st], h).wait_send()

        if produce is None:
            sb[st % 2, rows_of(h), :] = pd[rows_of(h), :]
            for d in (2, 1, 3):
                rs_copy(st, h, d).start()
            return

        def body(j, carry):
            cols = cols_of(j)
            sb[st % 2, rows_of(h), cols] = produce(j, cols).astype(bf16)
            if j in (2, 4):
                part = pl.ds(0, 768) if j == 2 else pl.ds(768, 512)
                for d in (2, 1, 3):
                    rs_copy(st, h, d, part).start()

        unrolled(D // TILE, body)

    def rs_take(st, h):
        total = sb[st % 2, chunk(h, z), :].astype(f32)
        rs_total(st, h).wait_recv()
        for d in (1, 2, 3):
            total = total + rb[st % 2, d - 1, pl.ds(h * RQ, RQ), :].astype(f32)
        return total

    def ag_copy(st, h, d, dst):
        at = dst.at[chunk(h, z)]
        return remote(at, at, ag_s.at[st, h], ag_r.at[st, h], z_peer[d])

    def ag_send(st, h, dst, value):
        dst[chunk(h, z), :] = value.astype(bf16)
        for d in (2, 1, 3):
            ag_copy(st, h, d, dst).start()

    def ag_total(st, h):
        ref = pd.at[pl.ds(0, 3 * RQ)]
        return remote(ref, ref, ag_s.at[st, h], ag_r.at[st, h], core)

    def ag_wait(st, h, dst):
        ag_total(st, h).wait_recv()

    def own(h):
        return pl.ds(h * RQ, RQ)

    def scale_of(v):
        return lax.rsqrt(jnp.mean(v * v, axis=-1, keepdims=True) + eps_norm)

    def norm(v, g):
        return v * scale_of(v) * g

    def norm_back(dn, v, g):
        r = scale_of(v)
        weighted = g * dn
        inner = jnp.mean(v * weighted, axis=-1, keepdims=True)
        return r * weighted - v * (r * r * r * inner), jnp.sum(dn * v * r, axis=0, keepdims=True)

    head_lane = lax.broadcasted_iota(jnp.int32, (1, ATT), 1)
    head_mask = [
        (head_lane >= HEAD_DIM * h) & (head_lane < HEAD_DIM * (h + 1)) for h in range(HEADS_HERE)
    ]

    def spread(v):
        wide = v.astype(f32)
        return jnp.concatenate(
            [jnp.where(m, wide, 0.0) for m in head_mask], axis=0
        ).astype(bf16)

    def gather(v):
        total = jnp.where(head_mask[0], v[:BLOCK], 0.0)
        for h in range(1, HEADS_HERE):
            total = total + jnp.where(head_mask[h], v[h * BLOCK : (h + 1) * BLOCK], 0.0)
        return total

    def turned(v, sign):
        high = v.astype(bf16)
        low = (v - high.astype(f32)).astype(bf16)
        swapped = mm(high, turn_ref[...]) + mm(low, turn_ref[...])
        if sign < 0:
            swapped = -swapped
        return v * cos_ref[...] + swapped * sin_ref[...]

    inv = 1.0 / math.sqrt(HEAD_DIM)

    def blocks_of(h):
        return range(h * RH // BLOCK, (h + 1) * RH // BLOCK)

    def attention_front(layer, h):
        for b in blocks_of(h):
            at = pl.ds(b * BLOCK, BLOCK)
            normed = nb[layer, at, :]
            first = b == 0
            if first:
                weights(layer, [("core", 0)])
            q = turned(mm_t(normed, wb[layer, 0:ATT, :]), 1).astype(bf16)
            if first:
                weights(layer, [("core", 1)])
            k = turned(mm_t(normed, wb[layer, ATT : 2 * ATT, :]), 1).astype(bf16)
            if first:
                weights(layer, [("core", 2)])
            v = mm_t(normed, wb[layer, 2 * ATT : 3 * ATT, :]).astype(bf16)
            qb[layer, 0, at, :] = q
            qb[layer, 1, at, :] = k
            qb[layer, 2, at, :] = v
            scores = mm_t(spread(q), k) * inv
            row = lax.broadcasted_iota(jnp.int32, scores.shape, 0) & (BLOCK - 1)
            col = lax.broadcasted_iota(jnp.int32, scores.shape, 1)
            allowed = (col <= row) & (col >= (row & (BLOCK - PATCHES)))
            scores = jnp.where(allowed, scores, masked_score)
            e = jnp.exp(scores - jnp.max(scores, axis=-1, keepdims=True))
            probs = e / jnp.sum(e, axis=-1, keepdims=True)
            pb[layer, b] = probs
            ct[layer, at, :] = gather(mm(probs.astype(bf16), v)).astype(bf16)

    def attention_back(layer, h):
        for b in blocks_of(h):
            at = pl.ds(b * BLOCK, BLOCK)
            spread_d = spread(mm_t(mb[at, :], wb[layer, 960:1280, :]).astype(bf16))
            spread_q = spread(qb[layer, 0, at, :])
            k = qb[layer, 1, at, :]
            v = qb[layer, 2, at, :]
            probs = pb[layer, b]
            d_probs = mm_t(spread_d, v)
            d_scores = (
                probs * (d_probs - jnp.sum(probs * d_probs, axis=-1, keepdims=True))
            ).astype(bf16)
            d_q = gather(mm(d_scores, k)) * inv
            d_k = tm(d_scores, spread_q) * inv
            dqb[0, at, :] = turned(d_q, -1).astype(bf16)
            dqb[1, at, :] = turned(d_k, -1).astype(bf16)
            dqb[2, at, :] = tm(probs.astype(bf16), spread_d).astype(bf16)

    contexts = pl.ds(pl.multiple_of(s * PATCHES, PATCHES), PATCHES)
    flags = missing_ref[contexts, :].astype(f32)
    values = series_ref[contexts, :] * (1.0 - flags)
    for j in range(PATCHES):
        at = pl.ds(j, PATCHES, stride=PATCHES)
        own_points = slice(j * PATCH, (j + 1) * PATCH)
        gpad[at, :] = jnp.concatenate(
            [values[:, own_points], flags[:, own_points], jnp.zeros((PATCHES, 64), f32)], axis=1
        )
    patch_ref[...] = gpad[:, 0:64].astype(bf16)
    for copy in small_inputs:
        copy.wait()
    for h in range(HALVES):
        at = rows_of(h)
        before = mm(patch_ref[at, :], w_in_ref[...])
        pre[at, :] = before
        tokh[at, :] = (before * jax.nn.sigmoid(before)).astype(bf16)
        rs_send(0, h, lambda j, cols: mm(tokh[at, :], w_hid_ref[:, cols]))
    gn_send.wait_recv()
    pltpu.make_async_copy(wb.at[s], wb.at[s], w_loc).wait()
    for h in range(HALVES):
        start_weights(4 + 2 * h, 6 + 2 * h)
        weights(0, [("y", 0)] if h == 0 else [("y", 1), ("y", 2)])
        stream = rs_take(0, h) + mm(patch_ref[chunk(h, z), :], w_res_ref[...])
        sx[0, own(h), :] = stream
        ag_send(0, h, nb.at[0], norm(stream, gn[0, 0:1, :]))
    start_weights(8, 10)
    weights(0, [("x", 0), ("y", 3), ("x", 1), ("x", 2), ("y", 4)])
    weights(1, [("y", 0), ("y", 1), ("y", 2)])

    def lo_rows(sec, h):
        return lo_ref.at[pl.ds(pl.multiple_of(sec * ROWS + h * RH + z * RQ, RQ), RQ)]

    def lo_keep(h):
        return pltpu.make_async_copy(ob.at[s, own(h)], lo_rows(s, h), lo_l.at[h])

    def lo_cross(h):
        return remote(ob.at[other, own(h)], lo_rows(s, h), lo_s.at[0, h], lo_r.at[0, h], y_a)

    def lo_arrive(h):
        return remote(ob.at[other, own(h)], lo_rows(other, h), lo_s.at[0, h], lo_r.at[0, h], y_a)

    def lo_own(h, d):
        return remote(ob.at[s, own(h)], lo_rows(s, h), lo_s.at[1, h], lo_r.at[1, h], z_peer[d])

    def lo_pass(h, d):
        ref = lo_rows(other, h)
        return remote(ref, ref, lo_s.at[2, h], lo_r.at[2, h], z_peer[d])

    def lo_total(i, h):
        ref = pd.at[pl.ds(0, 3 * RQ)]
        return remote(ref, ref, lo_s.at[i, h], lo_r.at[i, h], core)

    def cross_out(layer, h):
        @pl.when(s != layer)
        def _():
            lo_cross(h).start()

    def own_out(h):
        lo_keep(h).start()
        for d in (2, 1, 3):
            lo_own(h, d).start()

    def pass_out(h):
        lo_arrive(h).wait_recv()
        for d in (2, 1, 3):
            lo_pass(h, d).start()

    def mlp_out(layer, h):
        out = (mid[layer, own(h), :] + rs_take(2 + 2 * layer, h)).astype(bf16)
        ob[layer, own(h), :] = out
        cross_out(layer, h)
        return out

    for layer in range(2):
        for h in range(HALVES):
            ag_wait(2 * layer, h, nb.at[layer])
            attention_front(layer, h)
            if h == 0 and layer == 0:
                start_weights(10, 12)
                weights(0, [("y", 5), ("x", 3), ("x", 4), ("y", 6), ("core", 3)])
                weights(1, [("y", 3), ("y", 4), ("y", 5)])
            if h == 0 and layer == 1:
                weights(1, [("core", 3)])
            if h == 1 and layer == 0:
                weights(0, [("y", 7)])
            at = rows_of(h)
            rs_send(
                1 + 2 * layer, h, lambda j, cols: mm(ct[layer, at, :], wb[layer, 960:1280, cols])
            )
        if layer == 0:
            weights(0, [("y", 8), ("x", 5), ("x", 6)])
            weights(1, [("y", 6), ("x", 0), ("x", 1), ("x", 2), ("x", 3)])
        for h in range(HALVES):
            if layer == 0 and h == 1:
                weights(0, [("y", 9), ("x", 7), ("y", 10), ("y", 11)])
                weights(1, [("y", 7)])
            middle = sx[layer, own(h), :] + rs_take(1 + 2 * layer, h)
            mid[layer, own(h), :] = middle
            ag_send(1 + 2 * layer, h, nm.at[layer], norm(middle, gn[layer, 1:2, :]))
        if layer == 0:
            weights(0, [("x", 8)] + [("core", i) for i in range(4, 8)])
            weights(1, [("y", 8), ("y", 9), ("x", 4), ("x", 5)])
        else:
            weights(1, [("core", i) for i in range(4, 8)])
        for h in range(HALVES):
            ag_wait(1 + 2 * layer, h, nm.at[layer])
            at = rows_of(h)

            def up_tile(j, carry):
                cols = cols_of(j)
                up = mm(nm[layer, at, :], wb[layer, 1280:2560, cols])
                upb[layer, at, cols] = up
                t = jnp.tanh(GELU_A * (up + GELU_B * up * up * up))
                hb[at, cols] = (0.5 * up * (1.0 + t)).astype(bf16)

            unrolled(D // TILE, up_tile)
            if layer == 1:
                continue
            if h == 0 and layer == 0:
                weights(0, [("x", 9), ("x", 10), ("x", 11)] + [("core", i) for i in range(8, 12)])
                weights(1, [("y", 10), ("y", 11), ("x", 6), ("x", 7)])
            rs_send(
                2 + 2 * layer, h, lambda j, cols: mm(hb[at, :], wb[layer, 2560:3840, cols])
            )
        if layer == 0:
            weights(1, [("x", 8), ("x", 9)])
            for h in range(HALVES):
                out = mlp_out(0, h)
                stream = out.astype(f32)
                sx[1, own(h), :] = stream
                ag_send(2, h, nb.at[1], norm(stream, gn[1, 0:1, :]))
            weights(1, [("x", 10), ("x", 11)])

    xa = x + 1 - 2 * lax.rem(x, 2)
    xb = 3 - x
    to_xa = (s, xa * 4 + 2 * yh + c, z)
    to_xb = (s, xb * 4 + 2 * yh + c, z)
    j1 = lax.rem(lax.div(x + 1, 2), 2)
    j2 = lax.div(x, 2)
    i1 = lax.div(x, 2)
    i2 = lax.rem(x, 2)
    half_at = (64 + 64 * j1, 192 + 64 * i1)
    half_off = (64 + 64 * (1 - j1), 192 + 64 * (1 - i1))
    quarter_at = (half_at[0] + 32 * j2, half_at[1] + 32 * i2)
    quarter_off = (half_at[0] + 32 * (1 - j2), half_at[1] + 32 * (1 - i2))
    first_peer = (to_xa, to_xb)
    second_peer = (to_xb, to_xa)

    class Group:
        def __init__(self, layer, k):
            self.layer, self.k = layer, k
            self.buf = gv if layer == 1 else wb.at[1]
            self.mine = k * 1280 + c * 640
            self.theirs = k * 1280 + (1 - c) * 640
            self.home = s == layer

        def rows(self, at, n):
            return self.buf.at[pl.ds(pl.multiple_of(self.mine + at, 16), n)]

        def result(self, at, n):
            return go_ref.at[pl.ds(pl.multiple_of(self.mine + at, 16), n)]

        def move(self, i, src, dst, peer):
            return remote(src, dst, e_s.at[self.layer, self.k], e_r.at[self.layer, self.k, i], peer)

        def add(self, at, n, sources):
            def body(i, carry):
                here = pl.ds(pl.multiple_of(self.mine + at + i * 16, 16), 16)
                there = pl.ds(pl.multiple_of(i * 16, 16), 16)
                total = self.buf[here, :].astype(f32)
                for source in sources:
                    total = total + source[there, :].astype(f32)
                self.buf[here, :] = total.astype(bf16)
                return carry

            lax.fori_loop(0, n // 16, body, 0)

        def total(self, i, n):
            ref = th.at[self.k, pl.ds(0, n)]
            return self.move(i, ref, ref, core)

        def core(self):
            src = self.buf.at[pl.ds(pl.multiple_of(self.theirs, 16), 640)]
            return self.move(0, src, th.at[self.k], core)

        def first(self, b, hf):
            dst = r1.at[self.k, pl.ds(128 * b + 64 * hf, 64)]
            return self.move(1, self.rows(320 * hf + half_off[b], 64), dst, first_peer[b])

        def second(self, b, hf):
            dst = r2.at[self.k, pl.ds(64 * b + 32 * hf, 32)]
            return self.move(2, self.rows(320 * hf + quarter_off[b], 32), dst, second_peer[b])

        def a_over_y(self, d):
            src = self.rows(320 * lax.div(y_at[d], 2), 64)
            return self.move(3, src, ra1.at[self.k, d - 1], y_peer[d])

        def a_over_x(self, d):
            src = self.rows(320 * yh + 16 * x_at[d], 16)
            return self.move(4, src, ra2.at[self.k, d - 1], x_peer[d])

        def b_over_y(self, d, b):
            src = self.rows(320 * lax.div(y_at[d], 2) + quarter_at[b], 32)
            return self.move(5, src, rb3.at[self.k, d - 1, pl.ds(32 * b, 32)], y_peer[d])

        def a_back_x(self, d):
            at = 320 * yh + 16 * x
            return self.move(6, self.rows(at, 16), self.result(at, 16), x_peer[d])

        def b_back_y(self, b):
            at = 320 * yh + quarter_at[b]
            return self.move(7, self.rows(at, 32), self.result(at, 32), y_peer[2])

        def back_second(self, b, hf):
            ref = self.result(320 * hf + quarter_at[b], 32)
            return self.move(8, ref, ref, second_peer[b])

        def back_first(self, b, hf):
            ref = self.result(320 * hf + half_at[b], 64)
            return self.move(9, ref, ref, first_peer[b])

        def a_back_y(self):
            ref = self.result(320 * yh, 64)
            return self.move(10, ref, ref, y_peer[2])

        def back_core(self, at, n=640):
            ref = self.result(at, n)
            return self.move(11, ref, ref, core)

        def keep(self, at, n):
            return pltpu.make_async_copy(
                self.rows(at, n), self.result(at, n), e_l.at[self.layer, self.k]
            )

        def to_homes(self, copies):
            @pl.when(self.home)
            def _():
                for copy in copies(2):
                    copy.start()

            @pl.when(jnp.logical_not(self.home))
            def _():
                for d in (1, 3):
                    for copy in copies(d):
                        copy.start()

        def s0(self):
            if self.layer == 0:
                pl.semaphore_wait(free_th.at[self.k], 1)
            self.core().start()

        def s1(self):
            self.core().wait_recv()
            self.add(0, 640, [th.at[self.k]])
            if self.layer == 1:
                pl.semaphore_signal(free_th.at[self.k], inc=1, device_id=core, device_id_type=MESH)
            else:
                pl.semaphore_wait(free_r1.at[self.k], 2)
            for b in range(2):
                for hf in range(2):
                    self.first(b, hf).start()
            self.to_homes(lambda d: [self.a_over_y(d)])

        def s2(self):
            self.total(1, 256).wait_recv()
            for b in range(2):
                for hf in range(2):
                    self.add(
                        320 * hf + half_at[b], 64, [r1.at[self.k, pl.ds(128 * b + 64 * hf, 64)]]
                    )
            if self.layer == 1:
                for peer in (to_xa, to_xb):
                    pl.semaphore_signal(
                        free_r1.at[self.k], inc=1, device_id=peer, device_id_type=MESH
                    )
            else:
                pl.semaphore_wait(free_r2.at[self.k], 2)
            for b in range(2):
                for hf in range(2):
                    self.second(b, hf).start()

        def s3(self):
            self.total(2, 128).wait_recv()
            for b in range(2):
                for hf in range(2):
                    self.add(
                        320 * hf + quarter_at[b], 32, [r2.at[self.k, pl.ds(64 * b + 32 * hf, 32)]]
                    )
            if self.layer == 1:
                for peer in (to_xa, to_xb):
                    pl.semaphore_signal(
                        free_r2.at[self.k], inc=1, device_id=peer, device_id_type=MESH
                    )
            self.to_homes(lambda d: [self.b_over_y(d, b) for b in range(2)])

            @pl.when(self.home)
            def _():
                self.total(3, 192).wait_recv()
                self.add(320 * yh, 64, [ra1.at[self.k, i] for i in range(3)])
                for d in (2, 1, 3):
                    self.a_over_x(d).start()

        def s4(self):
            @pl.when(self.home)
            def _():
                self.total(5, 192).wait_recv()
                for b in range(2):
                    at = 320 * yh + quarter_at[b]
                    self.add(at, 32, [rb3.at[self.k, i, pl.ds(32 * b, 32)] for i in range(3)])
                    self.keep(at, 32).start()
                    self.b_back_y(b).start()
                self.total(4, 48).wait_recv()
                at = 320 * yh + 16 * x
                self.add(at, 16, [ra2.at[self.k, i] for i in range(3)])
                self.keep(at, 16).start()
                for d in (2, 1, 3):
                    self.a_back_x(d).start()

        def s5(self):
            @pl.when(self.home)
            def _():
                self.keep(0, 80).wait()
                self.total(7, 64).wait_recv()
                for b in range(2):
                    for hf in range(2):
                        self.back_second(b, hf).start()
                self.total(6, 48).wait_recv()
                self.a_back_y().start()

        def s6(self):
            @pl.when(self.home)
            def _():
                self.total(8, 128).wait_recv()
                for b in range(2):
                    for hf in range(2):
                        self.back_first(b, hf).start()
                for b in range(2):
                    for hf in range(2):
                        self.back_core(320 * hf + half_at[b], 64).start()

        def s7(self):
            @pl.when(self.home)
            def _():
                self.a_back_y().wait_recv()
                for hf in range(2):
                    self.back_core(320 * hf, 64).start()
                self.total(9, 256).wait_recv()
                for b in range(2):
                    for hf in range(2):
                        self.back_core(320 * hf + half_off[b], 64).start()

        def sent(self, n):
            ref = wb.at[0, pl.ds(0, n)]
            return remote(ref, ref, e_s.at[self.layer, self.k], e_r.at[self.layer, self.k, 0], core)

        def drain(self):
            @pl.when(self.home)
            def _():
                self.back_core(0).wait_recv()
                self.sent(1760 + 640).wait_send()

            @pl.when(jnp.logical_not(self.home))
            def _():
                self.sent(1280).wait_send()

    groups = {(layer, k): Group(layer, k) for layer in range(2) for k in range(3)}
    att1, up1, down1 = (groups[1, k] for k in range(3))
    att0, up0, down0 = (groups[0, k] for k in range(3))

    def put(layer, at, value):
        if layer == 1:
            gv[at, :] = value.astype(bf16)
        else:
            wb[1, at, :] = value.astype(bf16)

    def grad_tiles(layer, k, left, right):
        for i in range(D // TILE):
            put(layer, pl.ds(k * 1280 + i * TILE, TILE), tm(left[:, cols_of(i)], right[...]))
        groups[layer, k].s0()

    def t_move(i, src, dst, peer):
        return remote(src, dst, t_s.at[i], t_r.at[i], peer)

    def t_rows(sec, at, n):
        return gt.at[sec, pl.ds(pl.multiple_of(at, 16), n)]

    def t_result(at, n):
        return go_ref.at[pl.ds(pl.multiple_of(LAYER_ROWS + at, 16), n)]

    def t_core(sec):
        return t_move(0, t_rows(sec, 128 * (1 - c), 128), tt.at[sec], core)

    def t_over_x(d, sec):
        src = t_rows(sec, 128 * c + 32 * x_at[d], 32)
        return t_move(1, src, tx.at[d - 1, sec], x_peer[d])

    def t_over_y(d):
        src = t_rows(lax.rem(y_at[d], 2), 128 * c + 32 * x + 16 * lax.div(y_at[d], 2), 16)
        return t_move(2, src, ty.at[d - 1], y_peer[d])

    t_own = 128 * c + 32 * x + 16 * yh

    def t_back_y():
        return t_move(3, t_rows(s, t_own, 16), t_result(t_own, 16), y_peer[2])

    def t_keep():
        return pltpu.make_async_copy(t_rows(s, t_own, 16), t_result(t_own, 16), t_l)

    def t_back_x(d):
        ref = t_result(128 * c + 32 * x, 32)
        return t_move(4, ref, ref, x_peer[d])

    def t_back_core():
        ref = t_result(128 * c, 128)
        return t_move(5, ref, ref, core)

    def t_total(i, n):
        ref = gt.at[0, pl.ds(0, n)]
        return t_move(i, ref, ref, core)

    def t_add(sec, at, n, sources):
        here = pl.ds(pl.multiple_of(at, 16), n)
        total = gt[sec, here, :].astype(f32)
        for source in sources:
            total = total + source[...].astype(f32)
        gt[sec, here, :] = total.astype(bf16)

    def t1():
        t_total(0, 256).wait_recv()
        for sec in range(2):
            for i in range(4):
                t_add(sec, 128 * c + 32 * i, 32, [tt.at[sec, pl.ds(32 * i, 32)]])
            for d in (2, 1, 3):
                t_over_x(d, sec).start()

    def t2():
        t_total(1, 192).wait_recv()
        for sec in range(2):
            t_add(sec, 128 * c + 32 * x, 32, [tx.at[i, sec] for i in range(3)])
        for d in (2, 1, 3):
            t_over_y(d).start()

    def t3():
        t_total(2, 48).wait_recv()
        t_add(s, t_own, 16, [ty.at[i] for i in range(3)])
        t_keep().start()
        t_back_y().start()

    def t4():
        t_keep().wait()
        t_back_y().wait_recv()
        for d in (2, 1, 3):
            t_back_x(d).start()

    def t5():
        t_total(4, 96).wait_recv()
        t_back_core().start()

    weights(1, [("core", i) for i in range(8, 12)])
    cot_copy.wait()
    grad_tiles(1, 2, hb, gb.at[0])
    gg[...] = jnp.zeros_like(gg)

    for layer in (1, 0):
        st = 5 if layer == 1 else 7
        for h in range(HALVES):
            at = rows_of(h)
            if layer == 0:
                ag_wait(5, h, gb.at[1])

            def d_up_tile(j, carry):
                cols = cols_of(j)
                rows = pl.ds(2560 + j * TILE, TILE)
                d_hidden = mm_t(gb[1 - layer, at, :], wb[layer, rows, :])
                up = upb[layer, at, cols]
                t = jnp.tanh(GELU_A * (up + GELU_B * up * up * up))
                slope = 0.5 * (1.0 + t) + 0.5 * up * (1.0 - t * t) * (
                    GELU_A * (1.0 + 3.0 * GELU_B * up * up)
                )
                du[at, cols] = (d_hidden * slope).astype(bf16)
                if layer == 0:
                    hb[at, cols] = (0.5 * up * (1.0 + t)).astype(bf16)

            unrolled(D // TILE, d_up_tile)
            if layer == 0 and h == 1:
                up1.s2()
            if layer == 1 and h == 1:
                down1.s1()
            rs_send(
                st, h,
                lambda j, cols: mm_t(
                    du[at, :], wb[layer, pl.ds(1280 + j * TILE, TILE), :]
                ),
            )
        if layer == 0:
            w_sent(4, x_s, x_r).wait_send()
            w_sent(2, f_s, f_r).wait_send()
        if layer == 0:
            grad_tiles(0, 2, hb, gb.at[1])
        for h in range(HALVES):
            dn = rs_take(st, h)
            dx, gain = norm_back(dn, mid[layer, own(h), :], gn[layer, 1:2, :])
            dm = gb[1 - layer, chunk(h, z), :].astype(f32) + dx
            dmid[own(h), :] = dm
            gg[2 * layer + 1 : 2 * layer + 2, :] += gain
            if layer == 0:
                ag_total(4, h).wait_send()
            ag_send(st - 1, h, mb, dm)
        grad_tiles(layer, 1, nm.at[layer], du)
        if layer == 1:
            for j in range(D // TILE):
                pd[:, cols_of(j)] = mm(hb[...], wb[1, 2560:3840, cols_of(j)]).astype(bf16)
            down1.s2()
        else:
            down0.s1()
        for h in range(HALVES):
            ag_wait(st - 1, h, mb)
            attention_back(layer, h)
            if h == 1 and layer == 1:
                up1.s1()
            if h == 1 and layer == 0:
                up0.s1()
                up1.s3()
                att1.s2()
            at = rows_of(h)
            rs_send(
                st + 1, h,
                lambda j, cols: mm(dqb[0, at, :], wb[layer, 0:ATT, cols])
                + mm(dqb[1, at, :], wb[layer, ATT : 2 * ATT, cols])
                + mm(dqb[2, at, :], wb[layer, 2 * ATT : 3 * ATT, cols]),
            )
        for i in range(3):
            put(layer, pl.ds(i * ATT, ATT), tm(dqb[i], nb[layer]))
        put(layer, pl.ds(960, 320), tm(ct[layer], mb[...]))
        groups[layer, 0].s0()
        if layer == 1:
            down1.s3()
        else:
            down0.s2()
        for h in range(HALVES):
            dn = rs_take(st + 1, h)
            dx, gain = norm_back(dn, sx[layer, own(h), :], gn[layer, 0:1, :])
            gg[2 * layer : 2 * layer + 1, :] += gain
            ag_send(st, h, gb.at[layer], dmid[own(h), :] + dx)
        if layer == 1:
            att1.s1()
        else:
            att0.s1()
            up0.s2()
            down1.s4()

    def gg_copy(d):
        return remote(gg, ggr.at[d - 1], gg_s, gg_r, z_peer[d])

    for d in (1, 2, 3):
        gg_copy(d).start()

    for h in range(HALVES):
        ag_wait(7, h, gb.at[0])
        rs_send(4, h, None)
        at = rows_of(h)
        low = gb[0, at, :]
        before = pre[at, :]
        sig = jax.nn.sigmoid(before)
        d_pre = (
            mm_t(low, w_hid_ref[...]) * (sig * (1.0 + before * (1.0 - sig)))
        ).astype(bf16)
        dctx[at, :] = d_pre
        points = mm_t(d_pre, w_in_ref[...])
        points = points + jnp.where(z == 0, mm_t(low, w_res_ref[...]), 0.0)
        keep = 1.0 - patch_ref[at, :].astype(f32)
        gpad[at, 0:PATCH] = points[:, 0:PATCH] * keep[:, PATCH : 2 * PATCH]
    down0.s3()
    points = gpad[:, 0:64]
    high = points.astype(bf16)
    low = (points - high.astype(f32)).astype(bf16)
    row = lax.broadcasted_iota(jnp.int32, (ROWS, ROWS), 0)
    col = lax.broadcasted_iota(jnp.int32, (ROWS, ROWS), 1)
    swap = jnp.where(
        ((row >> 4) == (col & 15)) & ((row & 15) == (col >> 4)), 1.0, 0.0
    ).astype(bf16)
    points = mm(swap, high) + mm(swap, low)
    for k in range(8):
        dps[k, :, 0:64] = points[k * 32 : (k + 1) * 32]
        dps[k, :, 64:128] = jnp.zeros((32, 64), f32)
    me = s * 4 + z

    def dp_copy(d):
        to = lax.rem(me + d, 8)
        return remote(
            dps.at[to], dpr.at[me], dp_s, dp_r,
            (lax.div(to, 4), dp, lax.rem(to, 4)),
        )

    for d in range(1, 8):
        dp_copy(d).start()
    dpr[me] = dps[me]

    grad_low = gb[0]
    hid = tm(tokh[...], grad_low).astype(bf16)
    res = tm(patch_ref[...], grad_low).astype(bf16)
    inn = tm(patch_ref[...], dctx[...]).astype(bf16)
    for sec in range(2):
        lanes = slice(sec * 640, sec * 640 + 640)
        gt[sec, 0:160, 0:640] = hid[0:160, lanes]
        gt[sec, 0:160, 640:1280] = hid[160:320, lanes]
        gt[sec, 160:192, 0:640] = res[0:32, lanes]
        gt[sec, 160:192, 640:1280] = res[32:64, lanes]
        gt[sec, 192:224, :] = jnp.zeros((32, D), bf16)
        gt[sec, 192:224, 0:320] = inn[sec * 32 : sec * 32 + 32]
    total = gg[...]
    remote(ggr, ggr, gg_s, gg_r, core).wait_recv()
    for d in (1, 2, 3):
        total = total + ggr[d - 1]
    for sec in range(2):
        gt[sec, 224:256, :] = jnp.concatenate(
            [total[2 * sec : 2 * sec + 2], jnp.zeros((30, D), f32)], axis=0
        ).astype(bf16)

    for sec in range(2):
        t_core(sec).start()
    att1.s3()
    att0.s2()
    up0.s3()
    t1()
    down0.s4()
    down1.s5()
    att0.s3()
    up1.s4()
    t2()
    down0.s5()
    up0.s4()
    att1.s4()
    for h in range(HALVES):
        mlp_out(1, h)
        own_out(h)
    down1.s6()
    down0.s6()
    up0.s5()
    up1.s5()
    att0.s4()
    att1.s5()
    t3()
    att0.s5()
    up0.s6()
    up1.s6()
    down0.s7()
    down1.s7()
    t4()
    att0.s6()
    att1.s6()
    up0.s7()
    up1.s7()
    for h in range(HALVES):
        pass_out(h)
    t5()
    att0.s7()
    att1.s7()
    seven = dps.at[pl.ds(0, 7)]
    remote(seven, seven, dp_s, dp_r, core).wait_recv()
    for sec in range(2):
        points_ref[sec] = dpr[4 * sec] + dpr[4 * sec + 1] + dpr[4 * sec + 2] + dpr[4 * sec + 3]

    w_sent(4, w_s, w_r).wait_send()
    for group in groups.values():
        group.drain()
    for i, n in ((0, 256), (1, 192), (2, 48), (3, 16), (4, 96)):
        t_total(i, n).wait_send()
    t_back_core().wait()
    gn_send.wait_send()
    for h in range(HALVES):
        rs_total(7, h).wait_send()
        rs_total(4, h).wait_send()
        for st in (0, 1, 2, 3, 5, 6, 7):
            ag_total(st, h).wait_send()
        lo_cross(h).wait_send()
        lo_keep(h).wait()
        for i in (1, 2):
            lo_total(i, h).wait()
    remote(ggr, ggr, gg_s, gg_r, core).wait_send()
    remote(seven, seven, dp_s, dp_r, core).wait_send()


def run_layers(series, missing, w_in, w_hid, w_res, gain_a, gain_m, wq, wo, wu, wd, cotangent):
    cos, sin, turn = rotary_arrays()
    vm = pl.BlockSpec(memory_space=pltpu.VMEM)
    hbm = pl.BlockSpec(memory_space=pl.ANY)
    dma = pltpu.SemaphoreType.DMA
    scratch = [
        pltpu.VMEM((2 * PATCH, ATT), bf16),
        pltpu.VMEM((ATT, D), bf16),
        pltpu.VMEM((2 * PATCH, D), bf16),
        pltpu.VMEM((BLOCK, ATT), f32),
        pltpu.VMEM((BLOCK, ATT), f32),
        pltpu.VMEM((ATT, ATT), bf16),
        dma((6,)),
        pltpu.VMEM((ROWS, 2 * PATCH), bf16),
        pltpu.VMEM((2, LAYER_ROWS, D), bf16),
        pltpu.VMEM((2, 2, D), f32),
        pltpu.VMEM((ROWS, ATT), bf16),
        pltpu.VMEM((ROWS, ATT), f32),
        pltpu.VMEM((2, ROWS // 4, D), f32),
        pltpu.VMEM((2, ROWS // 4, D), f32),
        pltpu.VMEM((2, ROWS, D), bf16),
        pltpu.VMEM((2, ROWS, D), bf16),
        pltpu.VMEM((2, 3, ROWS, ATT), bf16),
        pltpu.VMEM((2, ROWS // BLOCK, HEADS_HERE * BLOCK, BLOCK), f32),
        pltpu.VMEM((2, ROWS, ATT), bf16),
        pltpu.VMEM((2, ROWS, D), f32),
        pltpu.VMEM((ROWS, D), bf16),
        pltpu.VMEM((2, ROWS, D), bf16),
        pltpu.VMEM((ROWS, D), bf16),
        pltpu.VMEM((ROWS, D), bf16),
        pltpu.VMEM((3, ROWS, ATT), bf16),
        pltpu.VMEM((ROWS, ATT), bf16),
        pltpu.VMEM((LAYER_ROWS, D), bf16),
        pltpu.VMEM((2, PACK_ROWS - LAYER_ROWS, D), bf16),
        pltpu.VMEM((2, ROWS, D), bf16),
        pltpu.VMEM((2, 3, ROWS // 4, D), bf16),
        pltpu.VMEM((ROWS // 4, D), f32),
        pltpu.VMEM((2, ROWS // 4, D), bf16),
        pltpu.VMEM((8, D), f32),
        pltpu.VMEM((3, 8, D), f32),
        pltpu.VMEM((8, 32, 128), f32),
        pltpu.VMEM((8, 32, 128), f32),
        pltpu.VMEM((ROWS, 128), f32),
        pltpu.VMEM((3, 640, D), bf16),
        pltpu.VMEM((3, 256, D), bf16),
        pltpu.VMEM((3, 128, D), bf16),
        pltpu.VMEM((3, 3, 64, D), bf16),
        pltpu.VMEM((3, 3, 16, D), bf16),
        pltpu.VMEM((3, 3, 64, D), bf16),
        pltpu.VMEM((2, 128, D), bf16),
        pltpu.VMEM((3, 2, 32, D), bf16),
        pltpu.VMEM((3, 16, D), bf16),
        pltpu.VMEM((ROWS, D), bf16),
        dma, *[dma, dma((N_PIECES,))] * 3,
        dma, dma, dma,
        dma((9, HALVES)), dma((9, HALVES)),
        dma((8, HALVES)), dma((8, HALVES)),
        dma((HALVES,)), dma((3, HALVES)), dma((3, HALVES)),
        dma, dma, dma, dma,
        dma((2, 3)), dma((2, 3, 12)), dma((2, 3)),
        dma((6,)), dma((6,)), dma,
        *[pltpu.SemaphoreType.REGULAR((3,))] * 3,
    ]
    return pl.pallas_call(
        layers_kernel,
        out_shape=(
            jax.ShapeDtypeStruct((2 * ROWS, D), bf16),
            jax.ShapeDtypeStruct((PACK_ROWS, D), bf16),
            jax.ShapeDtypeStruct((2, 32, 128), f32),
        ),
        in_specs=[vm] * 2 + [hbm] * 3 + [vm] * 2 + [hbm] * 8,
        out_specs=(hbm, hbm, vm),
        scratch_shapes=scratch,
        compiler_params=pltpu.CompilerParams(
            collective_id=0, has_side_effects=True, vmem_limit_bytes=62 * 2**20
        ),
        cost_estimate=pl.CostEstimate(
            flops=15_000_000_000, bytes_accessed=50_000_000, transcendentals=4_000_000
        ),
        name="layers",
    )(
        series, missing, w_in, w_hid, w_res, gain_a, gain_m, wq, wo, wu, wd, cotangent,
        jnp.asarray(cos, f32), jnp.asarray(sin, f32), jnp.asarray(turn, bf16),
    )


STEP = 320
STEPS = LAYER_ROWS // STEP


def widen_kernel(
    total_ref, lo_ref, points_ref,
    qkv, out, up, down, hid, res, inn, gain_a, gain_m, series_grad, lo_out,
    low, wide, small, kept, in_sem, out_sem, small_sem, lo_sem,
):
    places_of = [(qkv, i) for i in range(3)] + [(out, 0)]
    places_of += [(up, i) for i in range(4)] + [(down, i) for i in range(4)]

    def rows(i):
        return pl.ds(i * STEP, STEP)

    def load(i):
        return pltpu.make_async_copy(total_ref.at[rows(i)], low.at[rows(i)], in_sem.at[i])

    def store(i):
        ref, k = places_of[i]
        return pltpu.make_async_copy(wide.at[rows(i)], ref.at[rows(k)], out_sem.at[i])

    load_small = pltpu.make_async_copy(
        total_ref.at[pl.ds(LAYER_ROWS, PACK_ROWS - LAYER_ROWS)], small, small_sem
    )
    load_lo = pltpu.make_async_copy(lo_ref, kept, lo_sem)
    store_lo = pltpu.make_async_copy(kept, lo_out, lo_sem)
    for i in range(STEPS):
        load(i).start()
    load_small.start()
    load_lo.start()
    for i in range(STEPS):
        load(i).wait()

        def body(j, carry, i=i):
            at = pl.ds(pl.multiple_of(i * STEP + j * 32, 32), 32)
            wide[at, :] = low[at, :].astype(f32)
            return carry

        lax.fori_loop(0, STEP // 32, body, 0, unroll=2)
        store(i).start()
    load_lo.wait()
    store_lo.start()
    load_small.wait()
    values = small[...].astype(f32)
    hid[0:160, :] = values[0:160, 0:640]
    hid[160:320, :] = values[0:160, 640:1280]
    res[0:32, :] = values[160:192, 0:640]
    res[32:64, :] = values[160:192, 640:1280]
    inn[...] = values[192:224, 0:320]
    gain_a[...] = values[224:225]
    gain_m[...] = values[225:226]
    for sec in range(2):
        for j in range(2):
            series_grad[16 * sec : 16 * sec + 16, 32 * j : 32 * j + 32] = points_ref[
                sec, 16 * j : 16 * j + 16, 0:32
            ]
    for i in range(STEPS):
        store(i).wait()
    store_lo.wait()


def widen(total, layer_out, points):
    shapes = ((960, D), (320, D), (1280, D), (1280, D), (320, 640), (64, 640), (32, 320), (1, D), (1, D), (32, 64))
    hbm = pl.BlockSpec(memory_space=pl.ANY)
    vm = pl.BlockSpec(memory_space=pltpu.VMEM)
    dma = pltpu.SemaphoreType.DMA
    return pl.pallas_call(
        widen_kernel,
        out_shape=[jax.ShapeDtypeStruct(shape, f32) for shape in shapes]
        + [jax.ShapeDtypeStruct((2 * ROWS, D), bf16)],
        in_specs=[hbm, hbm, vm],
        out_specs=[hbm] * 4 + [vm] * 6 + [hbm],
        scratch_shapes=[
            pltpu.VMEM((LAYER_ROWS, D), bf16),
            pltpu.VMEM((LAYER_ROWS, D), f32),
            pltpu.VMEM((PACK_ROWS - LAYER_ROWS, D), bf16),
            pltpu.VMEM((2 * ROWS, D), bf16),
            dma((STEPS,)), dma((STEPS,)), dma, dma,
        ],
        compiler_params=pltpu.CompilerParams(vmem_limit_bytes=60 * 2**20),
        cost_estimate=pl.CostEstimate(flops=0, bytes_accessed=32_000_000, transcendentals=0),
        name="widen",
    )(total, layer_out, points)


def per_device(
    series, missing, w_in, w_hid, w_res, gain_attn, w_qkv, w_out, gain_mlp, w_up, w_down, cotangent
):
    wq = jnp.transpose(w_qkv[0], (1, 2, 0)).reshape(3 * ATT, D)
    layer_out, total, points = run_layers(
        series, missing, w_in, w_hid, w_res, gain_attn, gain_mlp, wq, w_out[0], w_up[0], w_down[0],
        cotangent,
    )
    g_qkv, g_out, g_up, g_down, g_hid, g_res, g_in, gain_a, gain_m, series_grad, layer_out = widen(
        total, layer_out, points
    )
    g_qkv = jnp.transpose(g_qkv.reshape(3, ATT, D), (2, 0, 1))
    return (
        layer_out[None],
        series_grad,
        g_in,
        g_hid,
        g_res,
        gain_a,
        g_qkv[None],
        g_out[None],
        gain_m,
        g_up[None],
        g_down[None],
    )


def solution(mesh):
    in_specs = (
        P("dp", None),
        P("dp", None),
        P(None, "tensor"),
        P("tensor", None),
        P(),
        P("section", None),
        P("section", None, None, "tensor"),
        P("section", "tensor", None),
        P("section", None),
        P("section", None, "tensor"),
        P("section", "tensor", None),
        P("dp", None),
    )
    out_specs = (
        P("section", "dp", None),
        P("dp", ("section", "tensor")),
        P("section", "tensor"),
        P("tensor", "section"),
        P(None, "section"),
        P("section", None),
        P("section", None, None, "tensor"),
        P("section", "tensor", None),
        P("section", None),
        P("section", None, "tensor"),
        P("section", "tensor", None),
    )
    return jax.shard_map(
        per_device, mesh=mesh, in_specs=in_specs, out_specs=out_specs, check_vma=False
    )
```

```python
import math

import jax
import jax.numpy as jnp
import numpy as np
from jax import lax
from jax.experimental import pallas as pl
from jax.experimental.pallas import tpu as pltpu
from jax.sharding import PartitionSpec as P

D = 1280
HEADS_HERE = 4
HEAD_DIM = 80
ATT = HEADS_HERE * HEAD_DIM
PATCH = 32
PATCHES = 16
ROWS = 256
HALVES = 2
RH = ROWS // HALVES
RQ = RH // 4
TILE = 256
BLOCK = 128
MATS = ((0, 960), (960, 320), (1280, 1280), (2560, 1280))
PIECES = tuple((320 * i, 320, 0 if i < 3 else 1 if i < 4 else 2 if i < 8 else 3) for i in range(12))
N_PIECES = len(PIECES)
LAYER_ROWS = 3840
PACK_ROWS = 4096
RS_BEFORE = {2: 0, 3: 1, 5: 3, 6: 2, 7: 5, 8: 6, 4: 8}
MESH = pl.DeviceIdType.MESH
f32 = jnp.float32
bf16 = jnp.bfloat16
eps_norm = 1e-06
masked_score = -1e30
GELU_A = math.sqrt(2.0 / math.pi)
GELU_B = 0.044715


def mm(a, b):
    return lax.dot_general(a, b, (((1,), (0,)), ((), ())), preferred_element_type=f32)


def mm_t(a, b):
    return lax.dot_general(a, b, (((1,), (1,)), ((), ())), preferred_element_type=f32)


def tm(a, b):
    return lax.dot_general(a, b, (((0,), (0,)), ((), ())), preferred_element_type=f32)


def unrolled(count, body):
    for j in range(count):
        body(j, 0)


def rotary_arrays():
    half = HEAD_DIM // 2
    position = (np.arange(BLOCK) % PATCHES).astype(np.float32)
    frequency = np.exp(
        np.arange(half, dtype=np.float32) * np.float32(-2.0 * math.log(10000.0) / HEAD_DIM)
    )
    angles = position[:, None] * frequency[None, :]
    lane = np.arange(ATT) % half
    turn = np.zeros((ATT, ATT), np.float32)
    for j in range(ATT):
        if j % HEAD_DIM < half:
            turn[j + half, j] = -1.0
        else:
            turn[j - half, j] = 1.0
    return np.cos(angles)[:, lane], np.sin(angles)[:, lane], turn


def places():
    s = lax.axis_index("section")
    dp = lax.axis_index("dp")
    z = lax.axis_index("tensor")
    c = lax.rem(dp, 2)
    yh = lax.rem(lax.div(dp, 2), 2)
    x = lax.div(dp, 4)
    return s, dp, z, x, yh, c


def layers_kernel(
    series_ref, missing_ref, w_in_in, w_hid_in, w_res_in, gain_a_ref, gain_m_ref, wq_ref, wo_ref, wu_ref, wd_ref,
    cot_ref, cos_in, sin_in, turn_in,
    lo_ref, go_ref, points_ref,
    w_in_ref, w_hid_ref, w_res_ref, cos_ref, sin_ref, turn_ref, in_l,
    patch_ref, wb, gn, tokh, pre, sx, mid, nb, nm, qb, pb, ct, upb, hb, gb, mb, du, dqb, dctx, gv, gt,
    sb, rb, dmid, ob, gg, ggr, dps, dpr, gpad,
    th, r1, r2, ra1, ra2, rb3, tt, tx, ty, pd,
    w_loc, w_s, w_r, x_s, x_r, f_s, f_r, gn_s, gn_r, cot_l,
    rs_s, rs_r, ag_s, ag_r, lo_l, lo_s, lo_r, gg_s, gg_r, dp_s, dp_r,
    e_s, e_r, e_l, t_s, t_r, t_l, free_th, free_r1, free_r2,
):
    s, dp, z, x, yh, c = places()
    other = 1 - s
    z_peer = [None] + [(s, dp, lax.rem(z + d, 4)) for d in (1, 2, 3)]
    z_at = [z] + [lax.rem(z + d, 4) for d in (1, 2, 3)]
    y_a = (other, dp, z)
    y_b = (other, dp + 2 - 4 * yh, z)
    core = (s, dp + 1 - 2 * c, z)
    across = [(other, dp, z_at[d]) for d in range(4)]
    y = 2 * yh + s
    x_at = [x] + [lax.rem(x + d, 4) for d in (1, 2, 3)]
    y_at = [y] + [lax.rem(y + d, 4) for d in (1, 2, 3)]
    x_peer = [None] + [(s, x_at[d] * 4 + 2 * yh + c, z) for d in (1, 2, 3)]
    y_peer = [None] + [
        (lax.rem(y_at[d], 2), x * 4 + 2 * lax.div(y_at[d], 2) + c, z) for d in (1, 2, 3)
    ]
    x_up, x_down = x_peer[1], x_peer[3]
    w_refs = (wq_ref, wo_ref, wu_ref, wd_ref)

    small_inputs = [
        pltpu.make_async_copy(src, dst, in_l.at[i])
        for i, (src, dst) in enumerate((
            (w_in_in, w_in_ref), (w_hid_in, w_hid_ref), (w_res_in, w_res_ref),
            (cos_in, cos_ref), (sin_in, sin_ref), (turn_in, turn_ref),
        ))
    ]
    for copy in small_inputs:
        copy.start()
    barrier = pltpu.get_barrier_semaphore()
    peers = z_peer[1:] + across + [y_b, core] + x_peer[1:] + [y_peer[2]]
    for peer in peers:
        pl.semaphore_signal(barrier, inc=1, device_id=peer, device_id_type=MESH)
    pl.semaphore_wait(barrier, len(peers))

    def remote(src, dst, ssem, rsem, peer):
        return pltpu.make_async_remote_copy(
            src_ref=src, dst_ref=dst, send_sem=ssem, recv_sem=rsem,
            device_id=peer, device_id_type=MESH,
        )

    odd = lax.rem(x, 2)

    def w_local(m):
        off, n = MATS[m]
        return pltpu.make_async_copy(w_refs[m], wb.at[s, pl.ds(off, n)], w_loc)

    def share(i, parity, k):
        off, n, m = PIECES[i]
        first = (n // 4 + 31) // 32 * 16 if i % 2 == 0 else n // 4 // 32 * 16
        size = first if k == 0 else n // 4 - first
        return (2 * c + parity) * (n // 4) + k * first, size

    def w_over_y(i, k):
        off, n, m = PIECES[i]
        at, size = share(i, odd, k)
        src = w_refs[m].at[pl.ds(pl.multiple_of(off - MATS[m][0] + at, 16), size)]
        dst = wb.at[s, pl.ds(pl.multiple_of(off + at, 16), size)]
        return remote(src, dst, w_s, w_r.at[i], (y_a, y_b)[k])

    def w_over_x(i, k, parity):
        at, size = share(i, parity, k)
        ref = wb.at[other, pl.ds(pl.multiple_of(PIECES[i][0] + at, 16), size)]
        return remote(ref, ref, x_s, x_r.at[i], (x_up, x_down)[k])

    def w_to_core(i, q):
        off, n, m = PIECES[i]
        parity = odd if q == 0 else 1 - odd
        ref = wb.at[other, pl.ds(pl.multiple_of(off + (2 * c + parity) * (n // 4), 16), n // 4)]
        return remote(ref, ref, f_s, f_r.at[i], core)

    def w_total(i, part, ssem, rsem):
        ref = wb.at[0, pl.ds(0, PIECES[i][1] // part)]
        return remote(ref, ref, ssem, rsem.at[i], core)

    def w_sent(part, ssem, rsem):
        ref = wb.at[0, pl.ds(0, LAYER_ROWS // part)]
        return remote(ref, ref, ssem, rsem.at[0], core)

    def weights(layer, steps):
        @pl.when(s != layer)
        def _():
            for step, i in steps:
                if step == "y":
                    w_total(i, 4, w_s, w_r).wait_recv()
                    for k in range(2):
                        w_over_x(i, k, odd).start()
                    w_to_core(i, 0).start()
                elif step == "x":
                    w_total(i, 4, x_s, x_r).wait_recv()
                    w_to_core(i, 1).start()
                else:
                    w_total(i, 2, f_s, f_r).wait_recv()

    gains = gn.at[s]
    gains[0:1, :] = gain_a_ref[...]
    gains[1:2, :] = gain_m_ref[...]
    gn_send = remote(gn.at[s], gn.at[s], gn_s, gn_r, y_a)
    cot_copy = pltpu.make_async_copy(
        cot_ref.at[pl.ds(pl.multiple_of(s * ROWS, ROWS), ROWS)], gb.at[0], cot_l
    )
    gn_send.start()
    def start_weights(first, last):
        for i in range(first, last):
            for k in range(2):
                w_over_y(i, k).start()

    start_weights(0, 4)
    for m in range(4):
        w_local(m).start()
    cot_copy.start()

    def rows_of(h):
        return pl.ds(h * RH, RH)

    def chunk(h, zz):
        return pl.ds(pl.multiple_of(h * RH + zz * RQ, RQ), RQ)

    def cols_of(j):
        return pl.ds(j * TILE, TILE)

    def rs_copy(st, h, d, cols=None):
        src = sb.at[st % 2, chunk(h, z_at[d])]
        dst = rb.at[st % 2, d - 1, pl.ds(h * RQ, RQ)]
        if cols is not None:
            src = sb.at[st % 2, chunk(h, z_at[d]), cols]
            dst = rb.at[st % 2, d - 1, pl.ds(h * RQ, RQ), cols]
        return remote(src, dst, rs_s.at[st, h], rs_r.at[st, h], z_peer[d])

    def rs_total(st, h):
        ref = rb.at[st % 2, pl.ds(0, 3), pl.ds(h * RQ, RQ)]
        return remote(ref, ref, rs_s.at[st, h], rs_r.at[st, h], core)

    def rs_send(st, h, produce):
        if st in RS_BEFORE:
            rs_total(RS_BEFORE[st], h).wait_send()

        if produce is None:
            sb[st % 2, rows_of(h), :] = pd[rows_of(h), :]
            for d in (2, 1, 3):
                rs_copy(st, h, d).start()
            return

        def body(j, carry):
            cols = cols_of(j)
            sb[st % 2, rows_of(h), cols] = produce(j, cols).astype(bf16)
            if j in (1, 3, 4):
                part = {1: pl.ds(0, 512), 3: pl.ds(512, 512), 4: pl.ds(1024, 256)}[j]
                for d in (2, 1, 3):
                    rs_copy(st, h, d, part).start()

        unrolled(D // TILE, body)

    def rs_take(st, h):
        total = sb[st % 2, chunk(h, z), :].astype(f32)
        rs_total(st, h).wait_recv()
        for d in (1, 2, 3):
            total = total + rb[st % 2, d - 1, pl.ds(h * RQ, RQ), :].astype(f32)
        return total

    def ag_copy(st, h, d, dst):
        at = dst.at[chunk(h, z)]
        return remote(at, at, ag_s.at[st, h], ag_r.at[st, h], z_peer[d])

    def ag_send(st, h, dst, value):
        dst[chunk(h, z), :] = value.astype(bf16)
        for d in (2, 1, 3):
            ag_copy(st, h, d, dst).start()

    def ag_total(st, h):
        ref = pd.at[pl.ds(0, 3 * RQ)]
        return remote(ref, ref, ag_s.at[st, h], ag_r.at[st, h], core)

    def ag_wait(st, h, dst):
        ag_total(st, h).wait_recv()

    def own(h):
        return pl.ds(h * RQ, RQ)

    def scale_of(v):
        return lax.rsqrt(jnp.mean(v * v, axis=-1, keepdims=True) + eps_norm)

    def norm(v, g):
        return v * scale_of(v) * g

    def norm_back(dn, v, g):
        r = scale_of(v)
        weighted = g * dn
        inner = jnp.mean(v * weighted, axis=-1, keepdims=True)
        return r * weighted - v * (r * r * r * inner), jnp.sum(dn * v * r, axis=0, keepdims=True)

    head_lane = lax.broadcasted_iota(jnp.int32, (1, ATT), 1)
    head_mask = [
        (head_lane >= HEAD_DIM * h) & (head_lane < HEAD_DIM * (h + 1)) for h in range(HEADS_HERE)
    ]

    def spread(v):
        wide = v.astype(f32)
        return jnp.concatenate(
            [jnp.where(m, wide, 0.0) for m in head_mask], axis=0
        ).astype(bf16)

    def gather(v):
        total = jnp.where(head_mask[0], v[:BLOCK], 0.0)
        for h in range(1, HEADS_HERE):
            total = total + jnp.where(head_mask[h], v[h * BLOCK : (h + 1) * BLOCK], 0.0)
        return total

    def turned(v, sign):
        high = v.astype(bf16)
        low = (v - high.astype(f32)).astype(bf16)
        swapped = mm(high, turn_ref[...]) + mm(low, turn_ref[...])
        if sign < 0:
            swapped = -swapped
        return v * cos_ref[...] + swapped * sin_ref[...]

    inv = 1.0 / math.sqrt(HEAD_DIM)

    def blocks_of(h):
        return range(h * RH // BLOCK, (h + 1) * RH // BLOCK)

    def attention_front(layer, h):
        for b in blocks_of(h):
            at = pl.ds(b * BLOCK, BLOCK)
            normed = nb[layer, at, :]
            first = b == 0
            if first:
                weights(layer, [("core", 0)])
            q = turned(mm_t(normed, wb[layer, 0:ATT, :]), 1).astype(bf16)
            if first:
                weights(layer, [("core", 1)])
            k = turned(mm_t(normed, wb[layer, ATT : 2 * ATT, :]), 1).astype(bf16)
            if first:
                weights(layer, [("core", 2)])
            v = mm_t(normed, wb[layer, 2 * ATT : 3 * ATT, :]).astype(bf16)
            qb[layer, 0, at, :] = q
            qb[layer, 1, at, :] = k
            qb[layer, 2, at, :] = v
            scores = mm_t(spread(q), k) * inv
            row = lax.broadcasted_iota(jnp.int32, scores.shape, 0) & (BLOCK - 1)
            col = lax.broadcasted_iota(jnp.int32, scores.shape, 1)
            allowed = (col <= row) & (col >= (row & (BLOCK - PATCHES)))
            scores = jnp.where(allowed, scores, masked_score)
            e = jnp.exp(scores - jnp.max(scores, axis=-1, keepdims=True))
            probs = e / jnp.sum(e, axis=-1, keepdims=True)
            pb[layer, b] = probs
            ct[layer, at, :] = gather(mm(probs.astype(bf16), v)).astype(bf16)

    def attention_back(layer, h):
        for b in blocks_of(h):
            at = pl.ds(b * BLOCK, BLOCK)
            spread_d = spread(mm_t(mb[at, :], wb[layer, 960:1280, :]).astype(bf16))
            spread_q = spread(qb[layer, 0, at, :])
            k = qb[layer, 1, at, :]
            v = qb[layer, 2, at, :]
            probs = pb[layer, b]
            d_probs = mm_t(spread_d, v)
            d_scores = (
                probs * (d_probs - jnp.sum(probs * d_probs, axis=-1, keepdims=True))
            ).astype(bf16)
            d_q = gather(mm(d_scores, k)) * inv
            d_k = tm(d_scores, spread_q) * inv
            dqb[0, at, :] = turned(d_q, -1).astype(bf16)
            dqb[1, at, :] = turned(d_k, -1).astype(bf16)
            dqb[2, at, :] = tm(probs.astype(bf16), spread_d).astype(bf16)

    contexts = pl.ds(pl.multiple_of(s * PATCHES, PATCHES), PATCHES)
    flags = missing_ref[contexts, :].astype(f32)
    values = series_ref[contexts, :] * (1.0 - flags)
    for j in range(PATCHES):
        at = pl.ds(j, PATCHES, stride=PATCHES)
        own_points = slice(j * PATCH, (j + 1) * PATCH)
        gpad[at, :] = jnp.concatenate(
            [values[:, own_points], flags[:, own_points], jnp.zeros((PATCHES, 64), f32)], axis=1
        )
    patch_ref[...] = gpad[:, 0:64].astype(bf16)
    for copy in small_inputs:
        copy.wait()
    for h in range(HALVES):
        at = rows_of(h)
        before = mm(patch_ref[at, :], w_in_ref[...])
        pre[at, :] = before
        tokh[at, :] = (before * jax.nn.sigmoid(before)).astype(bf16)
        rs_send(0, h, lambda j, cols: mm(tokh[at, :], w_hid_ref[:, cols]))
    gn_send.wait_recv()
    pltpu.make_async_copy(wb.at[s], wb.at[s], w_loc).wait()
    for h in range(HALVES):
        start_weights(4 + 2 * h, 6 + 2 * h)
        weights(0, [("y", 0)] if h == 0 else [("y", 1), ("y", 2)])
        stream = rs_take(0, h) + mm(patch_ref[chunk(h, z), :], w_res_ref[...])
        sx[0, own(h), :] = stream
        ag_send(0, h, nb.at[0], norm(stream, gn[0, 0:1, :]))
    start_weights(8, 10)
    weights(0, [("x", 0), ("y", 3), ("x", 1), ("x", 2), ("y", 4)])
    weights(1, [("y", 0), ("y", 1), ("y", 2)])

    def lo_rows(sec, h):
        return lo_ref.at[pl.ds(pl.multiple_of(sec * ROWS + h * RH + z * RQ, RQ), RQ)]

    def lo_keep(h):
        return pltpu.make_async_copy(ob.at[s, own(h)], lo_rows(s, h), lo_l.at[h])

    def lo_cross(h):
        return remote(ob.at[other, own(h)], lo_rows(s, h), lo_s.at[0, h], lo_r.at[0, h], y_a)

    def lo_arrive(h):
        return remote(ob.at[other, own(h)], lo_rows(other, h), lo_s.at[0, h], lo_r.at[0, h], y_a)

    def lo_own(h, d):
        return remote(ob.at[s, own(h)], lo_rows(s, h), lo_s.at[1, h], lo_r.at[1, h], z_peer[d])

    def lo_pass(h, d):
        ref = lo_rows(other, h)
        return remote(ref, ref, lo_s.at[2, h], lo_r.at[2, h], z_peer[d])

    def lo_total(i, h):
        ref = pd.at[pl.ds(0, 3 * RQ)]
        return remote(ref, ref, lo_s.at[i, h], lo_r.at[i, h], core)

    def cross_out(layer, h):
        @pl.when(s != layer)
        def _():
            lo_cross(h).start()

    def own_out(h):
        lo_keep(h).start()
        for d in (2, 1, 3):
            lo_own(h, d).start()

    def pass_out(h):
        lo_arrive(h).wait_recv()
        for d in (2, 1, 3):
            lo_pass(h, d).start()

    def mlp_out(layer, h):
        out = (mid[layer, own(h), :] + rs_take(2 + 2 * layer, h)).astype(bf16)
        ob[layer, own(h), :] = out
        cross_out(layer, h)
        return out

    for layer in range(2):
        for h in range(HALVES):
            ag_wait(2 * layer, h, nb.at[layer])
            attention_front(layer, h)
            if h == 0 and layer == 0:
                start_weights(10, 12)
                weights(0, [("y", 5), ("x", 3), ("x", 4), ("y", 6), ("core", 3)])
                weights(1, [("y", 3), ("y", 4), ("y", 5)])
            if h == 0 and layer == 1:
                weights(1, [("core", 3)])
            if h == 1 and layer == 0:
                weights(0, [("y", 7)])
            at = rows_of(h)
            rs_send(
                1 + 2 * layer, h, lambda j, cols: mm(ct[layer, at, :], wb[layer, 960:1280, cols])
            )
        if layer == 0:
            weights(0, [("y", 8), ("x", 5), ("x", 6)])
            weights(1, [("y", 6), ("x", 0), ("x", 1), ("x", 2), ("x", 3)])
        for h in range(HALVES):
            if layer == 0 and h == 1:
                weights(0, [("y", 9), ("x", 7), ("y", 10), ("y", 11)])
                weights(1, [("y", 7)])
            middle = sx[layer, own(h), :] + rs_take(1 + 2 * layer, h)
            mid[layer, own(h), :] = middle
            ag_send(1 + 2 * layer, h, nm.at[layer], norm(middle, gn[layer, 1:2, :]))
        if layer == 0:
            weights(0, [("x", 8)] + [("core", i) for i in range(4, 8)])
            weights(1, [("y", 8), ("y", 9), ("x", 4), ("x", 5)])
        else:
            weights(1, [("core", i) for i in range(4, 8)])
        for h in range(HALVES):
            ag_wait(1 + 2 * layer, h, nm.at[layer])
            at = rows_of(h)

            def up_tile(j, carry):
                cols = cols_of(j)
                up = mm(nm[layer, at, :], wb[layer, 1280:2560, cols])
                upb[layer, at, cols] = up
                t = jnp.tanh(GELU_A * (up + GELU_B * up * up * up))
                hb[at, cols] = (0.5 * up * (1.0 + t)).astype(bf16)

            unrolled(D // TILE, up_tile)
            if layer == 1:
                continue
            if h == 0 and layer == 0:
                weights(0, [("x", 9), ("x", 10), ("x", 11)] + [("core", i) for i in range(8, 12)])
                weights(1, [("y", 10), ("y", 11), ("x", 6), ("x", 7)])
            rs_send(
                2 + 2 * layer, h, lambda j, cols: mm(hb[at, :], wb[layer, 2560:3840, cols])
            )
        if layer == 0:
            weights(1, [("x", 8), ("x", 9)])
            for h in range(HALVES):
                out = mlp_out(0, h)
                stream = out.astype(f32)
                sx[1, own(h), :] = stream
                ag_send(2, h, nb.at[1], norm(stream, gn[1, 0:1, :]))
            weights(1, [("x", 10), ("x", 11)])

    xa = x + 1 - 2 * lax.rem(x, 2)
    xb = 3 - x
    to_xa = (s, xa * 4 + 2 * yh + c, z)
    to_xb = (s, xb * 4 + 2 * yh + c, z)
    j1 = lax.rem(lax.div(x + 1, 2), 2)
    j2 = lax.div(x, 2)
    i1 = lax.div(x, 2)
    i2 = lax.rem(x, 2)
    half_at = (64 + 64 * j1, 192 + 64 * i1)
    half_off = (64 + 64 * (1 - j1), 192 + 64 * (1 - i1))
    quarter_at = (half_at[0] + 32 * j2, half_at[1] + 32 * i2)
    quarter_off = (half_at[0] + 32 * (1 - j2), half_at[1] + 32 * (1 - i2))
    first_peer = (to_xa, to_xb)
    second_peer = (to_xb, to_xa)

    class Group:
        def __init__(self, layer, k):
            self.layer, self.k = layer, k
            self.buf = gv if layer == 1 else wb.at[1]
            self.mine = k * 1280 + c * 640
            self.theirs = k * 1280 + (1 - c) * 640
            self.home = s == layer

        def rows(self, at, n):
            return self.buf.at[pl.ds(pl.multiple_of(self.mine + at, 16), n)]

        def result(self, at, n):
            return go_ref.at[pl.ds(pl.multiple_of(self.mine + at, 16), n)]

        def move(self, i, src, dst, peer):
            return remote(src, dst, e_s.at[self.layer, self.k], e_r.at[self.layer, self.k, i], peer)

        def add(self, at, n, sources):
            step = 32 if n % 32 == 0 and len(sources) == 1 else 16

            def body(i, carry):
                here = pl.ds(pl.multiple_of(self.mine + at + i * step, 16), step)
                there = pl.ds(pl.multiple_of(i * step, 16), step)
                total = self.buf[here, :].astype(f32)
                for source in sources:
                    total = total + source[there, :].astype(f32)
                self.buf[here, :] = total.astype(bf16)
                return carry

            lax.fori_loop(0, n // step, body, 0)

        def total(self, i, n):
            ref = th.at[self.k, pl.ds(0, n)]
            return self.move(i, ref, ref, core)

        def core(self):
            src = self.buf.at[pl.ds(pl.multiple_of(self.theirs, 16), 640)]
            return self.move(0, src, th.at[self.k], core)

        def first(self, b, hf):
            dst = r1.at[self.k, pl.ds(128 * b + 64 * hf, 64)]
            return self.move(1, self.rows(320 * hf + half_off[b], 64), dst, first_peer[b])

        def second(self, b, hf):
            dst = r2.at[self.k, pl.ds(64 * b + 32 * hf, 32)]
            return self.move(2, self.rows(320 * hf + quarter_off[b], 32), dst, second_peer[b])

        def a_over_y(self, d):
            src = self.rows(320 * lax.div(y_at[d], 2), 64)
            return self.move(3, src, ra1.at[self.k, d - 1], y_peer[d])

        def a_over_x(self, d):
            src = self.rows(320 * yh + 16 * x_at[d], 16)
            return self.move(4, src, ra2.at[self.k, d - 1], x_peer[d])

        def b_over_y(self, d, b):
            src = self.rows(320 * lax.div(y_at[d], 2) + quarter_at[b], 32)
            return self.move(5, src, rb3.at[self.k, d - 1, pl.ds(32 * b, 32)], y_peer[d])

        def a_back_x(self, d):
            at = 320 * yh + 16 * x
            return self.move(6, self.rows(at, 16), self.result(at, 16), x_peer[d])

        def b_back_y(self, b):
            at = 320 * yh + quarter_at[b]
            return self.move(7, self.rows(at, 32), self.result(at, 32), y_peer[2])

        def back_second(self, b, hf):
            ref = self.result(320 * hf + quarter_at[b], 32)
            return self.move(8, ref, ref, second_peer[b])

        def back_first(self, b, hf):
            ref = self.result(320 * hf + half_at[b], 64)
            return self.move(9, ref, ref, first_peer[b])

        def a_back_y(self):
            ref = self.result(320 * yh, 64)
            return self.move(10, ref, ref, y_peer[2])

        def back_core(self, at, n=640):
            ref = self.result(at, n)
            return self.move(11, ref, ref, core)

        def keep(self, at, n):
            return pltpu.make_async_copy(
                self.rows(at, n), self.result(at, n), e_l.at[self.layer, self.k]
            )

        def to_homes(self, copies):
            @pl.when(self.home)
            def _():
                for copy in copies(2):
                    copy.start()

            @pl.when(jnp.logical_not(self.home))
            def _():
                for d in (1, 3):
                    for copy in copies(d):
                        copy.start()

        def s0(self):
            if self.layer == 0:
                pl.semaphore_wait(free_th.at[self.k], 1)
            self.core().start()

        def s1(self):
            self.core().wait_recv()
            self.add(0, 640, [th.at[self.k]])
            if self.layer == 1:
                pl.semaphore_signal(free_th.at[self.k], inc=1, device_id=core, device_id_type=MESH)
            else:
                pl.semaphore_wait(free_r1.at[self.k], 2)
            for b in range(2):
                for hf in range(2):
                    self.first(b, hf).start()
            self.to_homes(lambda d: [self.a_over_y(d)])

        def s2(self):
            self.total(1, 256).wait_recv()
            for b in range(2):
                for hf in range(2):
                    self.add(
                        320 * hf + half_at[b], 64, [r1.at[self.k, pl.ds(128 * b + 64 * hf, 64)]]
                    )
            if self.layer == 1:
                for peer in (to_xa, to_xb):
                    pl.semaphore_signal(
                        free_r1.at[self.k], inc=1, device_id=peer, device_id_type=MESH
                    )
            else:
                pl.semaphore_wait(free_r2.at[self.k], 2)
            for b in range(2):
                for hf in range(2):
                    self.second(b, hf).start()

        def s3(self):
            self.total(2, 128).wait_recv()
            for b in range(2):
                for hf in range(2):
                    self.add(
                        320 * hf + quarter_at[b], 32, [r2.at[self.k, pl.ds(64 * b + 32 * hf, 32)]]
                    )
            if self.layer == 1:
                for peer in (to_xa, to_xb):
                    pl.semaphore_signal(
                        free_r2.at[self.k], inc=1, device_id=peer, device_id_type=MESH
                    )
            self.to_homes(lambda d: [self.b_over_y(d, b) for b in range(2)])

            @pl.when(self.home)
            def _():
                self.total(3, 192).wait_recv()
                self.add(320 * yh, 64, [ra1.at[self.k, i] for i in range(3)])
                for d in (2, 1, 3):
                    self.a_over_x(d).start()

        def s4(self):
            @pl.when(self.home)
            def _():
                self.total(5, 192).wait_recv()
                for b in range(2):
                    at = 320 * yh + quarter_at[b]
                    self.add(at, 32, [rb3.at[self.k, i, pl.ds(32 * b, 32)] for i in range(3)])
                    self.keep(at, 32).start()
                    self.b_back_y(b).start()
                self.total(4, 48).wait_recv()
                at = 320 * yh + 16 * x
                self.add(at, 16, [ra2.at[self.k, i] for i in range(3)])
                self.keep(at, 16).start()
                for d in (2, 1, 3):
                    self.a_back_x(d).start()

        def s5(self):
            @pl.when(self.home)
            def _():
                self.keep(0, 80).wait()
                self.total(7, 64).wait_recv()
                for b in range(2):
                    for hf in range(2):
                        self.back_second(b, hf).start()
                self.total(6, 48).wait_recv()
                self.a_back_y().start()

        def s6(self):
            @pl.when(self.home)
            def _():
                self.total(8, 128).wait_recv()
                for b in range(2):
                    for hf in range(2):
                        self.back_first(b, hf).start()
                for b in range(2):
                    for hf in range(2):
                        self.back_core(320 * hf + half_at[b], 64).start()

        def s7(self):
            @pl.when(self.home)
            def _():
                self.a_back_y().wait_recv()
                for hf in range(2):
                    self.back_core(320 * hf, 64).start()
                self.total(9, 256).wait_recv()
                for b in range(2):
                    for hf in range(2):
                        self.back_core(320 * hf + half_off[b], 64).start()

        def sent(self, n):
            ref = wb.at[0, pl.ds(0, n)]
            return remote(ref, ref, e_s.at[self.layer, self.k], e_r.at[self.layer, self.k, 0], core)

        def drain(self):
            @pl.when(self.home)
            def _():
                self.back_core(0).wait_recv()
                self.sent(1760 + 640).wait_send()

            @pl.when(jnp.logical_not(self.home))
            def _():
                self.sent(1280).wait_send()

    groups = {(layer, k): Group(layer, k) for layer in range(2) for k in range(3)}
    att1, up1, down1 = (groups[1, k] for k in range(3))
    att0, up0, down0 = (groups[0, k] for k in range(3))

    def put(layer, at, value):
        if layer == 1:
            gv[at, :] = value.astype(bf16)
        else:
            wb[1, at, :] = value.astype(bf16)

    def grad_tiles(layer, k, left, right):
        for i in range(D // TILE):
            put(layer, pl.ds(k * 1280 + i * TILE, TILE), tm(left[:, cols_of(i)], right[...]))
        groups[layer, k].s0()

    def t_move(i, src, dst, peer):
        return remote(src, dst, t_s.at[i], t_r.at[i], peer)

    def t_rows(sec, at, n):
        return gt.at[sec, pl.ds(pl.multiple_of(at, 16), n)]

    def t_result(at, n):
        return go_ref.at[pl.ds(pl.multiple_of(LAYER_ROWS + at, 16), n)]

    def t_core(sec):
        return t_move(0, t_rows(sec, 128 * (1 - c), 128), tt.at[sec], core)

    def t_over_x(d, sec):
        src = t_rows(sec, 128 * c + 32 * x_at[d], 32)
        return t_move(1, src, tx.at[d - 1, sec], x_peer[d])

    def t_over_y(d):
        src = t_rows(lax.rem(y_at[d], 2), 128 * c + 32 * x + 16 * lax.div(y_at[d], 2), 16)
        return t_move(2, src, ty.at[d - 1], y_peer[d])

    t_own = 128 * c + 32 * x + 16 * yh

    def t_back_y():
        return t_move(3, t_rows(s, t_own, 16), t_result(t_own, 16), y_peer[2])

    def t_keep():
        return pltpu.make_async_copy(t_rows(s, t_own, 16), t_result(t_own, 16), t_l)

    def t_back_x(d):
        ref = t_result(128 * c + 32 * x, 32)
        return t_move(4, ref, ref, x_peer[d])

    def t_back_core():
        ref = t_result(128 * c, 128)
        return t_move(5, ref, ref, core)

    def t_total(i, n):
        ref = gt.at[0, pl.ds(0, n)]
        return t_move(i, ref, ref, core)

    def t_add(sec, at, n, sources):
        here = pl.ds(pl.multiple_of(at, 16), n)
        total = gt[sec, here, :].astype(f32)
        for source in sources:
            total = total + source[...].astype(f32)
        gt[sec, here, :] = total.astype(bf16)

    def t1():
        t_total(0, 256).wait_recv()
        for sec in range(2):
            for i in range(4):
                t_add(sec, 128 * c + 32 * i, 32, [tt.at[sec, pl.ds(32 * i, 32)]])
            for d in (2, 1, 3):
                t_over_x(d, sec).start()

    def t2():
        t_total(1, 192).wait_recv()
        for sec in range(2):
            t_add(sec, 128 * c + 32 * x, 32, [tx.at[i, sec] for i in range(3)])
        for d in (2, 1, 3):
            t_over_y(d).start()

    def t3():
        t_total(2, 48).wait_recv()
        t_add(s, t_own, 16, [ty.at[i] for i in range(3)])
        t_keep().start()
        t_back_y().start()

    def t4():
        t_keep().wait()
        t_back_y().wait_recv()
        for d in (2, 1, 3):
            t_back_x(d).start()

    def t5():
        t_total(4, 96).wait_recv()
        t_back_core().start()

    weights(1, [("core", i) for i in range(8, 12)])
    cot_copy.wait()
    grad_tiles(1, 2, hb, gb.at[0])
    gg[...] = jnp.zeros_like(gg)

    for layer in (1, 0):
        st = 5 if layer == 1 else 7
        for h in range(HALVES):
            at = rows_of(h)
            if layer == 0:
                ag_wait(5, h, gb.at[1])

            def d_up_tile(j, carry):
                cols = cols_of(j)
                rows = pl.ds(2560 + j * TILE, TILE)
                d_hidden = mm_t(gb[1 - layer, at, :], wb[layer, rows, :])
                up = upb[layer, at, cols]
                t = jnp.tanh(GELU_A * (up + GELU_B * up * up * up))
                slope = 0.5 * (1.0 + t) + 0.5 * up * (1.0 - t * t) * (
                    GELU_A * (1.0 + 3.0 * GELU_B * up * up)
                )
                du[at, cols] = (d_hidden * slope).astype(bf16)
                if layer == 0:
                    hb[at, cols] = (0.5 * up * (1.0 + t)).astype(bf16)

            unrolled(D // TILE, d_up_tile)
            if layer == 0 and h == 1:
                up1.s2()
            if layer == 1 and h == 1:
                down1.s1()
            rs_send(
                st, h,
                lambda j, cols: mm_t(
                    du[at, :], wb[layer, pl.ds(1280 + j * TILE, TILE), :]
                ),
            )
        if layer == 0:
            w_sent(4, x_s, x_r).wait_send()
            w_sent(2, f_s, f_r).wait_send()
        if layer == 0:
            grad_tiles(0, 2, hb, gb.at[1])
        for h in range(HALVES):
            dn = rs_take(st, h)
            dx, gain = norm_back(dn, mid[layer, own(h), :], gn[layer, 1:2, :])
            dm = gb[1 - layer, chunk(h, z), :].astype(f32) + dx
            dmid[own(h), :] = dm
            gg[2 * layer + 1 : 2 * layer + 2, :] += gain
            if layer == 0:
                ag_total(4, h).wait_send()
            ag_send(st - 1, h, mb, dm)
        grad_tiles(layer, 1, nm.at[layer], du)
        if layer == 1:
            for j in range(D // TILE):
                pd[:, cols_of(j)] = mm(hb[...], wb[1, 2560:3840, cols_of(j)]).astype(bf16)
            down1.s2()
        else:
            down0.s1()
        for h in range(HALVES):
            ag_wait(st - 1, h, mb)
            attention_back(layer, h)
            if h == 1 and layer == 1:
                up1.s1()
            if h == 1 and layer == 0:
                up0.s1()
                up1.s3()
                att1.s2()
            at = rows_of(h)
            rs_send(
                st + 1, h,
                lambda j, cols: mm(dqb[0, at, :], wb[layer, 0:ATT, cols])
                + mm(dqb[1, at, :], wb[layer, ATT : 2 * ATT, cols])
                + mm(dqb[2, at, :], wb[layer, 2 * ATT : 3 * ATT, cols]),
            )
        for i in range(3):
            put(layer, pl.ds(i * ATT, ATT), tm(dqb[i], nb[layer]))
        put(layer, pl.ds(960, 320), tm(ct[layer], mb[...]))
        groups[layer, 0].s0()
        if layer == 1:
            down1.s3()
        else:
            down0.s2()
        for h in range(HALVES):
            dn = rs_take(st + 1, h)
            dx, gain = norm_back(dn, sx[layer, own(h), :], gn[layer, 0:1, :])
            gg[2 * layer : 2 * layer + 1, :] += gain
            ag_send(st, h, gb.at[layer], dmid[own(h), :] + dx)
        if layer == 1:
            att1.s1()
        else:
            att0.s1()
            up0.s2()
            down1.s4()

    def gg_copy(d):
        return remote(gg, ggr.at[d - 1], gg_s, gg_r, z_peer[d])

    for d in (1, 2, 3):
        gg_copy(d).start()

    for h in range(HALVES):
        ag_wait(7, h, gb.at[0])
        rs_send(4, h, None)
        at = rows_of(h)
        low = gb[0, at, :]
        before = pre[at, :]
        sig = jax.nn.sigmoid(before)
        d_pre = (
            mm_t(low, w_hid_ref[...]) * (sig * (1.0 + before * (1.0 - sig)))
        ).astype(bf16)
        dctx[at, :] = d_pre
        points = mm_t(d_pre, w_in_ref[...])
        points = points + jnp.where(z == 0, mm_t(low, w_res_ref[...]), 0.0)
        keep = 1.0 - patch_ref[at, :].astype(f32)
        gpad[at, 0:PATCH] = points[:, 0:PATCH] * keep[:, PATCH : 2 * PATCH]
    down0.s3()
    points = gpad[:, 0:64]
    high = points.astype(bf16)
    low = (points - high.astype(f32)).astype(bf16)
    row = lax.broadcasted_iota(jnp.int32, (ROWS, ROWS), 0)
    col = lax.broadcasted_iota(jnp.int32, (ROWS, ROWS), 1)
    swap = jnp.where(
        ((row >> 4) == (col & 15)) & ((row & 15) == (col >> 4)), 1.0, 0.0
    ).astype(bf16)
    points = mm(swap, high) + mm(swap, low)
    for k in range(8):
        dps[k, :, 0:64] = points[k * 32 : (k + 1) * 32]
        dps[k, :, 64:128] = jnp.zeros((32, 64), f32)
    me = s * 4 + z

    def dp_copy(d):
        to = lax.rem(me + d, 8)
        return remote(
            dps.at[to], dpr.at[me], dp_s, dp_r,
            (lax.div(to, 4), dp, lax.rem(to, 4)),
        )

    for d in range(1, 8):
        dp_copy(d).start()
    dpr[me] = dps[me]

    grad_low = gb[0]
    hid = tm(tokh[...], grad_low).astype(bf16)
    res = tm(patch_ref[...], grad_low).astype(bf16)
    inn = tm(patch_ref[...], dctx[...]).astype(bf16)
    for sec in range(2):
        lanes = slice(sec * 640, sec * 640 + 640)
        gt[sec, 0:160, 0:640] = hid[0:160, lanes]
        gt[sec, 0:160, 640:1280] = hid[160:320, lanes]
        gt[sec, 160:192, 0:640] = res[0:32, lanes]
        gt[sec, 160:192, 640:1280] = res[32:64, lanes]
        gt[sec, 192:224, :] = jnp.zeros((32, D), bf16)
        gt[sec, 192:224, 0:320] = inn[sec * 32 : sec * 32 + 32]
    total = gg[...]
    remote(ggr, ggr, gg_s, gg_r, core).wait_recv()
    for d in (1, 2, 3):
        total = total + ggr[d - 1]
    for sec in range(2):
        gt[sec, 224:256, :] = jnp.concatenate(
            [total[2 * sec : 2 * sec + 2], jnp.zeros((30, D), f32)], axis=0
        ).astype(bf16)

    for sec in range(2):
        t_core(sec).start()
    att1.s3()
    att0.s2()
    up0.s3()
    t1()
    down0.s4()
    down1.s5()
    att0.s3()
    up1.s4()
    t2()
    down0.s5()
    up0.s4()
    att1.s4()
    for h in range(HALVES):
        mlp_out(1, h)
        own_out(h)
    down1.s6()
    down0.s6()
    up0.s5()
    up1.s5()
    att0.s4()
    att1.s5()
    t3()
    att0.s5()
    up0.s6()
    up1.s6()
    for h in range(HALVES):
        pass_out(h)
    down0.s7()
    down1.s7()
    t4()
    att0.s6()
    att1.s6()
    up0.s7()
    up1.s7()
    t5()
    att0.s7()
    att1.s7()
    seven = dps.at[pl.ds(0, 7)]
    remote(seven, seven, dp_s, dp_r, core).wait_recv()
    for sec in range(2):
        points_ref[sec] = dpr[4 * sec] + dpr[4 * sec + 1] + dpr[4 * sec + 2] + dpr[4 * sec + 3]

    w_sent(4, w_s, w_r).wait_send()
    for group in groups.values():
        group.drain()
    for i, n in ((0, 256), (1, 192), (2, 48), (3, 16), (4, 96)):
        t_total(i, n).wait_send()
    t_back_core().wait()
    gn_send.wait_send()
    for h in range(HALVES):
        rs_total(7, h).wait_send()
        rs_total(4, h).wait_send()
        for st in (0, 1, 2, 3, 5, 6, 7):
            ag_total(st, h).wait_send()
        lo_cross(h).wait_send()
        lo_keep(h).wait()
        for i in (1, 2):
            lo_total(i, h).wait()
    remote(ggr, ggr, gg_s, gg_r, core).wait_send()
    remote(seven, seven, dp_s, dp_r, core).wait_send()


def run_layers(series, missing, w_in, w_hid, w_res, gain_a, gain_m, wq, wo, wu, wd, cotangent):
    cos, sin, turn = rotary_arrays()
    vm = pl.BlockSpec(memory_space=pltpu.VMEM)
    hbm = pl.BlockSpec(memory_space=pl.ANY)
    dma = pltpu.SemaphoreType.DMA
    scratch = [
        pltpu.VMEM((2 * PATCH, ATT), bf16),
        pltpu.VMEM((ATT, D), bf16),
        pltpu.VMEM((2 * PATCH, D), bf16),
        pltpu.VMEM((BLOCK, ATT), f32),
        pltpu.VMEM((BLOCK, ATT), f32),
        pltpu.VMEM((ATT, ATT), bf16),
        dma((6,)),
        pltpu.VMEM((ROWS, 2 * PATCH), bf16),
        pltpu.VMEM((2, LAYER_ROWS, D), bf16),
        pltpu.VMEM((2, 2, D), f32),
        pltpu.VMEM((ROWS, ATT), bf16),
        pltpu.VMEM((ROWS, ATT), f32),
        pltpu.VMEM((2, ROWS // 4, D), f32),
        pltpu.VMEM((2, ROWS // 4, D), f32),
        pltpu.VMEM((2, ROWS, D), bf16),
        pltpu.VMEM((2, ROWS, D), bf16),
        pltpu.VMEM((2, 3, ROWS, ATT), bf16),
        pltpu.VMEM((2, ROWS // BLOCK, HEADS_HERE * BLOCK, BLOCK), f32),
        pltpu.VMEM((2, ROWS, ATT), bf16),
        pltpu.VMEM((2, ROWS, D), f32),
        pltpu.VMEM((ROWS, D), bf16),
        pltpu.VMEM((2, ROWS, D), bf16),
        pltpu.VMEM((ROWS, D), bf16),
        pltpu.VMEM((ROWS, D), bf16),
        pltpu.VMEM((3, ROWS, ATT), bf16),
        pltpu.VMEM((ROWS, ATT), bf16),
        pltpu.VMEM((LAYER_ROWS, D), bf16),
        pltpu.VMEM((2, PACK_ROWS - LAYER_ROWS, D), bf16),
        pltpu.VMEM((2, ROWS, D), bf16),
        pltpu.VMEM((2, 3, ROWS // 4, D), bf16),
        pltpu.VMEM((ROWS // 4, D), f32),
        pltpu.VMEM((2, ROWS // 4, D), bf16),
        pltpu.VMEM((8, D), f32),
        pltpu.VMEM((3, 8, D), f32),
        pltpu.VMEM((8, 32, 128), f32),
        pltpu.VMEM((8, 32, 128), f32),
        pltpu.VMEM((ROWS, 128), f32),
        pltpu.VMEM((3, 640, D), bf16),
        pltpu.VMEM((3, 256, D), bf16),
        pltpu.VMEM((3, 128, D), bf16),
        pltpu.VMEM((3, 3, 64, D), bf16),
        pltpu.VMEM((3, 3, 16, D), bf16),
        pltpu.VMEM((3, 3, 64, D), bf16),
        pltpu.VMEM((2, 128, D), bf16),
        pltpu.VMEM((3, 2, 32, D), bf16),
        pltpu.VMEM((3, 16, D), bf16),
        pltpu.VMEM((ROWS, D), bf16),
        dma, *[dma, dma((N_PIECES,))] * 3,
        dma, dma, dma,
        dma((9, HALVES)), dma((9, HALVES)),
        dma((8, HALVES)), dma((8, HALVES)),
        dma((HALVES,)), dma((3, HALVES)), dma((3, HALVES)),
        dma, dma, dma, dma,
        dma((2, 3)), dma((2, 3, 12)), dma((2, 3)),
        dma((6,)), dma((6,)), dma,
        *[pltpu.SemaphoreType.REGULAR((3,))] * 3,
    ]
    return pl.pallas_call(
        layers_kernel,
        out_shape=(
            jax.ShapeDtypeStruct((2 * ROWS, D), bf16),
            jax.ShapeDtypeStruct((PACK_ROWS, D), bf16),
            jax.ShapeDtypeStruct((2, 32, 128), f32),
        ),
        in_specs=[vm] * 2 + [hbm] * 3 + [vm] * 2 + [hbm] * 8,
        out_specs=(hbm, hbm, vm),
        scratch_shapes=scratch,
        compiler_params=pltpu.CompilerParams(
            collective_id=0, has_side_effects=True, vmem_limit_bytes=62 * 2**20
        ),
        cost_estimate=pl.CostEstimate(
            flops=15_000_000_000, bytes_accessed=50_000_000, transcendentals=4_000_000
        ),
        name="layers",
    )(
        series, missing, w_in, w_hid, w_res, gain_a, gain_m, wq, wo, wu, wd, cotangent,
        jnp.asarray(cos, f32), jnp.asarray(sin, f32), jnp.asarray(turn, bf16),
    )


STEP = 320
STEPS = LAYER_ROWS // STEP


def widen_kernel(
    total_ref, lo_ref, points_ref,
    qkv, out, up, down, hid, res, inn, gain_a, gain_m, series_grad, lo_out,
    low, wide, small, kept, in_sem, out_sem, small_sem, lo_sem,
):
    places_of = [(qkv, i) for i in range(3)] + [(out, 0)]
    places_of += [(up, i) for i in range(4)] + [(down, i) for i in range(4)]

    def rows(i):
        return pl.ds(i * STEP, STEP)

    def load(i):
        return pltpu.make_async_copy(total_ref.at[rows(i)], low.at[rows(i)], in_sem.at[i])

    def store(i):
        ref, k = places_of[i]
        return pltpu.make_async_copy(wide.at[rows(i)], ref.at[rows(k)], out_sem.at[i])

    load_small = pltpu.make_async_copy(
        total_ref.at[pl.ds(LAYER_ROWS, PACK_ROWS - LAYER_ROWS)], small, small_sem
    )
    load_lo = pltpu.make_async_copy(lo_ref, kept, lo_sem)
    store_lo = pltpu.make_async_copy(kept, lo_out, lo_sem)
    for i in range(STEPS):
        load(i).start()
    load_small.start()
    load_lo.start()
    for i in range(STEPS):
        load(i).wait()

        def body(j, carry, i=i):
            at = pl.ds(pl.multiple_of(i * STEP + j * 32, 32), 32)
            wide[at, :] = low[at, :].astype(f32)
            return carry

        lax.fori_loop(0, STEP // 32, body, 0, unroll=2)
        store(i).start()
    load_lo.wait()
    store_lo.start()
    load_small.wait()
    values = small[...].astype(f32)
    hid[0:160, :] = values[0:160, 0:640]
    hid[160:320, :] = values[0:160, 640:1280]
    res[0:32, :] = values[160:192, 0:640]
    res[32:64, :] = values[160:192, 640:1280]
    inn[...] = values[192:224, 0:320]
    gain_a[...] = values[224:225]
    gain_m[...] = values[225:226]
    for sec in range(2):
        for j in range(2):
            series_grad[16 * sec : 16 * sec + 16, 32 * j : 32 * j + 32] = points_ref[
                sec, 16 * j : 16 * j + 16, 0:32
            ]
    for i in range(STEPS):
        store(i).wait()
    store_lo.wait()


def widen(total, layer_out, points):
    shapes = ((960, D), (320, D), (1280, D), (1280, D), (320, 640), (64, 640), (32, 320), (1, D), (1, D), (32, 64))
    hbm = pl.BlockSpec(memory_space=pl.ANY)
    vm = pl.BlockSpec(memory_space=pltpu.VMEM)
    dma = pltpu.SemaphoreType.DMA
    return pl.pallas_call(
        widen_kernel,
        out_shape=[jax.ShapeDtypeStruct(shape, f32) for shape in shapes]
        + [jax.ShapeDtypeStruct((2 * ROWS, D), bf16)],
        in_specs=[hbm, hbm, vm],
        out_specs=[hbm] * 4 + [vm] * 6 + [hbm],
        scratch_shapes=[
            pltpu.VMEM((LAYER_ROWS, D), bf16),
            pltpu.VMEM((LAYER_ROWS, D), f32),
            pltpu.VMEM((PACK_ROWS - LAYER_ROWS, D), bf16),
            pltpu.VMEM((2 * ROWS, D), bf16),
            dma((STEPS,)), dma((STEPS,)), dma, dma,
        ],
        compiler_params=pltpu.CompilerParams(vmem_limit_bytes=60 * 2**20),
        cost_estimate=pl.CostEstimate(flops=0, bytes_accessed=32_000_000, transcendentals=0),
        name="widen",
    )(total, layer_out, points)


def per_device(
    series, missing, w_in, w_hid, w_res, gain_attn, w_qkv, w_out, gain_mlp, w_up, w_down, cotangent
):
    wq = jnp.transpose(w_qkv[0], (1, 2, 0)).reshape(3 * ATT, D)
    layer_out, total, points = run_layers(
        series, missing, w_in, w_hid, w_res, gain_attn, gain_mlp, wq, w_out[0], w_up[0], w_down[0],
        cotangent,
    )
    g_qkv, g_out, g_up, g_down, g_hid, g_res, g_in, gain_a, gain_m, series_grad, layer_out = widen(
        total, layer_out, points
    )
    g_qkv = jnp.transpose(g_qkv.reshape(3, ATT, D), (2, 0, 1))
    return (
        layer_out[None],
        series_grad,
        g_in,
        g_hid,
        g_res,
        gain_a,
        g_qkv[None],
        g_out[None],
        gain_m,
        g_up[None],
        g_down[None],
    )


def solution(mesh):
    in_specs = (
        P("dp", None),
        P("dp", None),
        P(None, "tensor"),
        P("tensor", None),
        P(),
        P("section", None),
        P("section", None, None, "tensor"),
        P("section", "tensor", None),
        P("section", None),
        P("section", None, "tensor"),
        P("section", "tensor", None),
        P("dp", None),
    )
    out_specs = (
        P("section", "dp", None),
        P("dp", ("section", "tensor")),
        P("section", "tensor"),
        P("tensor", "section"),
        P(None, "section"),
        P("section", None),
        P("section", None, None, "tensor"),
        P("section", "tensor", None),
        P("section", None),
        P("section", None, "tensor"),
        P("section", "tensor", None),
    )
    return jax.shard_map(
        per_device, mesh=mesh, in_specs=in_specs, out_specs=out_specs, check_vma=False
    )
```
